256 devices in a mesh: image: 8 (over y, x_lo), slab: 32 (over x_hi, z, core).
Axes of the slice: x: 4 (x_hi: 2, x_lo: 2; x = x_hi * 2 + x_lo), y: 4, z: 8, core: 2. Of those that a mesh axis runs over, the one named last changes fastest.
Arguments:
- positions: float32 [16, 3, 8192], P('image', None, 'slab')
- neighbours: int32 [262144], P('slab'), may hold values from -1 to 511, as said below
- ghost_slots: int32 [2, 4096], P(None, 'slab'), may hold values from 0 to 255, as said below
- climbing: int32 [1], replicated, may hold values from 1 to 14
- w_radial1: float32 [8, 128], replicated, may hold values from -2 to 2
- w_square: float32 [128, 128], replicated, may hold values from -0.5 to 0.5
- w_hidden: float32 [128, 128], replicated, may hold values from -0.5 to 0.5
- w_message: float32 [128, 128], replicated, may hold values from -0.5 to 0.5
- w_radial2: float32 [8, 128], replicated, may hold values from -2 to 2
- w_output: float32 [128, 128], replicated, may hold values from -0.5 to 0.5
- w_energy: float32 [128], replicated, may hold values from -0.5 to 0.5
Outputs:
- neb_force: float32 [16, 3, 8192], P('image', None, 'slab')
- energies: float32 [16], P('image')
The draws below stay inside these ranges and needn't reach their ends.
Inputs may be any that keep to these rules, and one draw needn't show every extreme that they name: `neighbours`: each atom has 32 slots in random order; filled slots name distinct atoms of the first, second or third layer of lattice sites around it, the slabs below and above reached through the other slabs' ghost_slots rows as described in the reference program. `ghost_slots`: the two rows of one slab hold each of its atoms once.
All inputs are finite; a program needn't handle non-finite values.
Results may differ from the reference program's by a relative error of at most 0.0003.
Values sent between devices are 32-bit elements; how exact they have to be, the bound alone decides.
No kernel may reach another device: no remote copies, remote signals or barrier semaphores. Data moves between devices by JAX's collectives and lax.ppermute only.
A program may use at most 64 MiB of HBM per device.

```python
import jax
import jax.numpy as jnp
import numpy as np
from jax import lax

CH = 128
NB = 8
NBR = 32
NX = 16
NY = 8
NZL = 2
LAYER = 128
ATOMS_DEV = 256
ATOMS = 8192
IMAGES = 16
N_SLAB = 32


LATTICE = 2.55


def slab_tables(key):
    slab_keys = jax.random.split(key, N_SLAB)
    site_of_slot = jax.vmap(lambda subkey: jax.random.permutation(subkey, ATOMS_DEV))(slab_keys).astype(jnp.int32)
    slot_of_site = jnp.argsort(site_of_slot, axis=1).astype(jnp.int32)
    return (site_of_slot, slot_of_site)


def draw_ghost_slots(key, part):
    site_of_slot, slot_of_site = slab_tables(key)
    key = jax.random.fold_in(key, 3)
    layer_size = NX * NY
    bottom = slot_of_site[:, :layer_size].reshape(-1)
    top_row = slot_of_site[:, (NZL - 1) * layer_size:].reshape(-1)
    return jnp.stack([bottom, top_row]).astype(jnp.int32)


def draw_neighbours(key, part):
    site_of_slot, slot_of_site = slab_tables(key)
    key = jax.random.fold_in(key, 5)
    keep_key, order_key = jax.random.split(key)
    layer_size = NX * NY
    offsets_table = np.array([[dx, dy, dz] for dz in (-1, 0, 1) for dy in (-1, 0, 1) for dx in (-1, 0, 1) if (dx, dy, dz) != (0, 0, 0)], dtype=np.int32)
    column = site_of_slot % NX
    row_index = site_of_slot // NX % NY
    level_index = site_of_slot // layer_size
    col_next = (column[:, :, None] + offsets_table[None, None, :, 0]) % NX
    row_next = (row_index[:, :, None] + offsets_table[None, None, :, 1]) % NY
    level_next = level_index[:, :, None] + offsets_table[None, None, :, 2]
    plane_index = row_next * NX + col_next
    inside_site = jnp.clip(level_next, 0, NZL - 1) * layer_size + plane_index
    owned_slot = jnp.take_along_axis(slot_of_site, inside_site.reshape(N_SLAB, -1), axis=1).reshape(inside_site.shape)
    local_index = jnp.where(level_next < 0, ATOMS_DEV + plane_index, jnp.where(level_next >= NZL, ATOMS_DEV + layer_size + plane_index, owned_slot))
    vertical = (offsets_table[:, 0] == 0) & (offsets_table[:, 1] == 0)
    kept_mask = (jax.random.randint(keep_key, local_index.shape, 0, 5) > 0) | jnp.asarray(vertical)[None, None, :]
    local_index = jnp.where(kept_mask, local_index, -1)
    padded = jnp.concatenate([local_index, jnp.full((N_SLAB, ATOMS_DEV, NBR - 26), -1, jnp.int32)], axis=2)
    scores = jax.random.randint(order_key, padded.shape, 0, 1 << 20) * NBR + jnp.arange(NBR, dtype=jnp.int32)
    shuffle_index = jnp.argsort(scores, axis=2)
    return jnp.take_along_axis(padded, shuffle_index, axis=2).reshape(-1).astype(jnp.int32)


def draw_positions(key, part):
    site_of_slot, slot_of_site = slab_tables(key)
    key = jax.random.fold_in(key, 7)
    base_key, path_key, step_key, noise_key = jax.random.split(key, 4)
    layer_size = NX * NY
    column = (site_of_slot % NX).astype(jnp.float32)
    row_index = (site_of_slot // NX % NY).astype(jnp.float32)
    level_index = (site_of_slot // layer_size + NZL * jnp.arange(N_SLAB, dtype=jnp.int32)[:, None]).astype(jnp.float32)
    lattice = LATTICE * (jnp.stack([column, row_index, level_index]) + 0.5).reshape(3, ATOMS)
    rest_shift = jax.random.uniform(base_key, (3, ATOMS), jnp.float32, -0.1, 0.1)
    swing_field = jax.random.uniform(path_key, (3, ATOMS), jnp.float32, -0.35, 0.35)
    jitter = jax.random.uniform(noise_key, (IMAGES, 3, ATOMS), jnp.float32, -0.05, 0.05)
    progress = (jnp.arange(IMAGES, dtype=jnp.float32) + jax.random.uniform(step_key, (IMAGES,), jnp.float32, -0.3, 0.3)) / (IMAGES - 1)
    return lattice[None] + rest_shift[None] + progress[:, None, None] * swing_field[None] + jitter


def noise(key, extent, scale, most, kind=jnp.bfloat16):
    return jnp.clip(scale * jax.random.normal(key, extent, jnp.float32), -most, most).astype(kind)


def setup_inputs(seed: int = 0) -> dict:
    splits = jax.random.split(jax.random.key(seed), 12)
    return {
        "positions": draw_positions(jax.random.fold_in(splits[11], 71), 0),
        "neighbours": draw_neighbours(jax.random.fold_in(splits[11], 71), 0),
        "ghost_slots": draw_ghost_slots(jax.random.fold_in(splits[11], 71), 0),
        "climbing": jax.random.randint(splits[3], (1,), 1, IMAGES - 1).astype(jnp.int32),
        "w_radial1": noise(splits[4], (NB, CH), NB ** -0.5, 2.0, jnp.float32),
        "w_square": noise(splits[5], (CH, CH), CH ** -0.5, 0.5, jnp.float32),
        "w_hidden": noise(splits[6], (CH, CH), CH ** -0.5, 0.5, jnp.float32),
        "w_message": noise(splits[7], (CH, CH), CH ** -0.5, 0.5, jnp.float32),
        "w_radial2": noise(splits[8], (NB, CH), NB ** -0.5, 2.0, jnp.float32),
        "w_output": noise(splits[9], (CH, CH), CH ** -0.5, 0.5, jnp.float32),
        "w_energy": noise(splits[10], (CH,), CH ** -0.5, 0.5, jnp.float32),
    }


LATTICE = 2.55
CUTOFF = 5.0
STIFFNESS = 5.0
PRECISE = lax.Precision.HIGHEST

def contract(pattern, left_part, right_part):
    return jnp.einsum(pattern, left_part, right_part, precision=PRECISE)

def radial_basis(radius, valid_edge):
    frequency = (jnp.arange(NB, dtype=jnp.float32) + 1.0) * (jnp.pi / CUTOFF)
    smooth = jnp.where(radius < CUTOFF, 0.5 * (jnp.cos(jnp.pi * radius / CUTOFF) + 1.0), 0.0)
    angles = frequency[:, None] * radius[None, :]
    return smooth[None, :] * jnp.sin(angles) / radius[None, :] * valid_edge[None, :]

def wrap_offsets(offsets, cell_box):
    half_box = 0.5 * cell_box
    return jnp.where(offsets > half_box, offsets - cell_box, jnp.where(offsets < -half_box, offsets + cell_box, offsets))

def global_targets(neighbours, ghost_slots):
    local_index = neighbours.reshape(N_SLAB, ATOMS_DEV * NBR)
    slab_id = jnp.arange(N_SLAB, dtype=jnp.int32)[:, None]
    tables = ghost_slots.reshape(2, N_SLAB, LAYER)
    slab_below = (slab_id - 1) % N_SLAB
    slab_above = (slab_id + 1) % N_SLAB
    below_pick = jnp.clip(local_index - ATOMS_DEV, 0, LAYER - 1)
    above_pick = jnp.clip(local_index - ATOMS_DEV - LAYER, 0, LAYER - 1)
    from_below = slab_below * ATOMS_DEV + tables[1][slab_below, below_pick]
    from_above = slab_above * ATOMS_DEV + tables[0][slab_above, above_pick]
    owned_atom = slab_id * ATOMS_DEV + jnp.clip(local_index, 0, ATOMS_DEV - 1)
    target = jnp.where(local_index < 0, 0, jnp.where(local_index < ATOMS_DEV, owned_atom, jnp.where(local_index < ATOMS_DEV + LAYER, from_below, from_above)))
    return target.reshape(-1).astype(jnp.int32)

def tangent_weights(v_prev, v_here, v_next):
    big_step = jnp.maximum(jnp.abs(v_next - v_here), jnp.abs(v_prev - v_here))
    small_step = jnp.minimum(jnp.abs(v_next - v_here), jnp.abs(v_prev - v_here))
    rising = (v_next > v_here) & (v_here > v_prev)
    falling = (v_next < v_here) & (v_here < v_prev)
    higher = v_next > v_prev
    weight_up = jnp.where(rising, 1.0, jnp.where(falling, 0.0, jnp.where(higher, big_step, small_step)))
    weight_down = jnp.where(rising, 0.0, jnp.where(falling, 1.0, jnp.where(higher, small_step, big_step)))
    return (weight_up, weight_down)

def reference(positions, neighbours, ghost_slots, climbing, w_radial1, w_square, w_hidden, w_message, w_radial2, w_output, w_energy):
    target = global_targets(neighbours, ghost_slots)
    valid_mask = neighbours >= 0
    valid_edge = valid_mask.astype(jnp.float32)
    centre = jnp.repeat(jnp.arange(ATOMS, dtype=jnp.int32), NBR)
    cell_box = jnp.array([NX * LATTICE, NY * LATTICE, N_SLAB * NZL * LATTICE], dtype=jnp.float32)[:, None]

    def image_energy(coords):
        offsets = wrap_offsets(coords[:, target] - coords[:, centre], cell_box)
        squared = lax.optimization_barrier(jnp.sum(offsets * offsets, axis=0))
        radius = jnp.sqrt(jnp.where(valid_mask, squared, 1.0))
        edge_basis = radial_basis(radius, valid_edge)
        summed = edge_basis.reshape(NB, ATOMS, NBR).sum(-1)
        radial_mix = contract('bc,ba->ca', w_radial1, summed)
        mixed = radial_mix + contract('cd,ca->da', w_square, radial_mix * radial_mix)
        hidden = jax.nn.silu(contract('cd,ca->da', w_hidden, mixed))
        message = contract('cd,ca->da', w_message, hidden)
        edge_radial = contract('bc,be->ce', w_radial2, edge_basis)
        second = (edge_radial * message[:, target]).reshape(CH, ATOMS, NBR).sum(-1)
        energy_pre = contract('cd,ca->da', w_output, second + hidden)
        return jnp.sum(contract('c,ca->a', w_energy, jax.nn.silu(energy_pre)))

    def one_image(coords):
        return jax.value_and_grad(image_energy)(coords)
    energies, gradients = lax.map(one_image, positions)
    forces = -gradients
    zero_image = jnp.zeros_like(positions[:1])
    delta_up = jnp.concatenate([positions[1:], zero_image], axis=0) - positions
    delta_down = positions - jnp.concatenate([zero_image, positions[:-1]], axis=0)
    v_next = jnp.concatenate([energies[1:], energies[-1:]], axis=0)
    v_prev = jnp.concatenate([energies[:1], energies[:-1]], axis=0)
    weight_up, weight_down = tangent_weights(v_prev, energies, v_next)
    tangent = weight_up[:, None, None] * delta_up + weight_down[:, None, None] * delta_down
    tangent_sq = lax.optimization_barrier(jnp.sum(tangent * tangent, axis=(1, 2)))
    force_tan = lax.optimization_barrier(jnp.sum(forces * tangent, axis=(1, 2)))
    length_up = lax.optimization_barrier(jnp.sum(delta_up * delta_up, axis=(1, 2)))
    length_down = lax.optimization_barrier(jnp.sum(delta_down * delta_down, axis=(1, 2)))
    norm_tan = jnp.sqrt(tangent_sq)
    along = force_tan / norm_tan
    elastic_pull = STIFFNESS * (jnp.sqrt(length_up) - jnp.sqrt(length_down))
    unit = tangent / norm_tan[:, None, None]
    normal_force = forces - (along - elastic_pull)[:, None, None] * unit
    climb_force = forces - 2.0 * along[:, None, None] * unit
    image_rank = jnp.arange(IMAGES, dtype=jnp.int32)
    result = jnp.where((image_rank == climbing[0])[:, None, None], climb_force, normal_force)
    endpoint = (image_rank == 0) | (image_rank == IMAGES - 1)
    result = jnp.where(endpoint[:, None, None], 0.0, result)
    return (result, energies)
```

```python
import math

import jax
import jax.numpy as jnp
from jax import lax
from jax.experimental import pallas as pl
from jax.experimental.pallas import tpu as pltpu
from jax.sharding import PartitionSpec as P

NB = 8
NX = 16
NY = 8
NZL = 2
LAYER = 128
CH = 128
NOFF = 26
ROWS = 40

LATTICE = 2.55
CUTOFF = 5.0
STIFFNESS = 5.0
F32 = jnp.float32
BF16 = jnp.bfloat16
I32 = jnp.int32

OFFSETS = [
    (dx, dy, dz)
    for dz in (-1, 0, 1)
    for dy in (-1, 0, 1)
    for dx in (-1, 0, 1)
    if (dx, dy, dz) != (0, 0, 0)
]
ROW_OF = {offset: row for row, offset in enumerate(OFFSETS)}
LATERALS = [(dx, dy) for dy in (-1, 0, 1) for dx in (-1, 0, 1)]
LATERAL_OF = {lateral: number for number, lateral in enumerate(LATERALS)}


def take(values, index):
    return jnp.take_along_axis(values, index, axis=1, mode="promise_in_bounds")


def iota(shape, dim):
    return lax.broadcasted_iota(I32, shape, dim)


def shifted_site(shape, dx, dy):
    lane = iota(shape, len(shape) - 1)
    return ((((lane >> 4) + dy) & (NY - 1)) << 4) | ((lane + dx) & (NX - 1))


def site_of_row():
    row = iota((32, LAYER), 0)
    code = row + (row >= 13).astype(I32)
    level = (code >= 9).astype(I32) + (code >= 18).astype(I32)
    rest = code - 9 * level
    line = (rest >= 3).astype(I32) + (rest >= 6).astype(I32)
    column = rest - 3 * line
    return shifted_site((32, LAYER), column - 1, line - 1) & (LAYER - 1)


def silu_parts(values):
    sigma = 1.0 / (1.0 + jnp.exp(-values))
    return values * sigma, sigma * (1.0 + values * (1.0 - sigma))


def halves(values):
    high = values.astype(BF16)
    low = (values - high.astype(F32)).astype(BF16)
    return high, low


def stationary(matrix):
    high, low = halves(matrix)
    return jnp.concatenate(
        [jnp.concatenate([high, high], axis=1), jnp.concatenate([low, low], axis=1)], axis=0
    )


def product(packed, values):
    high, low = halves(values)
    out = jnp.dot(packed, jnp.concatenate([high, low], axis=0), preferred_element_type=F32)
    rows = packed.shape[0] // 2
    return out[:rows] + out[rows:]


def radial_stationary(matrix):
    high, low = halves(matrix.T)
    return jnp.concatenate([high, high, low, low], axis=1)


def radial_moving(values):
    high = values.astype(BF16).astype(F32)
    both = jnp.concatenate([high, values - high], axis=0).astype(BF16)
    return jnp.concatenate([both, both], axis=0)


def prepare_kernel(positions, neighbours, ghost_slots, out, site_of_slot):
    slots = ghost_slots[...]
    inverse = jnp.zeros((8, 2 * LAYER), F32)
    for layer in range(NZL):
        hit = (jnp.broadcast_to(slots[layer : layer + 1], (2 * LAYER, LAYER)) == iota((2 * LAYER, LAYER), 0))
        sites = (iota((8, LAYER), 1) + layer * LAYER).astype(F32).astype(BF16)
        inverse = inverse + lax.dot_general(
            sites,
            jnp.where(hit, 1.0, 0.0).astype(BF16),
            (((1,), (1,)), ((), ())),
            preferred_element_type=F32,
        )
    inverse = inverse.astype(I32)
    site_of_slot[...] = inverse
    first = jnp.broadcast_to(inverse[0:1, :LAYER], (32, LAYER))
    second = jnp.broadcast_to(inverse[0:1, LAYER:], (32, LAYER))
    coords = jnp.concatenate([positions[0], positions[1], jnp.zeros((2, 2 * LAYER), F32)], axis=0)
    listed = neighbours[...].astype(F32)
    turned = jnp.concatenate([listed, jnp.zeros((64, LAYER), F32)], axis=0).T
    site = iota((32, LAYER), 1)
    row = iota((32, LAYER), 0)
    for layer in range(NZL):
        here = slice(layer * LAYER, (layer + 1) * LAYER)
        slot = jnp.broadcast_to(slots[layer : layer + 1], (8, LAYER))
        low = slot & (LAYER - 1)
        out[32:40, here] = jnp.where(slot < LAYER, take(coords[:, :LAYER], low), take(coords[:, LAYER:], low))
        slot = jnp.broadcast_to(slots[layer : layer + 1], (32, LAYER))
        picked = take(turned[0:32], slot >> 2)
        for part in range(1, 4):
            picked = jnp.where((slot & 3) == part, take(turned[32 * part : 32 * part + 32], slot >> 2), picked)
        entry = picked.astype(I32)
        low = entry & (LAYER - 1)
        own = jnp.where(entry < LAYER, take(first, low), take(second, low))
        inside = entry < 2 * LAYER
        level = jnp.where(inside, own >> 7, jnp.where(entry < 3 * LAYER, -1, NZL))
        target = jnp.where(inside, own & (LAYER - 1), low)
        column = ((target & (NX - 1)) - (site & (NX - 1)) + 1) & (NX - 1)
        line = ((target >> 4) - (site >> 4) + 1) & (NY - 1)
        code = (level - layer + 1) * 9 + line * 3 + column
        code = jnp.where(code > 13, code - 1, code) & 31
        bits = jnp.where(entry >= 0, jnp.left_shift(jnp.ones_like(code), code), 0)
        bits = bits[0:16] | bits[16:32]
        bits = bits[0:8] | bits[8:16]
        bits = bits[0:4] | bits[4:8]
        bits = bits[0:2] | bits[2:4]
        bits = bits[0:1] | bits[1:2]
        mask = (jnp.broadcast_to(bits, (32, LAYER)) >> row) & 1
        out[0:32, here] = jnp.where(row < NOFF, mask.astype(F32), 0.0)


SIN_TERMS = [(-1.0) ** k / math.factorial(2 * k + 1) for k in range(7)]
COS_TERMS = [(-1.0) ** k / math.factorial(2 * k) for k in range(8)]


def horner(terms, square):
    total = jnp.full_like(square, terms[-1])
    for term in terms[-2::-1]:
        total = total * square + term
    return total


def forces_kernel(
    cell_z,
    parity,
    below,
    middle,
    above,
    path,
    w_radial1,
    w_square,
    w_hidden,
    w_message,
    w_radial2,
    w_output,
    w_energy,
    kept,
    sent,
    sums,
    coords,
    reach,
    inverse_radius,
    phi,
    slope,
    summed,
    radial_mix,
    hidden,
    hidden_slope,
    message,
    edge_radial,
    grad_out,
    grad_summed,
    pair_grad,
    pair_grad_turned,
):
    even = parity[0] == 0
    blocks = [(ref, slice(k * LAYER, (k + 1) * LAYER)) for ref in (below, middle, above) for k in range(4)]
    for level, (ref, here) in enumerate(blocks):
        coords[level, 0:3] = jnp.where(even, ref[32:35, here], ref[35:38, here])
    row = iota((32, LAYER), 0)
    site = site_of_row()
    boxes = (NX * LATTICE, NY * LATTICE, cell_z)

    for e in range(10):
        ref, here = blocks[e + 1]
        mask = ref[0:32, here]
        squared = None
        for c in range(3):
            centre = coords[e + 1, c : c + 1]
            source = jnp.where(
                row < 9,
                jnp.broadcast_to(coords[e, c : c + 1], (32, LAYER)),
                jnp.where(
                    row < 17,
                    jnp.broadcast_to(centre, (32, LAYER)),
                    jnp.broadcast_to(coords[e + 2, c : c + 1], (32, LAYER)),
                ),
            )
            d = take(source, site) - jnp.broadcast_to(centre, (32, LAYER))
            box = jnp.float32(boxes[c])
            half = jnp.float32(0.5) * box
            d = jnp.where(d > half, d - box, jnp.where(d < -half, d + box, d))
            if 3 <= e <= 6:
                reach[e - 3, c] = d
            squared = d * d if squared is None else squared + d * d
        squared = jnp.where(squared > 0.0, squared, 1.0)
        radius = jnp.sqrt(squared)
        inverse = 1.0 / radius
        if 3 <= e <= 6:
            inverse_radius[e - 3] = inverse
        inside = radius < CUTOFF
        angle = jnp.minimum(radius * (math.pi / (2.0 * CUTOFF)), 0.5 * math.pi)
        square = angle * angle
        sine = angle * horner(SIN_TERMS, square)
        cosine = horner(COS_TERMS, square)
        sine1 = 2.0 * sine * cosine
        cosine1 = 1.0 - 2.0 * sine * sine
        smooth = jnp.where(inside, cosine * cosine, 0.0)
        cut_slope = jnp.where(inside, (-math.pi / CUTOFF) * sine * cosine, 0.0)
        scale = mask * smooth * inverse
        tilt = mask * (cut_slope - smooth * inverse) * inverse
        twice = 2.0 * cosine1
        s_prev, s_here = jnp.zeros_like(sine1), sine1
        c_prev, c_here = jnp.ones_like(sine1), cosine1
        for b in range(NB):
            phi[e, pl.ds(b, 32, stride=NB), :] = scale * s_here
            if 2 <= e <= 7:
                slope[e - 2, pl.ds(b, 32, stride=NB), :] = tilt * s_here + scale * (
                    ((b + 1) * math.pi / CUTOFF) * c_here
                )
            s_prev, s_here = s_here, twice * s_here - s_prev
            c_prev, c_here = c_here, twice * c_here - c_prev
        total = phi[e, 0:NB]
        for o in range(1, NOFF):
            total = total + phi[e, o * NB : (o + 1) * NB]
        summed[e] = total

    first = radial_stationary(w_radial1[...])
    second = radial_stationary(w_radial2[...])
    square_t = stationary(w_square[...].T)
    hidden_t = stationary(w_hidden[...].T)
    message_t = stationary(w_message[...].T)

    def nodes(pair, carry):
        e = 2 * pair
        mix = jnp.dot(
            first,
            radial_moving(jnp.concatenate([summed[e], summed[e + 1]], axis=1)),
            preferred_element_type=F32,
        )
        mixed = mix + product(square_t, mix * mix)
        act, act_slope = silu_parts(product(hidden_t, mixed))
        sent_on = product(message_t, act)
        for k in range(2):
            here = slice(k * LAYER, (k + 1) * LAYER)
            radial_mix[e + k] = mix[:, here]
            hidden[e + k] = act[:, here]
            hidden_slope[e + k] = act_slope[:, here]
            for number, (dx, dy) in enumerate(LATERALS):
                part = sent_on[:, here]
                if (dx, dy) != (0, 0):
                    part = take(part, shifted_site((CH, LAYER), dx, dy))
                message[number, e + k] = part
        return carry

    lax.fori_loop(0, 5, nodes, 0)

    output_t = stationary(w_output[...].T)
    output_n = stationary(w_output[...])
    weight = jnp.broadcast_to(w_energy[...], (8, CH)).T[:, 0:1]

    def readout(pair, energy):
        a = 2 * pair
        e = a + 1
        total = jnp.concatenate([hidden[e], hidden[e + 1]], axis=1)
        for o, (dx, dy, dz) in enumerate(OFFSETS):
            here = slice(o * NB, (o + 1) * NB)
            radial = jnp.dot(
                second,
                radial_moving(jnp.concatenate([phi[e, here], phi[e + 1, here]], axis=1)),
                preferred_element_type=F32,
            )
            edge_radial[a, o] = radial[:, :LAYER]
            edge_radial[a + 1, o] = radial[:, LAYER:]
            number = LATERAL_OF[(dx, dy)]
            total = total + radial * jnp.concatenate([message[number, e + dz], message[number, e + 1 + dz]], axis=1)
        act, act_slope = silu_parts(product(output_t, total))
        grad = product(output_n, weight * act_slope)
        grad_out[a] = grad[:, :LAYER]
        grad_out[a + 1] = grad[:, LAYER:]
        part = jnp.sum(weight * act, axis=0, keepdims=True)
        own = jnp.logical_or(pair == 1, pair == 2)
        return energy + jnp.where(own, part, 0.0)

    energy = lax.fori_loop(0, 4, readout, jnp.zeros((1, 2 * LAYER), F32))

    message_n = stationary(w_message[...])
    hidden_n = stationary(w_hidden[...])
    square_n = stationary(w_square[...])
    first_n = stationary(w_radial1[...])
    second_n = stationary(w_radial2[...])

    def back(pair, carry):
        f = 2 * pair
        parts = []
        for k in range(2):
            grad_message = None
            for dx, dy in LATERALS:
                total = None
                for dz in (-1, 0, 1):
                    if (dx, dy, dz) == (0, 0, 0):
                        continue
                    a = f + k + 1 - dz
                    term = grad_out[a] * edge_radial[a, ROW_OF[(dx, dy, dz)]]
                    total = term if total is None else total + term
                if (dx, dy) != (0, 0):
                    total = take(total, shifted_site((CH, LAYER), -dx, -dy))
                grad_message = total if grad_message is None else grad_message + total
            parts.append(grad_message)
        grad_hidden = jnp.concatenate([grad_out[f + 1], grad_out[f + 2]], axis=1) + product(
            message_n, jnp.concatenate(parts, axis=1)
        )
        grad_pre = grad_hidden * jnp.concatenate([hidden_slope[f + 2], hidden_slope[f + 3]], axis=1)
        grad_mixed = product(hidden_n, grad_pre)
        mix = jnp.concatenate([radial_mix[f + 2], radial_mix[f + 3]], axis=1)
        grad_radial = grad_mixed + 2.0 * mix * product(square_n, grad_mixed)
        grad = product(first_n, grad_radial)
        grad_summed[f] = grad[:, :LAYER]
        grad_summed[f + 1] = grad[:, LAYER:]
        return carry

    lax.fori_loop(0, 3, back, 0)

    for f in range(6):
        pair_grad_turned[f] = jnp.zeros((32, LAYER), F32)
    for f in range(4):
        pair_grad[f] = jnp.zeros((32, LAYER), F32)

    def edges(f0, f1, offset0, offset1):
        number = LATERAL_OF[offset0[:2]]
        moved = jnp.concatenate(
            [
                grad_out[f0 + 1] * message[number, f0 + 2 + offset0[2]],
                grad_out[f1 + 1] * message[number, f1 + 2 + offset1[2]],
            ],
            axis=1,
        )
        grad = product(second_n, moved)
        out = []
        for k, (f, offset) in enumerate(((f0, offset0), (f1, offset1))):
            o = ROW_OF[offset]
            value = (grad[:, k * LAYER : (k + 1) * LAYER] + grad_summed[f]) * slope[f, o * NB : (o + 1) * NB]
            out.append(jnp.sum(value, axis=0, keepdims=True))
        return out

    def own_edges(pair, carry):
        f = 2 * pair + 1
        for o, offset in enumerate(OFFSETS):
            left, right = edges(f, f + 1, offset, offset)
            pair_grad[f - 1, o : o + 1] = left
            pair_grad[f, o : o + 1] = right
            pair_grad_turned[f, 25 - o : 26 - o] = left
            pair_grad_turned[f + 1, 25 - o : 26 - o] = right
        return carry

    lax.fori_loop(0, 2, own_edges, 0)
    for dx, dy in LATERALS:
        up, down = (dx, dy, 1), (dx, dy, -1)
        left, right = edges(0, 5, up, down)
        pair_grad_turned[0, 25 - ROW_OF[up] : 26 - ROW_OF[up]] = left
        pair_grad_turned[5, 25 - ROW_OF[down] : 26 - ROW_OF[down]] = right

    force_parts = []
    for f in range(1, 5):
        source = jnp.where(
            row < 9, pair_grad_turned[f - 1], jnp.where(row < 17, pair_grad_turned[f], pair_grad_turned[f + 1])
        )
        pull = (pair_grad[f - 1] + take(source, site)) * inverse_radius[f - 1]
        force_parts.append(
            jnp.concatenate([jnp.sum(pull * reach[f - 1, c], axis=0, keepdims=True) for c in range(3)], axis=0)
        )
    force = jnp.concatenate(force_parts, axis=1)

    low, high = middle[32:35, :], middle[35:38, :]
    beside = path[0:3, :]
    up = jnp.where(even, high - low, beside - high)
    down = jnp.where(even, low - beside, high - low)
    lane = iota((1, LAYER), 1)
    values = jnp.zeros((1, LAYER), F32)
    terms = (
        energy,
        force * up,
        force * down,
        up * up,
        down * down,
        up * down,
    )
    for k, term in enumerate(terms):
        values = values + jnp.where(lane == k, jnp.sum(term), 0.0)
    sums[...] = values
    both = jnp.concatenate([force, beside, jnp.zeros((2, 4 * LAYER), F32)], axis=0)
    left, right = both[:, : 2 * LAYER], both[:, 2 * LAYER :]
    kept[...] = jnp.where(even, left, right)
    sent[...] = jnp.where(even, right, left)


def combine_kernel(image_group, parity, climbing, table, own, kept, received, site_of_slot, out, energies, totals):
    even = parity[0] == 0
    group = image_group[0]
    groups = table.shape[0] // 32
    for g in range(groups):
        total = table[32 * g : 32 * g + 8]
        for k in range(1, 4):
            total = total + table[32 * g + 8 * k : 32 * g + 8 * k + 8]
        total = total[0:4] + total[4:8]
        totals[2 * g : 2 * g + 2] = total[0:2] + total[2:4]
    images = 2 * groups
    low, high = own[32:35, :], own[35:38, :]
    f_kept, f_received = kept[0:3, :], received[0:3, :]
    p_kept, p_received = kept[3:6, :], received[3:6, :]
    sides = (
        (jnp.where(even, f_kept, f_received), high - low, low - jnp.where(even, p_kept, p_received)),
        (jnp.where(even, f_received, f_kept), jnp.where(even, p_received, p_kept) - high, high - low),
    )
    slot = jnp.concatenate([site_of_slot[...]], axis=0)
    for k, (force, up, down) in enumerate(sides):
        image = 2 * group + k
        here = totals[pl.ds(image, 1), :]
        after = totals[pl.ds(jnp.minimum(image + 1, images - 1), 1), :]
        before = totals[pl.ds(jnp.maximum(image - 1, 0), 1), :]
        v_here, v_next, v_prev = here[:, 0:1], after[:, 0:1], before[:, 0:1]
        big = jnp.maximum(jnp.abs(v_next - v_here), jnp.abs(v_prev - v_here))
        small = jnp.minimum(jnp.abs(v_next - v_here), jnp.abs(v_prev - v_here))
        rising = jnp.logical_and(v_next > v_here, v_here > v_prev)
        falling = jnp.logical_and(v_next < v_here, v_here < v_prev)
        higher = v_next > v_prev
        a = jnp.where(rising, 1.0, jnp.where(falling, 0.0, jnp.where(higher, big, small)))
        b = jnp.where(rising, 0.0, jnp.where(falling, 1.0, jnp.where(higher, small, big)))
        fu, fd, uu, dd, ud = (here[:, i : i + 1] for i in range(1, 6))
        tangent_sq = a * a * uu + 2.0 * a * b * ud + b * b * dd
        norm = jnp.sqrt(tangent_sq)
        along = (a * fu + b * fd) / norm
        pull = STIFFNESS * (jnp.sqrt(uu) - jnp.sqrt(dd))
        amount = jnp.where(image == climbing[0], 2.0 * along, along - pull) / norm
        tangent = a * up + b * down
        result = force - amount * tangent
        end = jnp.logical_or(image == 0, image == images - 1)
        result = jnp.where(end, 0.0, result)
        result = jnp.concatenate([result, jnp.zeros((5, 2 * LAYER), F32)], axis=0)
        for part in range(NZL):
            index = slot[:, part * LAYER : (part + 1) * LAYER]
            low_index = index & (LAYER - 1)
            back = jnp.where(index < LAYER, take(result[:, :LAYER], low_index), take(result[:, LAYER:], low_index))
            out[k, :, part * LAYER : (part + 1) * LAYER] = back[0:3]
        energies[k] = here[0, 0]


def vmem():
    return pl.BlockSpec(memory_space=pltpu.VMEM)


def smem():
    return pl.BlockSpec(memory_space=pltpu.SMEM)


def local(
    positions,
    neighbours,
    ghost_slots,
    climbing,
    w_radial1,
    w_square,
    w_hidden,
    w_message,
    w_radial2,
    w_output,
    w_energy,
):
    slabs = lax.axis_size("slab")
    groups = lax.axis_size("image")
    group = lax.axis_index("image")
    slab = lax.axis_index("slab")
    parity = slab % 2
    even = parity == 0
    parity_arg = parity.astype(I32).reshape(1)

    prepared, site_of_slot = pl.pallas_call(
        prepare_kernel,
        out_shape=(
            jax.ShapeDtypeStruct((ROWS, 2 * LAYER), F32),
            jax.ShapeDtypeStruct((8, 2 * LAYER), I32),
        ),
        in_specs=[vmem()] * 3,
        out_specs=(vmem(), vmem()),
    )(positions, neighbours.reshape(64, LAYER), ghost_slots)

    mate = lax.ppermute(prepared, "slab", [(i, i ^ 1) for i in range(slabs)])
    middle = jnp.concatenate([jnp.where(even, prepared, mate), jnp.where(even, mate, prepared)], axis=1)
    below = lax.ppermute(middle, "slab", [(i, (i + 2) % slabs) for i in range(slabs)])
    above = lax.ppermute(middle, "slab", [((i + 2) % slabs, i) for i in range(slabs)])
    mine = jnp.where(even, middle[32:35], middle[35:38])
    hops = []
    for g in range(groups):
        for s in range(slabs):
            if s % 2 and g + 1 < groups:
                hops.append((g * slabs + s, (g + 1) * slabs + s - 1))
            if s % 2 == 0 and g > 0:
                hops.append((g * slabs + s, (g - 1) * slabs + s + 1))
    path = lax.ppermute(mine, ("image", "slab"), hops)

    kept, sent, sums = pl.pallas_call(
        lambda *refs: forces_kernel(slabs * NZL * LATTICE, *refs),
        out_shape=(
            jax.ShapeDtypeStruct((8, 2 * LAYER), F32),
            jax.ShapeDtypeStruct((8, 2 * LAYER), F32),
            jax.ShapeDtypeStruct((1, LAYER), F32),
        ),
        in_specs=[smem()] + [vmem()] * 11,
        out_specs=(vmem(), vmem(), vmem()),
        scratch_shapes=[
            pltpu.VMEM((12, 8, LAYER), F32),
            pltpu.VMEM((4, 3, 32, LAYER), F32),
            pltpu.VMEM((4, 32, LAYER), F32),
            pltpu.VMEM((10, 32 * NB, LAYER), F32),
            pltpu.VMEM((6, 32 * NB, LAYER), F32),
            pltpu.VMEM((10, NB, LAYER), F32),
            pltpu.VMEM((10, CH, LAYER), F32),
            pltpu.VMEM((10, CH, LAYER), F32),
            pltpu.VMEM((10, CH, LAYER), F32),
            pltpu.VMEM((9, 10, CH, LAYER), F32),
            pltpu.VMEM((8, NOFF, CH, LAYER), F32),
            pltpu.VMEM((8, CH, LAYER), F32),
            pltpu.VMEM((6, NB, LAYER), F32),
            pltpu.VMEM((4, 32, LAYER), F32),
            pltpu.VMEM((6, 32, LAYER), F32),
        ],
        compiler_params=pltpu.CompilerParams(vmem_limit_bytes=48 * 1024 * 1024),
    )(
        parity_arg,
        below,
        middle,
        above,
        path,
        w_radial1,
        w_square,
        w_hidden,
        w_message,
        w_radial2,
        w_output,
        w_energy.reshape(1, CH),
    )

    devices = groups * slabs
    received = lax.ppermute(sent, "slab", [(i, i ^ 1) for i in range(slabs)])
    table = lax.all_to_all(
        jnp.broadcast_to(sums[None], (devices, 1, LAYER)), ("image", "slab"), 0, 0, tiled=False
    ).reshape(devices, LAYER)

    return pl.pallas_call(
        combine_kernel,
        out_shape=(
            jax.ShapeDtypeStruct(positions.shape, F32),
            jax.ShapeDtypeStruct((2,), F32),
        ),
        in_specs=[smem()] * 3 + [vmem()] * 5,
        out_specs=(vmem(), smem()),
        scratch_shapes=[pltpu.VMEM((2 * groups, LAYER), F32)],
    )(
        group.astype(I32).reshape(1),
        parity_arg,
        climbing,
        table,
        prepared,
        kept,
        received,
        site_of_slot,
    )


def solution(mesh):
    return jax.shard_map(
        local,
        mesh=mesh,
        in_specs=(
            P("image", None, "slab"),
            P("slab"),
            P(None, "slab"),
            P(),
            P(),
            P(),
            P(),
            P(),
            P(),
            P(),
            P(),
        ),
        out_specs=(P("image", None, "slab"), P("image")),
        check_vma=False,
    )
```

```python
import math

import jax
import jax.numpy as jnp
from jax import lax
from jax.experimental import pallas as pl
from jax.experimental.pallas import tpu as pltpu
from jax.sharding import PartitionSpec as P

NB = 8
NX = 16
NY = 8
NZL = 2
LAYER = 128
CH = 128
NOFF = 26
ROWS = 40

LATTICE = 2.55
CUTOFF = 5.0
STIFFNESS = 5.0
F32 = jnp.float32
BF16 = jnp.bfloat16
I32 = jnp.int32

OFFSETS = [
    (dx, dy, dz)
    for dz in (-1, 0, 1)
    for dy in (-1, 0, 1)
    for dx in (-1, 0, 1)
    if (dx, dy, dz) != (0, 0, 0)
]
ROW_OF = {offset: row for row, offset in enumerate(OFFSETS)}
LATERALS = [(dx, dy) for dy in (-1, 0, 1) for dx in (-1, 0, 1)]
LATERAL_OF = {lateral: number for number, lateral in enumerate(LATERALS)}


def take(values, index):
    return jnp.take_along_axis(values, index, axis=1, mode="promise_in_bounds")


def iota(shape, dim):
    return lax.broadcasted_iota(I32, shape, dim)


def shifted_site(shape, dx, dy):
    lane = iota(shape, len(shape) - 1)
    return ((((lane >> 4) + dy) & (NY - 1)) << 4) | ((lane + dx) & (NX - 1))


def site_of_row():
    row = iota((32, LAYER), 0)
    code = row + (row >= 13).astype(I32)
    level = (code >= 9).astype(I32) + (code >= 18).astype(I32)
    rest = code - 9 * level
    line = (rest >= 3).astype(I32) + (rest >= 6).astype(I32)
    column = rest - 3 * line
    return shifted_site((32, LAYER), column - 1, line - 1) & (LAYER - 1)


def silu_parts(values):
    sigma = 1.0 / (1.0 + jnp.exp(-values))
    return values * sigma, sigma * (1.0 + values * (1.0 - sigma))


def halves(values):
    high = values.astype(BF16)
    low = (values - high.astype(F32)).astype(BF16)
    return high, low


def stationary(matrix):
    high, low = halves(matrix)
    return jnp.concatenate(
        [jnp.concatenate([high, high], axis=1), jnp.concatenate([low, low], axis=1)], axis=0
    )


def product(packed, values):
    high, low = halves(values)
    out = jnp.dot(packed, jnp.concatenate([high, low], axis=0), preferred_element_type=F32)
    rows = packed.shape[0] // 2
    return out[:rows] + out[rows:]


def radial_stationary(matrix):
    high, low = halves(matrix.T)
    return jnp.concatenate([high, high, low, low], axis=1)


def radial_moving(values):
    high = values.astype(BF16).astype(F32)
    both = jnp.concatenate([high, values - high], axis=0).astype(BF16)
    return jnp.concatenate([both, both], axis=0)


def prepare_kernel(packed, out, site_of_slot):
    slots = packed[64:66, :].astype(I32)
    inverse = jnp.zeros((8, 2 * LAYER), F32)
    for layer in range(NZL):
        hit = (jnp.broadcast_to(slots[layer : layer + 1], (2 * LAYER, LAYER)) == iota((2 * LAYER, LAYER), 0))
        sites = (iota((8, LAYER), 1) + layer * LAYER).astype(F32).astype(BF16)
        inverse = inverse + lax.dot_general(
            sites,
            jnp.where(hit, 1.0, 0.0).astype(BF16),
            (((1,), (1,)), ((), ())),
            preferred_element_type=F32,
        )
    inverse = inverse.astype(I32)
    site_of_slot[...] = inverse
    first = jnp.broadcast_to(inverse[0:1, :LAYER], (32, LAYER))
    second = jnp.broadcast_to(inverse[0:1, LAYER:], (32, LAYER))
    sides = [
        jnp.concatenate(
            [packed[66 + 4 * c + 2 * half + k : 67 + 4 * c + 2 * half + k] for k in range(2) for c in range(3)]
            + [jnp.zeros((2, LAYER), F32)],
            axis=0,
        )
        for half in range(2)
    ]
    listed = packed[0:64, :]
    turned = jnp.concatenate([listed, jnp.zeros((64, LAYER), F32)], axis=0).T
    site = iota((32, LAYER), 1)
    row = iota((32, LAYER), 0)
    for layer in range(NZL):
        here = slice(layer * LAYER, (layer + 1) * LAYER)
        slot = jnp.broadcast_to(slots[layer : layer + 1], (8, LAYER))
        low = slot & (LAYER - 1)
        out[32:40, here] = jnp.where(slot < LAYER, take(sides[0], low), take(sides[1], low))
        slot = jnp.broadcast_to(slots[layer : layer + 1], (32, LAYER))
        picked = take(turned[0:32], slot >> 2)
        for part in range(1, 4):
            picked = jnp.where((slot & 3) == part, take(turned[32 * part : 32 * part + 32], slot >> 2), picked)
        entry = picked.astype(I32)
        low = entry & (LAYER - 1)
        own = jnp.where(entry < LAYER, take(first, low), take(second, low))
        inside = entry < 2 * LAYER
        level = jnp.where(inside, own >> 7, jnp.where(entry < 3 * LAYER, -1, NZL))
        target = jnp.where(inside, own & (LAYER - 1), low)
        column = ((target & (NX - 1)) - (site & (NX - 1)) + 1) & (NX - 1)
        line = ((target >> 4) - (site >> 4) + 1) & (NY - 1)
        code = (level - layer + 1) * 9 + line * 3 + column
        code = jnp.where(code > 13, code - 1, code) & 31
        bits = jnp.where(entry >= 0, jnp.left_shift(jnp.ones_like(code), code), 0)
        bits = bits[0:16] | bits[16:32]
        bits = bits[0:8] | bits[8:16]
        bits = bits[0:4] | bits[4:8]
        bits = bits[0:2] | bits[2:4]
        bits = bits[0:1] | bits[1:2]
        mask = (jnp.broadcast_to(bits, (32, LAYER)) >> row) & 1
        out[0:32, here] = jnp.where(row < NOFF, mask.astype(F32), 0.0)


SIN_TERMS = [(-1.0) ** k / math.factorial(2 * k + 1) for k in range(7)]
COS_TERMS = [(-1.0) ** k / math.factorial(2 * k) for k in range(8)]


def horner(terms, square):
    total = jnp.full_like(square, terms[-1])
    for term in terms[-2::-1]:
        total = total * square + term
    return total


SQUARE, HIDDEN, MESSAGE, OUTPUT = range(4)


def weights_kernel(squares, radials, turned, straight, radial, radial_turned, energy):
    for number in range(4):
        turned[number] = stationary(squares[number].T)
        straight[number] = stationary(squares[number])
    for number in range(2):
        radial[number] = stationary(radials[number])
        radial_turned[number] = radial_stationary(radials[number])
    energy[...] = jnp.broadcast_to(radials[2, 0:1], (CH, CH)).T


def stacked(arrays):
    shape = (len(arrays),) + arrays[0].shape
    out = jnp.broadcast_to(arrays[-1][None], shape)
    for number, array in enumerate(arrays[:-1]):
        out = jnp.where(iota(shape, 0) == number, jnp.broadcast_to(array[None], shape), out)
    return out


def forward_kernel(
    cell_z,
    parity,
    below,
    middle,
    above,
    turned,
    straight,
    radial_turned,
    w_energy,
    along,
    reach,
    inverse_radius,
    slope,
    radial_mix,
    hidden_slope,
    message,
    phi,
    grad_out,
    coords,
    summed,
    hidden,
):
    even = parity[0] == 0
    blocks = [(ref, slice(k * LAYER, (k + 1) * LAYER)) for ref in (below, middle, above) for k in range(4)]
    for level, (ref, here) in enumerate(blocks):
        coords[level, 0:3] = jnp.where(even, ref[32:35, here], ref[35:38, here])
    row = iota((32, LAYER), 0)
    site = site_of_row()
    boxes = (NX * LATTICE, NY * LATTICE, cell_z)

    for e in range(10):
        ref, here = blocks[e + 1]
        mask = ref[0:32, here]
        squared = None
        for c in range(3):
            centre = coords[e + 1, c : c + 1]
            source = jnp.where(
                row < 9,
                jnp.broadcast_to(coords[e, c : c + 1], (32, LAYER)),
                jnp.where(
                    row < 17,
                    jnp.broadcast_to(centre, (32, LAYER)),
                    jnp.broadcast_to(coords[e + 2, c : c + 1], (32, LAYER)),
                ),
            )
            d = take(source, site) - jnp.broadcast_to(centre, (32, LAYER))
            box = jnp.float32(boxes[c])
            half = jnp.float32(0.5) * box
            d = jnp.where(d > half, d - box, jnp.where(d < -half, d + box, d))
            if 3 <= e <= 6:
                reach[e - 3, c] = d
            squared = d * d if squared is None else squared + d * d
        squared = jnp.where(squared > 0.0, squared, 1.0)
        radius = jnp.sqrt(squared)
        inverse = 1.0 / radius
        if 3 <= e <= 6:
            inverse_radius[e - 3] = inverse
        inside = radius < CUTOFF
        angle = jnp.minimum(radius * (math.pi / (2.0 * CUTOFF)), 0.5 * math.pi)
        square = angle * angle
        sine = angle * horner(SIN_TERMS, square)
        cosine = horner(COS_TERMS, square)
        sine1 = 2.0 * sine * cosine
        cosine1 = 1.0 - 2.0 * sine * sine
        smooth = jnp.where(inside, cosine * cosine, 0.0)
        cut_slope = jnp.where(inside, (-math.pi / CUTOFF) * sine * cosine, 0.0)
        scale = mask * smooth * inverse
        tilt = mask * (cut_slope - smooth * inverse) * inverse
        twice = 2.0 * cosine1
        s_prev, s_here = jnp.zeros_like(sine1), sine1
        c_prev, c_here = jnp.ones_like(sine1), cosine1
        for b in range(NB):
            phi[e, pl.ds(b, 32, stride=NB), :] = scale * s_here
            if 2 <= e <= 7:
                slope[e - 2, pl.ds(b, 32, stride=NB), :] = tilt * s_here + scale * (
                    ((b + 1) * math.pi / CUTOFF) * c_here
                )
            s_prev, s_here = s_here, twice * s_here - s_prev
            c_prev, c_here = c_here, twice * c_here - c_prev
        total = phi[e, 0:NB]
        for o in range(1, NOFF):
            total = total + phi[e, o * NB : (o + 1) * NB]
        summed[e] = total

    first, second = radial_turned[0], radial_turned[1]
    square_t, hidden_t, message_t = turned[SQUARE], turned[HIDDEN], turned[MESSAGE]

    def nodes(pair):
        e = 2 * pair
        mix = jnp.dot(
            first,
            radial_moving(jnp.concatenate([summed[e], summed[e + 1]], axis=1)),
            preferred_element_type=F32,
        )
        mixed = mix + product(square_t, mix * mix)
        act, act_slope = silu_parts(product(hidden_t, mixed))
        sent_on = product(message_t, act)
        for k in range(2):
            here = slice(k * LAYER, (k + 1) * LAYER)
            hidden[e + k] = act[:, here]
            if 2 <= e <= 6:
                radial_mix[e + k - 2] = mix[:, here]
                hidden_slope[e + k - 2] = act_slope[:, here]
            for number, (dx, dy) in enumerate(LATERALS):
                part = sent_on[:, here]
                if (dx, dy) != (0, 0):
                    part = take(part, shifted_site((CH, LAYER), dx, dy))
                message[number, e + k] = part

    for pair in range(5):
        nodes(pair)

    output_t, output_n = turned[OUTPUT], straight[OUTPUT]
    weight = jnp.concatenate([w_energy[...], w_energy[...]], axis=1)

    def readout(pair):
        a = 2 * pair
        e = a + 1
        total = jnp.concatenate([hidden[e], hidden[e + 1]], axis=1)
        for o, (dx, dy, dz) in enumerate(OFFSETS):
            here = slice(o * NB, (o + 1) * NB)
            radial = jnp.dot(
                second,
                radial_moving(jnp.concatenate([phi[e, here], phi[e + 1, here]], axis=1)),
                preferred_element_type=F32,
            )
            number = LATERAL_OF[(dx, dy)]
            total = total + radial * jnp.concatenate([message[number, e + dz], message[number, e + 1 + dz]], axis=1)
        act, act_slope = silu_parts(product(output_t, total))
        grad = product(output_n, weight * act_slope)
        grad_out[a] = grad[:, :LAYER]
        grad_out[a + 1] = grad[:, LAYER:]
        return jnp.sum(weight * act, axis=0, keepdims=True)

    parts = [readout(pair) for pair in range(4)]
    energy = parts[1] + parts[2]

    along[0:3] = jnp.where(even, middle[32:35, :], middle[35:38, :])
    along[3:4] = jnp.where(iota((1, 4 * LAYER), 1) == 0, jnp.sum(energy), 0.0)
    along[4:8] = jnp.zeros((4, 4 * LAYER), F32)


def backward_kernel(
    reach,
    inverse_radius,
    slope,
    radial_mix,
    hidden_slope,
    message,
    phi,
    grad_out,
    straight,
    radial,
    radial_turned,
    forces,
    grad_summed,
    pair_grad,
    pair_grad_turned,
):
    row = iota((32, LAYER), 0)
    site = site_of_row()
    square_n, hidden_n, message_n = straight[SQUARE], straight[HIDDEN], straight[MESSAGE]
    first_n, second_n = radial[0], radial[1]
    second = radial_turned[1]

    def back(pair):
        f = 2 * pair
        parts = [None, None]
        for dx, dy in LATERALS:
            total = None
            for dz in (-1, 0, 1):
                if (dx, dy, dz) == (0, 0, 0):
                    continue
                a = f + 1 - dz
                o = ROW_OF[(dx, dy, dz)]
                here = slice(o * NB, (o + 1) * NB)
                edge_radial = jnp.dot(
                    second,
                    radial_moving(jnp.concatenate([phi[a + 1, here], phi[a + 2, here]], axis=1)),
                    preferred_element_type=F32,
                )
                term = edge_radial * jnp.concatenate([grad_out[a], grad_out[a + 1]], axis=1)
                total = term if total is None else total + term
            for k in range(2):
                part = total[:, k * LAYER : (k + 1) * LAYER]
                if (dx, dy) != (0, 0):
                    part = take(part, shifted_site((CH, LAYER), -dx, -dy))
                parts[k] = part if parts[k] is None else parts[k] + part
        grad_hidden = jnp.concatenate([grad_out[f + 1], grad_out[f + 2]], axis=1) + product(
            message_n, jnp.concatenate(parts, axis=1)
        )
        grad_pre = grad_hidden * jnp.concatenate([hidden_slope[f], hidden_slope[f + 1]], axis=1)
        grad_mixed = product(hidden_n, grad_pre)
        mix = jnp.concatenate([radial_mix[f], radial_mix[f + 1]], axis=1)
        grad_radial = grad_mixed + 2.0 * mix * product(square_n, grad_mixed)
        grad = product(first_n, grad_radial)
        grad_summed[f] = grad[:, :LAYER]
        grad_summed[f + 1] = grad[:, LAYER:]

    for pair in range(3):
        back(pair)

    for f in range(6):
        pair_grad_turned[f] = jnp.zeros((32, LAYER), F32)
    for f in range(4):
        pair_grad[f] = jnp.zeros((32, LAYER), F32)

    def edges(f0, f1, offset0, offset1):
        number = LATERAL_OF[offset0[:2]]
        moved = jnp.concatenate(
            [
                grad_out[f0 + 1] * message[number, f0 + 2 + offset0[2]],
                grad_out[f1 + 1] * message[number, f1 + 2 + offset1[2]],
            ],
            axis=1,
        )
        grad = product(second_n, moved)
        out = []
        for k, (f, offset) in enumerate(((f0, offset0), (f1, offset1))):
            o = ROW_OF[offset]
            value = (grad[:, k * LAYER : (k + 1) * LAYER] + grad_summed[f]) * slope[f, o * NB : (o + 1) * NB]
            out.append(jnp.sum(value, axis=0, keepdims=True))
        return out

    def own_edges(pair):
        f = 2 * pair + 1
        for o, offset in enumerate(OFFSETS):
            left, right = edges(f, f + 1, offset, offset)
            pair_grad[f - 1, o : o + 1] = left
            pair_grad[f, o : o + 1] = right
            pair_grad_turned[f, 25 - o : 26 - o] = left
            pair_grad_turned[f + 1, 25 - o : 26 - o] = right

    for pair in range(2):
        own_edges(pair)
    for dx, dy in LATERALS:
        up, down = (dx, dy, 1), (dx, dy, -1)
        left, right = edges(0, 5, up, down)
        pair_grad_turned[0, 25 - ROW_OF[up] : 26 - ROW_OF[up]] = left
        pair_grad_turned[5, 25 - ROW_OF[down] : 26 - ROW_OF[down]] = right

    force_parts = []
    for f in range(1, 5):
        source = jnp.where(
            row < 9, pair_grad_turned[f - 1], jnp.where(row < 17, pair_grad_turned[f], pair_grad_turned[f + 1])
        )
        pull = (pair_grad[f - 1] + take(source, site)) * inverse_radius[f - 1]
        force_parts.append(
            jnp.concatenate([jnp.sum(pull * reach[f - 1, c], axis=0, keepdims=True) for c in range(3)], axis=0)
        )
    force = jnp.concatenate(force_parts, axis=1)

    forces[0:3] = force
    forces[3:8] = jnp.zeros((5, 4 * LAYER), F32)


def sums_kernel(parity, middle, forces, along, path, table, kept, sent):
    even = parity[0] == 0
    low, high = middle[32:35, :], middle[35:38, :]
    force, beside = forces[0:3], path[0:3]
    up = jnp.where(even, high - low, beside - high)
    down = jnp.where(even, low - beside, high - low)
    lane = iota((1, LAYER), 1)
    values = jnp.where(
        lane == 0, along[3:4, 0:1], jnp.where(lane == 6, jnp.broadcast_to(path[3:4, 0:1], (1, LAYER)), 0.0)
    )
    for k, term in enumerate((force * up, force * down, up * up, down * down, up * down)):
        total = jnp.sum(jnp.sum(term, axis=1, keepdims=True), axis=0, keepdims=True)
        values = values + jnp.where(lane == k + 1, total, 0.0)
    table[...] = jnp.broadcast_to(values, table.shape)
    both = jnp.concatenate([force, beside, jnp.zeros((2, 4 * LAYER), F32)], axis=0)
    left, right = both[:, : 2 * LAYER], both[:, 2 * LAYER :]
    kept[...] = jnp.where(even, left, right)
    sent[...] = jnp.where(even, right, left)


def combine_kernel(images, image_group, parity, climbing, table, own, kept, received, site_of_slot, out, energies):
    even = parity[0] == 0
    total = table[0:8]
    for k in range(8, table.shape[0], 8):
        total = total + table[k : k + 8]
    total = total[0:4] + total[4:8]
    total = total[0:2] + total[2:4]
    energy = (total[0:1, 6:7], total[0:1, 0:1], total[1:2, 0:1], total[1:2, 6:7])
    low, high = own[32:35, :], own[35:38, :]
    f_kept, f_received = kept[0:3, :], received[0:3, :]
    p_kept, p_received = kept[3:6, :], received[3:6, :]
    sides = (
        (jnp.where(even, f_kept, f_received), high - low, low - jnp.where(even, p_kept, p_received)),
        (jnp.where(even, f_received, f_kept), jnp.where(even, p_received, p_kept) - high, high - low),
    )
    slot = site_of_slot[...]
    for k, (force, up, down) in enumerate(sides):
        image = 2 * image_group[0] + k
        here = total[k : k + 1]
        v_prev, v_here, v_next = energy[k : k + 3]
        big = jnp.maximum(jnp.abs(v_next - v_here), jnp.abs(v_prev - v_here))
        small = jnp.minimum(jnp.abs(v_next - v_here), jnp.abs(v_prev - v_here))
        rising = jnp.logical_and(v_next > v_here, v_here > v_prev)
        falling = jnp.logical_and(v_next < v_here, v_here < v_prev)
        higher = v_next > v_prev
        a = jnp.where(rising, 1.0, jnp.where(falling, 0.0, jnp.where(higher, big, small)))
        b = jnp.where(rising, 0.0, jnp.where(falling, 1.0, jnp.where(higher, small, big)))
        fu, fd, uu, dd, ud = (here[:, i : i + 1] for i in range(1, 6))
        tangent_sq = a * a * uu + 2.0 * a * b * ud + b * b * dd
        norm = jnp.sqrt(tangent_sq)
        along = (a * fu + b * fd) / norm
        pull = STIFFNESS * (jnp.sqrt(uu) - jnp.sqrt(dd))
        amount = jnp.where(image == climbing[0], 2.0 * along, along - pull) / norm
        tangent = a * up + b * down
        result = force - amount * tangent
        end = jnp.logical_or(image == 0, image == images - 1)
        result = jnp.where(end, 0.0, result)
        result = jnp.concatenate([result, jnp.zeros((5, 2 * LAYER), F32)], axis=0)
        for part in range(NZL):
            index = slot[:, part * LAYER : (part + 1) * LAYER]
            low_index = index & (LAYER - 1)
            back = jnp.where(index < LAYER, take(result[:, :LAYER], low_index), take(result[:, LAYER:], low_index))
            for c in range(3):
                out[c, k : k + 1, part * LAYER : (part + 1) * LAYER] = back[c : c + 1]
        energies[k] = here[0, 0]


def vmem():
    return pl.BlockSpec(memory_space=pltpu.VMEM)


def smem():
    return pl.BlockSpec(memory_space=pltpu.SMEM)


def local(
    positions,
    neighbours,
    ghost_slots,
    climbing,
    w_radial1,
    w_square,
    w_hidden,
    w_message,
    w_radial2,
    w_output,
    w_energy,
):
    slabs = lax.axis_size("slab")
    groups = lax.axis_size("image")
    group = lax.axis_index("image")
    slab = lax.axis_index("slab")
    parity = slab % 2
    even = parity == 0
    parity_arg = parity.astype(I32).reshape(1)

    small = pltpu.CompilerParams(vmem_limit_bytes=4 * 1024 * 1024)
    packed = jnp.concatenate(
        [
            neighbours.reshape(64, LAYER).astype(F32),
            ghost_slots.astype(F32),
            positions.transpose(1, 0, 2).reshape(3, 2, 2, LAYER).transpose(0, 2, 1, 3).reshape(12, LAYER),
        ],
        axis=0,
    )
    prepared, site_of_slot = pl.pallas_call(
        prepare_kernel,
        out_shape=(
            jax.ShapeDtypeStruct((ROWS, 2 * LAYER), F32),
            jax.ShapeDtypeStruct((8, 2 * LAYER), I32),
        ),
        in_specs=[vmem()],
        out_specs=(vmem(), vmem()),
        compiler_params=small,
    )(packed)

    mate = lax.ppermute(prepared, "slab", [(i, i ^ 1) for i in range(slabs)])
    middle = jnp.concatenate([jnp.where(even, prepared, mate), jnp.where(even, mate, prepared)], axis=1)
    below = lax.ppermute(middle, "slab", [(i, (i + 2) % slabs) for i in range(slabs)])
    above = lax.ppermute(middle, "slab", [((i + 2) % slabs, i) for i in range(slabs)])

    def whole(*extents):
        return jax.ShapeDtypeStruct(extents, F32)

    turned, straight, radial, radial_turned, energy_column = pl.pallas_call(
        weights_kernel,
        out_shape=(
            jax.ShapeDtypeStruct((4, 2 * CH, 2 * CH), BF16),
            jax.ShapeDtypeStruct((4, 2 * CH, 2 * CH), BF16),
            jax.ShapeDtypeStruct((2, 2 * NB, 2 * CH), BF16),
            jax.ShapeDtypeStruct((2, CH, 4 * NB), BF16),
            whole(CH, CH),
        ),
        in_specs=[vmem()] * 2,
        out_specs=tuple(vmem() for _ in range(5)),
        compiler_params=small,
        cost_estimate=pl.CostEstimate(flops=10**8, bytes_accessed=1 << 22, transcendentals=0),
    )(
        stacked([w_square, w_hidden, w_message, w_output]),
        stacked([w_radial1, w_radial2, jnp.broadcast_to(w_energy[None], (NB, CH))]),
    )

    along, *saved = pl.pallas_call(
        lambda *refs: forward_kernel(slabs * NZL * LATTICE, *refs),
        out_shape=(
            whole(8, 4 * LAYER),
            whole(4, 3, 32, LAYER),
            whole(4, 32, LAYER),
            whole(6, 32 * NB, LAYER),
            whole(6, CH, LAYER),
            whole(6, CH, LAYER),
            whole(9, 10, CH, LAYER),
            whole(10, 32 * NB, LAYER),
            whole(8, CH, LAYER),
        ),
        in_specs=[smem()] + [vmem()] * 7,
        out_specs=tuple(vmem() for _ in range(9)),
        scratch_shapes=[
            pltpu.VMEM((12, 8, LAYER), F32),
            pltpu.VMEM((10, NB, LAYER), F32),
            pltpu.VMEM((10, CH, LAYER), F32),
        ],
        compiler_params=pltpu.CompilerParams(vmem_limit_bytes=20 * 1024 * 1024),
    )(
        parity_arg,
        below,
        middle,
        above,
        turned,
        straight,
        radial_turned,
        energy_column,
    )

    hops = []
    for g in range(groups):
        for s in range(slabs):
            if s % 2 and g + 1 < groups:
                hops.append((g * slabs + s, (g + 1) * slabs + s - 1))
            if s % 2 == 0 and g > 0:
                hops.append((g * slabs + s, (g - 1) * slabs + s + 1))
    path = lax.ppermute(along, ("image", "slab"), hops)

    forces = pl.pallas_call(
        backward_kernel,
        out_shape=whole(8, 4 * LAYER),
        in_specs=[vmem()] * 11,
        out_specs=vmem(),
        scratch_shapes=[
            pltpu.VMEM((6, NB, LAYER), F32),
            pltpu.VMEM((4, 32, LAYER), F32),
            pltpu.VMEM((6, 32, LAYER), F32),
        ],
        compiler_params=pltpu.CompilerParams(vmem_limit_bytes=20 * 1024 * 1024),
        cost_estimate=pl.CostEstimate(flops=4 * 10**9, bytes_accessed=1 << 22, transcendentals=0),
    )(*saved, straight, radial, radial_turned)

    table, kept, sent = pl.pallas_call(
        sums_kernel,
        out_shape=(whole(slabs, LAYER), whole(8, 2 * LAYER), whole(8, 2 * LAYER)),
        in_specs=[smem()] + [vmem()] * 4,
        out_specs=(vmem(), vmem(), vmem()),
        compiler_params=small,
    )(parity_arg, middle, forces, along, path)

    received = lax.ppermute(sent, "slab", [(i, i ^ 1) for i in range(slabs)])
    table = lax.all_to_all(table.reshape(slabs, 1, LAYER), "slab", 0, 0, tiled=False).reshape(slabs, LAYER)

    result, energies = pl.pallas_call(
        lambda *refs: combine_kernel(2 * groups, *refs),
        out_shape=(
            jax.ShapeDtypeStruct((3, 2, 2 * LAYER), F32),
            jax.ShapeDtypeStruct((2,), F32),
        ),
        in_specs=[smem()] * 3 + [vmem()] * 5,
        out_specs=(vmem(), smem()),
        compiler_params=small,
    )(
        group.astype(I32).reshape(1),
        parity_arg,
        climbing,
        table,
        prepared,
        kept,
        received,
        site_of_slot,
    )
    return result.transpose(1, 0, 2), energies


def solution(mesh):
    return jax.shard_map(
        local,
        mesh=mesh,
        in_specs=(
            P("image", None, "slab"),
            P("slab"),
            P(None, "slab"),
            P(),
            P(),
            P(),
            P(),
            P(),
            P(),
            P(),
            P(),
        ),
        out_specs=(P("image", None, "slab"), P("image")),
        check_vma=False,
    )
```

```python
import math

import jax
import jax.numpy as jnp
from jax import lax
from jax.experimental import pallas as pl
from jax.experimental.pallas import tpu as pltpu
from jax.sharding import PartitionSpec as P

NB = 8
NX = 16
NY = 8
NZL = 2
LAYER = 128
CH = 128
NOFF = 26
ROWS = 32

LATTICE = 2.55
CUTOFF = 5.0
STIFFNESS = 5.0
F32 = jnp.float32
BF16 = jnp.bfloat16
I32 = jnp.int32

OFFSETS = [
    (dx, dy, dz)
    for dz in (-1, 0, 1)
    for dy in (-1, 0, 1)
    for dx in (-1, 0, 1)
    if (dx, dy, dz) != (0, 0, 0)
]
ROW_OF = {offset: row for row, offset in enumerate(OFFSETS)}
LATERALS = [(dx, dy) for dy in (-1, 0, 1) for dx in (-1, 0, 1)]
LATERAL_OF = {lateral: number for number, lateral in enumerate(LATERALS)}


def take(values, index):
    return jnp.take_along_axis(values, index, axis=1, mode="promise_in_bounds")


def iota(shape, dim):
    return lax.broadcasted_iota(I32, shape, dim)


def shifted_site(shape, dx, dy):
    lane = iota(shape, len(shape) - 1)
    return ((((lane >> 4) + dy) & (NY - 1)) << 4) | ((lane + dx) & (NX - 1))


def site_of_row():
    row = iota((32, LAYER), 0)
    code = row + (row >= 13).astype(I32)
    level = (code >= 9).astype(I32) + (code >= 18).astype(I32)
    rest = code - 9 * level
    line = (rest >= 3).astype(I32) + (rest >= 6).astype(I32)
    column = rest - 3 * line
    return shifted_site((32, LAYER), column - 1, line - 1) & (LAYER - 1)


def silu_parts(values):
    sigma = 1.0 / (1.0 + jnp.exp(-values))
    return values * sigma, sigma * (1.0 + values * (1.0 - sigma))


def halves(values):
    high = values.astype(BF16)
    low = (values - high.astype(F32)).astype(BF16)
    return high, low


def stationary(matrix):
    high, low = halves(matrix)
    return jnp.concatenate(
        [jnp.concatenate([high, high], axis=1), jnp.concatenate([low, low], axis=1)], axis=0
    )


def product(packed, values):
    high, low = halves(values)
    out = jnp.dot(packed, jnp.concatenate([high, low], axis=0), preferred_element_type=F32)
    rows = packed.shape[0] // 2
    return out[:rows] + out[rows:]


def radial_stationary(matrix):
    high, low = halves(matrix.T)
    return jnp.concatenate([high, high, low, low], axis=1)


def radial_moving(values):
    high = values.astype(BF16).astype(F32)
    both = jnp.concatenate([high, values - high], axis=0).astype(BF16)
    return jnp.concatenate([both, both], axis=0)


def prepare_kernel(packed, positions, out, site_of_slot):
    slots = packed[64:66, :]
    inverse = jnp.zeros((8, 2 * LAYER), F32)
    for layer in range(NZL):
        hit = (jnp.broadcast_to(slots[layer : layer + 1], (2 * LAYER, LAYER)) == iota((2 * LAYER, LAYER), 0))
        sites = (iota((8, LAYER), 1) + layer * LAYER).astype(F32).astype(BF16)
        inverse = inverse + lax.dot_general(
            sites,
            jnp.where(hit, 1.0, 0.0).astype(BF16),
            (((1,), (1,)), ((), ())),
            preferred_element_type=F32,
        )
    inverse = inverse.astype(I32)
    site_of_slot[...] = inverse
    first = jnp.broadcast_to(inverse[0:1, :LAYER], (32, LAYER))
    second = jnp.broadcast_to(inverse[0:1, LAYER:], (32, LAYER))
    sides = [
        jnp.concatenate(
            [positions[c, k : k + 1, half * LAYER : (half + 1) * LAYER] for k in range(2) for c in range(3)]
            + [jnp.zeros((2, LAYER), F32)],
            axis=0,
        )
        for half in range(2)
    ]
    listed = packed[0:64, :].astype(F32)
    turned = jnp.concatenate([listed, jnp.zeros((64, LAYER), F32)], axis=0).T
    site = iota((32, LAYER), 1)
    row = iota((32, LAYER), 0)
    for layer in range(NZL):
        here = slice(layer * LAYER, (layer + 1) * LAYER)
        slot = jnp.broadcast_to(slots[layer : layer + 1], (8, LAYER))
        low = slot & (LAYER - 1)
        coords = jnp.where(slot < LAYER, take(sides[0], low), take(sides[1], low))
        slot = jnp.broadcast_to(slots[layer : layer + 1], (32, LAYER))
        picked = take(turned[0:32], slot >> 2)
        for part in range(1, 4):
            picked = jnp.where((slot & 3) == part, take(turned[32 * part : 32 * part + 32], slot >> 2), picked)
        entry = picked.astype(I32)
        low = entry & (LAYER - 1)
        own = jnp.where(entry < LAYER, take(first, low), take(second, low))
        inside = entry < 2 * LAYER
        level = jnp.where(inside, own >> 7, jnp.where(entry < 3 * LAYER, -1, NZL))
        target = jnp.where(inside, own & (LAYER - 1), low)
        column = ((target & (NX - 1)) - (site & (NX - 1)) + 1) & (NX - 1)
        line = ((target >> 4) - (site >> 4) + 1) & (NY - 1)
        code = (level - layer + 1) * 9 + line * 3 + column
        code = jnp.where(code > 13, code - 1, code) & 31
        bits = jnp.where(entry >= 0, jnp.left_shift(jnp.ones_like(code), code), 0)
        bits = bits[0:16] | bits[16:32]
        bits = bits[0:8] | bits[8:16]
        bits = bits[0:4] | bits[4:8]
        bits = bits[0:2] | bits[2:4]
        bits = bits[0:1] | bits[1:2]
        mask = (jnp.broadcast_to(bits, (32, LAYER)) >> row) & 1
        out[0:NOFF, here] = mask[0:NOFF].astype(F32)
        out[NOFF:32, here] = coords[0:6]


SIN_TERMS = [(-1.0) ** k / math.factorial(2 * k + 1) for k in range(7)]
COS_TERMS = [(-1.0) ** k / math.factorial(2 * k) for k in range(8)]


def horner(terms, square):
    total = jnp.full_like(square, terms[-1])
    for term in terms[-2::-1]:
        total = total * square + term
    return total


SQUARE, HIDDEN, MESSAGE, OUTPUT = range(4)


def weights_kernel(squares, radials, turned, straight, radial, radial_turned, energy):
    for number in range(4):
        turned[number] = stationary(squares[number].T)
        straight[number] = stationary(squares[number])
    for number in range(2):
        radial[number] = stationary(radials[number])
        radial_turned[number] = radial_stationary(radials[number])
    energy[...] = jnp.broadcast_to(radials[2, 0:1], (CH, CH)).T


def stacked(arrays):
    shape = (len(arrays),) + arrays[0].shape
    out = jnp.broadcast_to(arrays[-1][None], shape)
    for number, array in enumerate(arrays[:-1]):
        out = jnp.where(iota(shape, 0) == number, jnp.broadcast_to(array[None], shape), out)
    return out


def forward_kernel(
    cell_z,
    parity,
    far,
    middle,
    traded,
    turned,
    straight,
    radial_turned,
    w_energy,
    along,
    reach,
    inverse_radius,
    slope,
    radial_mix,
    hidden_slope,
    message,
    phi,
    grad_out,
    coords,
    summed,
    hidden,
):
    even = parity[0] == 0

    def level_rows(level, first, last):
        here = slice(level % 4 * LAYER, (level % 4 + 1) * LAYER)
        if 4 <= level < 8:
            return middle[first:last, here]
        mine, other = far[first:last, here], traded[first:last, here]
        return jnp.where(even, mine, other) if level < 4 else jnp.where(even, other, mine)

    for level in range(12):
        both = level_rows(level, 24, 32)
        coords[level, 0:3] = jnp.where(even, both[2:5], both[5:8])
    row = iota((32, LAYER), 0)
    site = site_of_row()
    boxes = (NX * LATTICE, NY * LATTICE, cell_z)

    for e in range(10):
        mask = jnp.where(row < NOFF, level_rows(e + 1, 0, 32), 0.0)
        squared = None
        for c in range(3):
            centre = coords[e + 1, c : c + 1]
            source = jnp.where(
                row < 9,
                jnp.broadcast_to(coords[e, c : c + 1], (32, LAYER)),
                jnp.where(
                    row < 17,
                    jnp.broadcast_to(centre, (32, LAYER)),
                    jnp.broadcast_to(coords[e + 2, c : c + 1], (32, LAYER)),
                ),
            )
            d = take(source, site) - jnp.broadcast_to(centre, (32, LAYER))
            box = jnp.float32(boxes[c])
            half = jnp.float32(0.5) * box
            d = jnp.where(d > half, d - box, jnp.where(d < -half, d + box, d))
            if 3 <= e <= 6:
                reach[e - 3, c] = d
            squared = d * d if squared is None else squared + d * d
        squared = jnp.where(squared > 0.0, squared, 1.0)
        radius = jnp.sqrt(squared)
        inverse = 1.0 / radius
        if 3 <= e <= 6:
            inverse_radius[e - 3] = inverse
        inside = radius < CUTOFF
        angle = jnp.minimum(radius * (math.pi / (2.0 * CUTOFF)), 0.5 * math.pi)
        square = angle * angle
        sine = angle * horner(SIN_TERMS, square)
        cosine = horner(COS_TERMS, square)
        sine1 = 2.0 * sine * cosine
        cosine1 = 1.0 - 2.0 * sine * sine
        smooth = jnp.where(inside, cosine * cosine, 0.0)
        cut_slope = jnp.where(inside, (-math.pi / CUTOFF) * sine * cosine, 0.0)
        scale = mask * smooth * inverse
        tilt = mask * (cut_slope - smooth * inverse) * inverse
        twice = 2.0 * cosine1
        s_prev, s_here = jnp.zeros_like(sine1), sine1
        c_prev, c_here = jnp.ones_like(sine1), cosine1
        for b in range(NB):
            phi[e, pl.ds(b, 32, stride=NB), :] = scale * s_here
            if 2 <= e <= 7:
                slope[e - 2, pl.ds(b, 32, stride=NB), :] = tilt * s_here + scale * (
                    ((b + 1) * math.pi / CUTOFF) * c_here
                )
            s_prev, s_here = s_here, twice * s_here - s_prev
            c_prev, c_here = c_here, twice * c_here - c_prev
        total = phi[e, 0:NB]
        for o in range(1, NOFF):
            total = total + phi[e, o * NB : (o + 1) * NB]
        summed[e] = total

    first, second = radial_turned[0], radial_turned[1]
    square_t, hidden_t, message_t = turned[SQUARE], turned[HIDDEN], turned[MESSAGE]

    mix = jnp.dot(
        first,
        radial_moving(jnp.concatenate([summed[e] for e in range(10)], axis=1)),
        preferred_element_type=F32,
    )
    mixed = mix + product(square_t, mix * mix)
    act, act_slope = silu_parts(product(hidden_t, mixed))
    sent_on = product(message_t, act)
    for e in range(10):
        here = slice(e * LAYER, (e + 1) * LAYER)
        hidden[e] = act[:, here]
        if 2 <= e <= 7:
            radial_mix[e - 2] = mix[:, here]
            hidden_slope[e - 2] = act_slope[:, here]
        for number, (dx, dy) in enumerate(LATERALS):
            part = sent_on[:, here]
            if (dx, dy) != (0, 0):
                part = take(part, shifted_site((CH, LAYER), dx, dy))
            message[number, e] = part

    output_t, output_n = turned[OUTPUT], straight[OUTPUT]

    def readout(pair):
        a = 2 * pair
        e = a + 1
        total = jnp.concatenate([hidden[e], hidden[e + 1]], axis=1)
        for o, (dx, dy, dz) in enumerate(OFFSETS):
            here = slice(o * NB, (o + 1) * NB)
            radial = jnp.dot(
                second,
                radial_moving(jnp.concatenate([phi[e, here], phi[e + 1, here]], axis=1)),
                preferred_element_type=F32,
            )
            number = LATERAL_OF[(dx, dy)]
            total = total + radial * jnp.concatenate([message[number, e + dz], message[number, e + 1 + dz]], axis=1)
        return total

    total = jnp.concatenate([readout(pair) for pair in range(4)], axis=1)
    weight = jnp.concatenate([w_energy[...]] * 8, axis=1)
    act, act_slope = silu_parts(product(output_t, total))
    grad = product(output_n, weight * act_slope)
    for a in range(8):
        grad_out[a] = grad[:, a * LAYER : (a + 1) * LAYER]
    own = slice(2 * LAYER, 6 * LAYER)
    energy = jnp.sum(weight[:, own] * act[:, own], axis=0, keepdims=True)

    along[0:3] = jnp.where(even, middle[26:29, :], middle[29:32, :])
    along[3:4] = jnp.where(iota((1, 4 * LAYER), 1) == 0, jnp.sum(energy), 0.0)
    along[4:8] = jnp.zeros((4, 4 * LAYER), F32)


def backward_kernel(
    reach,
    inverse_radius,
    slope,
    radial_mix,
    hidden_slope,
    message,
    phi,
    grad_out,
    straight,
    radial,
    radial_turned,
    forces,
    grad_summed,
    pair_grad,
    pair_grad_turned,
):
    row = iota((32, LAYER), 0)
    site = site_of_row()
    square_n, hidden_n, message_n = straight[SQUARE], straight[HIDDEN], straight[MESSAGE]
    first_n, second_n = radial[0], radial[1]
    second = radial_turned[1]

    def back(pair):
        f = 2 * pair
        parts = [None, None]
        for dx, dy in LATERALS:
            total = None
            for dz in (-1, 0, 1):
                if (dx, dy, dz) == (0, 0, 0):
                    continue
                a = f + 1 - dz
                o = ROW_OF[(dx, dy, dz)]
                here = slice(o * NB, (o + 1) * NB)
                edge_radial = jnp.dot(
                    second,
                    radial_moving(jnp.concatenate([phi[a + 1, here], phi[a + 2, here]], axis=1)),
                    preferred_element_type=F32,
                )
                term = edge_radial * jnp.concatenate([grad_out[a], grad_out[a + 1]], axis=1)
                total = term if total is None else total + term
            for k in range(2):
                part = total[:, k * LAYER : (k + 1) * LAYER]
                if (dx, dy) != (0, 0):
                    part = take(part, shifted_site((CH, LAYER), -dx, -dy))
                parts[k] = part if parts[k] is None else parts[k] + part
        return jnp.concatenate(parts, axis=1)

    grad_message = jnp.concatenate([back(pair) for pair in range(3)], axis=1)
    grad_hidden = jnp.concatenate([grad_out[a] for a in range(1, 7)], axis=1) + product(message_n, grad_message)
    grad_pre = grad_hidden * jnp.concatenate([hidden_slope[f] for f in range(6)], axis=1)
    grad_mixed = product(hidden_n, grad_pre)
    mix = jnp.concatenate([radial_mix[f] for f in range(6)], axis=1)
    grad = product(first_n, grad_mixed + 2.0 * mix * product(square_n, grad_mixed))
    for f in range(6):
        grad_summed[f] = grad[:, f * LAYER : (f + 1) * LAYER]

    for f in range(6):
        pair_grad_turned[f] = jnp.zeros((32, LAYER), F32)
    for f in range(4):
        pair_grad[f] = jnp.zeros((32, LAYER), F32)

    def edges(f0, f1, offset0, offset1):
        number = LATERAL_OF[offset0[:2]]
        moved = jnp.concatenate(
            [
                grad_out[f0 + 1] * message[number, f0 + 2 + offset0[2]],
                grad_out[f1 + 1] * message[number, f1 + 2 + offset1[2]],
            ],
            axis=1,
        )
        grad = product(second_n, moved)
        out = []
        for k, (f, offset) in enumerate(((f0, offset0), (f1, offset1))):
            o = ROW_OF[offset]
            value = (grad[:, k * LAYER : (k + 1) * LAYER] + grad_summed[f]) * slope[f, o * NB : (o + 1) * NB]
            out.append(jnp.sum(value, axis=0, keepdims=True))
        return out

    def own_edges(pair):
        f = 2 * pair + 1
        for o, offset in enumerate(OFFSETS):
            left, right = edges(f, f + 1, offset, offset)
            pair_grad[f - 1, o : o + 1] = left
            pair_grad[f, o : o + 1] = right
            pair_grad_turned[f, 25 - o : 26 - o] = left
            pair_grad_turned[f + 1, 25 - o : 26 - o] = right

    for pair in range(2):
        own_edges(pair)
    for dx, dy in LATERALS:
        up, down = (dx, dy, 1), (dx, dy, -1)
        left, right = edges(0, 5, up, down)
        pair_grad_turned[0, 25 - ROW_OF[up] : 26 - ROW_OF[up]] = left
        pair_grad_turned[5, 25 - ROW_OF[down] : 26 - ROW_OF[down]] = right

    force_parts = []
    for f in range(1, 5):
        source = jnp.where(
            row < 9, pair_grad_turned[f - 1], jnp.where(row < 17, pair_grad_turned[f], pair_grad_turned[f + 1])
        )
        pull = (pair_grad[f - 1] + take(source, site)) * inverse_radius[f - 1]
        force_parts.append(
            jnp.concatenate([jnp.sum(pull * reach[f - 1, c], axis=0, keepdims=True) for c in range(3)], axis=0)
        )
    force = jnp.concatenate(force_parts, axis=1)

    forces[0:3] = force
    forces[3:8] = jnp.zeros((5, 4 * LAYER), F32)


def sums_kernel(parity, middle, forces, along, path, table, kept, sent):
    even = parity[0] == 0
    low, high = middle[26:29, :], middle[29:32, :]
    force, beside = forces[0:3], path[0:3]
    up = jnp.where(even, high - low, beside - high)
    down = jnp.where(even, low - beside, high - low)
    lane = iota((1, LAYER), 1)
    values = jnp.where(
        lane == 0, along[3:4, 0:1], jnp.where(lane == 6, jnp.broadcast_to(path[3:4, 0:1], (1, LAYER)), 0.0)
    )
    for k, term in enumerate((force * up, force * down, up * up, down * down, up * down)):
        total = jnp.sum(jnp.sum(term, axis=1, keepdims=True), axis=0, keepdims=True)
        values = values + jnp.where(lane == k + 1, total, 0.0)
    table[...] = jnp.broadcast_to(values, table.shape)
    both = jnp.concatenate([force, beside, jnp.zeros((2, 4 * LAYER), F32)], axis=0)
    left, right = both[:, : 2 * LAYER], both[:, 2 * LAYER :]
    kept[...] = jnp.where(even, left, right)
    sent[...] = jnp.where(even, right, left)


def combine_kernel(images, image_group, parity, climbing, table, own, kept, received, site_of_slot, out, energies):
    even = parity[0] == 0
    total = table[0:8]
    for k in range(8, table.shape[0], 8):
        total = total + table[k : k + 8]
    total = total[0:4] + total[4:8]
    total = total[0:2] + total[2:4]
    energy = (total[0:1, 6:7], total[0:1, 0:1], total[1:2, 0:1], total[1:2, 6:7])
    low, high = own[26:29, :], own[29:32, :]
    f_kept, f_received = kept[0:3, :], received[0:3, :]
    p_kept, p_received = kept[3:6, :], received[3:6, :]
    sides = (
        (jnp.where(even, f_kept, f_received), high - low, low - jnp.where(even, p_kept, p_received)),
        (jnp.where(even, f_received, f_kept), jnp.where(even, p_received, p_kept) - high, high - low),
    )
    slot = site_of_slot[...]
    for k, (force, up, down) in enumerate(sides):
        image = 2 * image_group[0] + k
        here = total[k : k + 1]
        v_prev, v_here, v_next = energy[k : k + 3]
        big = jnp.maximum(jnp.abs(v_next - v_here), jnp.abs(v_prev - v_here))
        small = jnp.minimum(jnp.abs(v_next - v_here), jnp.abs(v_prev - v_here))
        rising = jnp.logical_and(v_next > v_here, v_here > v_prev)
        falling = jnp.logical_and(v_next < v_here, v_here < v_prev)
        higher = v_next > v_prev
        a = jnp.where(rising, 1.0, jnp.where(falling, 0.0, jnp.where(higher, big, small)))
        b = jnp.where(rising, 0.0, jnp.where(falling, 1.0, jnp.where(higher, small, big)))
        fu, fd, uu, dd, ud = (here[:, i : i + 1] for i in range(1, 6))
        tangent_sq = a * a * uu + 2.0 * a * b * ud + b * b * dd
        norm = jnp.sqrt(tangent_sq)
        along = (a * fu + b * fd) / norm
        pull = STIFFNESS * (jnp.sqrt(uu) - jnp.sqrt(dd))
        amount = jnp.where(image == climbing[0], 2.0 * along, along - pull) / norm
        tangent = a * up + b * down
        result = force - amount * tangent
        end = jnp.logical_or(image == 0, image == images - 1)
        result = jnp.where(end, 0.0, result)
        result = jnp.concatenate([result, jnp.zeros((5, 2 * LAYER), F32)], axis=0)
        for part in range(NZL):
            index = slot[:, part * LAYER : (part + 1) * LAYER]
            low_index = index & (LAYER - 1)
            back = jnp.where(index < LAYER, take(result[:, :LAYER], low_index), take(result[:, LAYER:], low_index))
            for c in range(3):
                out[c, k : k + 1, part * LAYER : (part + 1) * LAYER] = back[c : c + 1]
        energies[k] = here[0, 0]


def vmem():
    return pl.BlockSpec(memory_space=pltpu.VMEM)


def smem():
    return pl.BlockSpec(memory_space=pltpu.SMEM)


def local(
    positions,
    neighbours,
    ghost_slots,
    climbing,
    w_radial1,
    w_square,
    w_hidden,
    w_message,
    w_radial2,
    w_output,
    w_energy,
):
    slabs = lax.axis_size("slab")
    groups = lax.axis_size("image")
    group = lax.axis_index("image")
    slab = lax.axis_index("slab")
    parity = slab % 2
    even = parity == 0
    parity_arg = parity.astype(I32).reshape(1)

    small = pltpu.CompilerParams(vmem_limit_bytes=4 * 1024 * 1024)
    packed = jnp.concatenate([neighbours.reshape(64, LAYER), ghost_slots], axis=0)
    prepared, site_of_slot = pl.pallas_call(
        prepare_kernel,
        out_shape=(
            jax.ShapeDtypeStruct((ROWS, 2 * LAYER), F32),
            jax.ShapeDtypeStruct((8, 2 * LAYER), I32),
        ),
        in_specs=[vmem()] * 2,
        out_specs=(vmem(), vmem()),
        compiler_params=small,
    )(packed, positions.transpose(1, 0, 2))

    mate = lax.ppermute(prepared, "slab", [(i, i ^ 1) for i in range(slabs)])
    middle = jnp.concatenate([jnp.where(even, prepared, mate), jnp.where(even, mate, prepared)], axis=1)
    far = lax.ppermute(
        middle, "slab", [(i, (i + 2) % slabs) if i % 2 == 0 else (i, (i - 2) % slabs) for i in range(slabs)]
    )
    def whole(*extents):
        return jax.ShapeDtypeStruct(extents, F32)

    turned, straight, radial, radial_turned, energy_column = pl.pallas_call(
        weights_kernel,
        out_shape=(
            jax.ShapeDtypeStruct((4, 2 * CH, 2 * CH), BF16),
            jax.ShapeDtypeStruct((4, 2 * CH, 2 * CH), BF16),
            jax.ShapeDtypeStruct((2, 2 * NB, 2 * CH), BF16),
            jax.ShapeDtypeStruct((2, CH, 4 * NB), BF16),
            whole(CH, CH),
        ),
        in_specs=[vmem()] * 2,
        out_specs=tuple(vmem() for _ in range(5)),
        compiler_params=small,
        cost_estimate=pl.CostEstimate(flops=10**8, bytes_accessed=1 << 22, transcendentals=0),
    )(
        stacked([w_square, w_hidden, w_message, w_output]),
        stacked([w_radial1, w_radial2, jnp.broadcast_to(w_energy[None], (NB, CH))]),
    )

    far, turned, straight = lax.optimization_barrier((far, turned, straight))
    traded = lax.ppermute(far, "slab", [(i, i ^ 1) for i in range(slabs)])

    along, *saved = pl.pallas_call(
        lambda *refs: forward_kernel(slabs * NZL * LATTICE, *refs),
        out_shape=(
            whole(8, 4 * LAYER),
            whole(4, 3, 32, LAYER),
            whole(4, 32, LAYER),
            whole(6, 32 * NB, LAYER),
            whole(6, CH, LAYER),
            whole(6, CH, LAYER),
            whole(9, 10, CH, LAYER),
            whole(10, 32 * NB, LAYER),
            whole(8, CH, LAYER),
        ),
        in_specs=[smem()] + [vmem()] * 7,
        out_specs=tuple(vmem() for _ in range(9)),
        scratch_shapes=[
            pltpu.VMEM((12, 8, LAYER), F32),
            pltpu.VMEM((10, NB, LAYER), F32),
            pltpu.VMEM((10, CH, LAYER), F32),
        ],
        compiler_params=pltpu.CompilerParams(vmem_limit_bytes=20 * 1024 * 1024),
    )(
        parity_arg,
        far,
        middle,
        traded,
        turned,
        straight,
        radial_turned,
        energy_column,
    )

    hops = []
    for g in range(groups):
        for s in range(slabs):
            if s % 2 and g + 1 < groups:
                hops.append((g * slabs + s, (g + 1) * slabs + s - 1))
            if s % 2 == 0 and g > 0:
                hops.append((g * slabs + s, (g - 1) * slabs + s + 1))
    path = lax.ppermute(along, ("image", "slab"), hops)

    forces = pl.pallas_call(
        backward_kernel,
        out_shape=whole(8, 4 * LAYER),
        in_specs=[vmem()] * 11,
        out_specs=vmem(),
        scratch_shapes=[
            pltpu.VMEM((6, NB, LAYER), F32),
            pltpu.VMEM((4, 32, LAYER), F32),
            pltpu.VMEM((6, 32, LAYER), F32),
        ],
        compiler_params=pltpu.CompilerParams(vmem_limit_bytes=20 * 1024 * 1024),
        cost_estimate=pl.CostEstimate(flops=4 * 10**9, bytes_accessed=1 << 22, transcendentals=0),
    )(*saved, straight, radial, radial_turned)

    table, kept, sent = pl.pallas_call(
        sums_kernel,
        out_shape=(whole(slabs, LAYER), whole(8, 2 * LAYER), whole(8, 2 * LAYER)),
        in_specs=[smem()] + [vmem()] * 4,
        out_specs=(vmem(), vmem(), vmem()),
        compiler_params=small,
    )(parity_arg, middle, forces, along, path)

    received = lax.ppermute(sent, "slab", [(i, i ^ 1) for i in range(slabs)])
    table = lax.all_to_all(table.reshape(slabs, 1, LAYER), "slab", 0, 0, tiled=False).reshape(slabs, LAYER)

    result, energies = pl.pallas_call(
        lambda *refs: combine_kernel(2 * groups, *refs),
        out_shape=(
            jax.ShapeDtypeStruct((3, 2, 2 * LAYER), F32),
            jax.ShapeDtypeStruct((2,), F32),
        ),
        in_specs=[smem()] * 3 + [vmem()] * 5,
        out_specs=(vmem(), smem()),
        compiler_params=small,
    )(
        group.astype(I32).reshape(1),
        parity_arg,
        climbing,
        table,
        prepared,
        kept,
        received,
        site_of_slot,
    )
    return result.transpose(1, 0, 2), energies


def solution(mesh):
    return jax.shard_map(
        local,
        mesh=mesh,
        in_specs=(
            P("image", None, "slab"),
            P("slab"),
            P(None, "slab"),
            P(),
            P(),
            P(),
            P(),
            P(),
            P(),
            P(),
            P(),
        ),
        out_specs=(P("image", None, "slab"), P("image")),
        check_vma=False,
    )
```

```python
import math

import jax
import jax.numpy as jnp
from jax import lax
from jax.experimental import pallas as pl
from jax.experimental.pallas import tpu as pltpu
from jax.sharding import PartitionSpec as P

NB = 8
NX = 16
NY = 8
NZL = 2
LAYER = 128
CH = 128
NOFF = 26
ROWS = 32

LATTICE = 2.55
CUTOFF = 5.0
STIFFNESS = 5.0
F32 = jnp.float32
BF16 = jnp.bfloat16
I32 = jnp.int32

OFFSETS = [
    (dx, dy, dz)
    for dz in (-1, 0, 1)
    for dy in (-1, 0, 1)
    for dx in (-1, 0, 1)
    if (dx, dy, dz) != (0, 0, 0)
]
ROW_OF = {offset: row for row, offset in enumerate(OFFSETS)}
LATERALS = [(dx, dy) for dy in (-1, 0, 1) for dx in (-1, 0, 1)]
LATERAL_OF = {lateral: number for number, lateral in enumerate(LATERALS)}


def take(values, index):
    return jnp.take_along_axis(values, index, axis=1, mode="promise_in_bounds")


def iota(shape, dim):
    return lax.broadcasted_iota(I32, shape, dim)


def shifted_site(shape, dx, dy):
    lane = iota(shape, len(shape) - 1)
    return ((((lane >> 4) + dy) & (NY - 1)) << 4) | ((lane + dx) & (NX - 1))


def site_of_row():
    row = iota((32, LAYER), 0)
    code = row + (row >= 13).astype(I32)
    level = (code >= 9).astype(I32) + (code >= 18).astype(I32)
    rest = code - 9 * level
    line = (rest >= 3).astype(I32) + (rest >= 6).astype(I32)
    column = rest - 3 * line
    return shifted_site((32, LAYER), column - 1, line - 1) & (LAYER - 1)


def silu_parts(values):
    sigma = 1.0 / (1.0 + jnp.exp(-values))
    return values * sigma, sigma * (1.0 + values * (1.0 - sigma))


def halves(values):
    high = values.astype(BF16)
    low = (values - high.astype(F32)).astype(BF16)
    return high, low


def stationary(matrix):
    high, low = halves(matrix)
    return jnp.concatenate(
        [jnp.concatenate([high, high], axis=1), jnp.concatenate([low, low], axis=1)], axis=0
    )


def product(packed, values):
    high, low = halves(values)
    out = jnp.dot(packed, jnp.concatenate([high, low], axis=0), preferred_element_type=F32)
    rows = packed.shape[0] // 2
    return out[:rows] + out[rows:]


def radial_stationary(matrix):
    high, low = halves(matrix.T)
    return jnp.concatenate([high, high, low, low], axis=1)


def radial_moving(values):
    high = values.astype(BF16).astype(F32)
    both = jnp.concatenate([high, values - high], axis=0).astype(BF16)
    return jnp.concatenate([both, both], axis=0)


def prepare_kernel(
    neighbours_hbm, ghost_hbm, positions_hbm, out, site_of_slot, neighbours, ghost_slots, positions, arrived
):
    copies = [
        pltpu.make_async_copy(source, target, arrived.at[number])
        for number, (source, target) in enumerate(
            ((ghost_hbm, ghost_slots), (neighbours_hbm, neighbours), (positions_hbm, positions))
        )
    ]
    for copy in copies:
        copy.start()
    for copy in copies:
        copy.wait()
    slots = ghost_slots[...]
    inverse = jnp.zeros((8, 2 * LAYER), F32)
    for layer in range(NZL):
        hit = (jnp.broadcast_to(slots[layer : layer + 1], (2 * LAYER, LAYER)) == iota((2 * LAYER, LAYER), 0))
        sites = (iota((8, LAYER), 1) + layer * LAYER).astype(F32).astype(BF16)
        inverse = inverse + lax.dot_general(
            sites,
            jnp.where(hit, 1.0, 0.0).astype(BF16),
            (((1,), (1,)), ((), ())),
            preferred_element_type=F32,
        )
    inverse = inverse.astype(I32)
    site_of_slot[...] = inverse
    first = jnp.broadcast_to(inverse[0:1, :LAYER], (32, LAYER))
    second = jnp.broadcast_to(inverse[0:1, LAYER:], (32, LAYER))
    sides = [
        jnp.concatenate(
            [positions[c, k : k + 1, half * LAYER : (half + 1) * LAYER] for k in range(2) for c in range(3)]
            + [jnp.zeros((2, LAYER), F32)],
            axis=0,
        )
        for half in range(2)
    ]
    listed = neighbours[...].astype(F32)
    turned = jnp.concatenate([listed, jnp.zeros((64, LAYER), F32)], axis=0).T
    site = iota((32, LAYER), 1)
    row = iota((32, LAYER), 0)
    for layer in range(NZL):
        here = slice(layer * LAYER, (layer + 1) * LAYER)
        slot = jnp.broadcast_to(slots[layer : layer + 1], (8, LAYER))
        low = slot & (LAYER - 1)
        coords = jnp.where(slot < LAYER, take(sides[0], low), take(sides[1], low))
        slot = jnp.broadcast_to(slots[layer : layer + 1], (32, LAYER))
        picked = take(turned[0:32], slot >> 2)
        for part in range(1, 4):
            picked = jnp.where((slot & 3) == part, take(turned[32 * part : 32 * part + 32], slot >> 2), picked)
        entry = picked.astype(I32)
        low = entry & (LAYER - 1)
        own = jnp.where(entry < LAYER, take(first, low), take(second, low))
        inside = entry < 2 * LAYER
        level = jnp.where(inside, own >> 7, jnp.where(entry < 3 * LAYER, -1, NZL))
        target = jnp.where(inside, own & (LAYER - 1), low)
        column = ((target & (NX - 1)) - (site & (NX - 1)) + 1) & (NX - 1)
        line = ((target >> 4) - (site >> 4) + 1) & (NY - 1)
        code = (level - layer + 1) * 9 + line * 3 + column
        code = jnp.where(code > 13, code - 1, code) & 31
        bits = jnp.where(entry >= 0, jnp.left_shift(jnp.ones_like(code), code), 0)
        bits = bits[0:16] | bits[16:32]
        bits = bits[0:8] | bits[8:16]
        bits = bits[0:4] | bits[4:8]
        bits = bits[0:2] | bits[2:4]
        bits = bits[0:1] | bits[1:2]
        mask = (jnp.broadcast_to(bits, (32, LAYER)) >> row) & 1
        out[0:NOFF, here] = mask[0:NOFF].astype(F32)
        out[NOFF:32, here] = coords[0:6]


SIN_TERMS = [(-1.0) ** k / math.factorial(2 * k + 1) for k in range(7)]
COS_TERMS = [(-1.0) ** k / math.factorial(2 * k) for k in range(8)]


def horner(terms, square):
    total = jnp.full_like(square, terms[-1])
    for term in terms[-2::-1]:
        total = total * square + term
    return total


SQUARE, HIDDEN, MESSAGE, OUTPUT = range(4)


def weights_kernel(
    w_square,
    w_hidden,
    w_message,
    w_output,
    w_radial1,
    w_radial2,
    w_energy,
    turned,
    straight,
    radial,
    radial_turned,
    energy,
    squares,
    radials,
    column,
    arrived,
):
    moves = [(ref, squares.at[number]) for number, ref in enumerate((w_square, w_hidden, w_message, w_output))]
    moves += [(w_radial1, radials.at[0]), (w_radial2, radials.at[1]), (w_energy, column)]
    copies = [pltpu.make_async_copy(*move, arrived.at[number]) for number, move in enumerate(moves)]
    for copy in copies:
        copy.start()
    for copy in copies:
        copy.wait()
    for number in range(4):
        turned[number] = stationary(squares[number].T)
        straight[number] = stationary(squares[number])
    for number in range(2):
        radial[number] = stationary(radials[number])
        radial_turned[number] = radial_stationary(radials[number])
    energy[...] = jnp.broadcast_to(column[...], (CH, CH)).T


def forward_kernel(
    cell_z,
    parity,
    far,
    middle,
    traded,
    turned,
    straight,
    radial_turned,
    w_energy,
    along,
    reach,
    inverse_radius,
    slope,
    radial_mix,
    hidden_slope,
    message,
    phi,
    grad_out,
    coords,
    summed,
    hidden,
):
    even = parity[0] == 0

    def level_rows(level, first, last):
        here = slice(level % 4 * LAYER, (level % 4 + 1) * LAYER)
        if 4 <= level < 8:
            return middle[first:last, here]
        mine, other = far[first:last, here], traded[first:last, here]
        return jnp.where(even, mine, other) if level < 4 else jnp.where(even, other, mine)

    for level in range(12):
        both = level_rows(level, 24, 32)
        coords[level, 0:3] = jnp.where(even, both[2:5], both[5:8])
    row = iota((32, LAYER), 0)
    site = site_of_row()
    boxes = (NX * LATTICE, NY * LATTICE, cell_z)

    for e in range(10):
        mask = jnp.where(row < NOFF, level_rows(e + 1, 0, 32), 0.0)
        squared = None
        for c in range(3):
            centre = coords[e + 1, c : c + 1]
            source = jnp.where(
                row < 9,
                jnp.broadcast_to(coords[e, c : c + 1], (32, LAYER)),
                jnp.where(
                    row < 17,
                    jnp.broadcast_to(centre, (32, LAYER)),
                    jnp.broadcast_to(coords[e + 2, c : c + 1], (32, LAYER)),
                ),
            )
            d = take(source, site) - jnp.broadcast_to(centre, (32, LAYER))
            box = jnp.float32(boxes[c])
            half = jnp.float32(0.5) * box
            d = jnp.where(d > half, d - box, jnp.where(d < -half, d + box, d))
            if 3 <= e <= 6:
                reach[e - 3, c] = d
            squared = d * d if squared is None else squared + d * d
        squared = jnp.where(squared > 0.0, squared, 1.0)
        radius = jnp.sqrt(squared)
        inverse = 1.0 / radius
        if 3 <= e <= 6:
            inverse_radius[e - 3] = inverse
        inside = radius < CUTOFF
        angle = jnp.minimum(radius * (math.pi / (2.0 * CUTOFF)), 0.5 * math.pi)
        square = angle * angle
        sine = angle * horner(SIN_TERMS, square)
        cosine = horner(COS_TERMS, square)
        sine1 = 2.0 * sine * cosine
        cosine1 = 1.0 - 2.0 * sine * sine
        smooth = jnp.where(inside, cosine * cosine, 0.0)
        cut_slope = jnp.where(inside, (-math.pi / CUTOFF) * sine * cosine, 0.0)
        scale = mask * smooth * inverse
        tilt = mask * (cut_slope - smooth * inverse) * inverse
        twice = 2.0 * cosine1
        s_prev, s_here = jnp.zeros_like(sine1), sine1
        c_prev, c_here = jnp.ones_like(sine1), cosine1
        for b in range(NB):
            phi[e, pl.ds(b, 32, stride=NB), :] = scale * s_here
            if 2 <= e <= 7:
                slope[e - 2, pl.ds(b, 32, stride=NB), :] = tilt * s_here + scale * (
                    ((b + 1) * math.pi / CUTOFF) * c_here
                )
            s_prev, s_here = s_here, twice * s_here - s_prev
            c_prev, c_here = c_here, twice * c_here - c_prev
        total = phi[e, 0:NB]
        for o in range(1, NOFF):
            total = total + phi[e, o * NB : (o + 1) * NB]
        summed[e] = total

    first, second = radial_turned[0], radial_turned[1]
    square_t, hidden_t, message_t = turned[SQUARE], turned[HIDDEN], turned[MESSAGE]

    held = {}

    def node_mix(pair):
        mix = jnp.dot(
            first,
            radial_moving(jnp.concatenate([summed[2 * pair], summed[2 * pair + 1]], axis=1)),
            preferred_element_type=F32,
        )
        for k in range(2):
            if 2 <= 2 * pair <= 6:
                radial_mix[2 * pair + k - 2] = mix[:, k * LAYER : (k + 1) * LAYER]
        held[pair] = mix, product(square_t, mix * mix)

    def node_hidden(pair):
        mix, mixed = held[pair]
        held[pair] = product(hidden_t, mix + mixed)

    def node_message(pair):
        act, act_slope = silu_parts(held[pair])
        for k in range(2):
            hidden[2 * pair + k] = act[:, k * LAYER : (k + 1) * LAYER]
            if 2 <= 2 * pair <= 6:
                hidden_slope[2 * pair + k - 2] = act_slope[:, k * LAYER : (k + 1) * LAYER]
        held[pair] = product(message_t, act)

    def node_send(pair):
        for k in range(2):
            for number, (dx, dy) in enumerate(LATERALS):
                part = held[pair][:, k * LAYER : (k + 1) * LAYER]
                if (dx, dy) != (0, 0):
                    part = take(part, shifted_site((CH, LAYER), dx, dy))
                message[number, 2 * pair + k] = part

    stages = (node_mix, node_hidden, node_message, node_send)
    for step in range(5 + len(stages) - 1):
        for number, stage in enumerate(stages):
            if 0 <= step - number < 5:
                stage(step - number)

    output_t, output_n = turned[OUTPUT], straight[OUTPUT]

    def readout(pair):
        a = 2 * pair
        e = a + 1
        total = jnp.concatenate([hidden[e], hidden[e + 1]], axis=1)
        for o, (dx, dy, dz) in enumerate(OFFSETS):
            here = slice(o * NB, (o + 1) * NB)
            radial = jnp.dot(
                second,
                radial_moving(jnp.concatenate([phi[e, here], phi[e + 1, here]], axis=1)),
                preferred_element_type=F32,
            )
            number = LATERAL_OF[(dx, dy)]
            total = total + radial * jnp.concatenate([message[number, e + dz], message[number, e + 1 + dz]], axis=1)
        held[pair] = total

    weight = jnp.concatenate([w_energy[...]] * 2, axis=1)
    energies = []

    def readout_energy(pair):
        act, act_slope = silu_parts(product(output_t, held[pair]))
        if 1 <= pair <= 2:
            energies.append(jnp.sum(weight * act, axis=0, keepdims=True))
        held[pair] = weight * act_slope

    def readout_grad(pair):
        grad = product(output_n, held[pair])
        grad_out[2 * pair] = grad[:, :LAYER]
        grad_out[2 * pair + 1] = grad[:, LAYER:]

    stages = (readout, readout_energy, readout_grad)
    for step in range(4 + len(stages) - 1):
        for number, stage in enumerate(stages):
            if 0 <= step - number < 4:
                stage(step - number)
    energy = energies[0] + energies[1]

    along[0:3] = jnp.where(even, middle[26:29, :], middle[29:32, :])
    along[3:4] = jnp.where(iota((1, 4 * LAYER), 1) == 0, jnp.sum(energy), 0.0)
    along[4:8] = jnp.zeros((4, 4 * LAYER), F32)


def backward_kernel(
    reach,
    inverse_radius,
    slope,
    radial_mix,
    hidden_slope,
    message,
    phi,
    grad_out,
    straight,
    radial,
    radial_turned,
    forces,
    grad_summed,
    pair_grad,
    pair_grad_turned,
):
    row = iota((32, LAYER), 0)
    site = site_of_row()
    square_n, hidden_n, message_n = straight[SQUARE], straight[HIDDEN], straight[MESSAGE]
    first_n, second_n = radial[0], radial[1]
    second = radial_turned[1]

    def back(pair):
        f = 2 * pair
        parts = [None, None]
        for dx, dy in LATERALS:
            total = None
            for dz in (-1, 0, 1):
                if (dx, dy, dz) == (0, 0, 0):
                    continue
                a = f + 1 - dz
                o = ROW_OF[(dx, dy, dz)]
                here = slice(o * NB, (o + 1) * NB)
                edge_radial = jnp.dot(
                    second,
                    radial_moving(jnp.concatenate([phi[a + 1, here], phi[a + 2, here]], axis=1)),
                    preferred_element_type=F32,
                )
                term = edge_radial * jnp.concatenate([grad_out[a], grad_out[a + 1]], axis=1)
                total = term if total is None else total + term
            for k in range(2):
                part = total[:, k * LAYER : (k + 1) * LAYER]
                if (dx, dy) != (0, 0):
                    part = take(part, shifted_site((CH, LAYER), -dx, -dy))
                parts[k] = part if parts[k] is None else parts[k] + part
        return jnp.concatenate(parts, axis=1)

    grad_message = jnp.concatenate([back(pair) for pair in range(3)], axis=1)
    grad_hidden = jnp.concatenate([grad_out[a] for a in range(1, 7)], axis=1) + product(message_n, grad_message)
    grad_pre = grad_hidden * jnp.concatenate([hidden_slope[f] for f in range(6)], axis=1)
    grad_mixed = product(hidden_n, grad_pre)
    mix = jnp.concatenate([radial_mix[f] for f in range(6)], axis=1)
    grad = product(first_n, grad_mixed + 2.0 * mix * product(square_n, grad_mixed))
    for f in range(6):
        grad_summed[f] = grad[:, f * LAYER : (f + 1) * LAYER]

    for f in range(6):
        pair_grad_turned[f] = jnp.zeros((32, LAYER), F32)
    for f in range(4):
        pair_grad[f] = jnp.zeros((32, LAYER), F32)

    def edges(f0, f1, offset0, offset1):
        number = LATERAL_OF[offset0[:2]]
        moved = jnp.concatenate(
            [
                grad_out[f0 + 1] * message[number, f0 + 2 + offset0[2]],
                grad_out[f1 + 1] * message[number, f1 + 2 + offset1[2]],
            ],
            axis=1,
        )
        grad = product(second_n, moved)
        out = []
        for k, (f, offset) in enumerate(((f0, offset0), (f1, offset1))):
            o = ROW_OF[offset]
            value = (grad[:, k * LAYER : (k + 1) * LAYER] + grad_summed[f]) * slope[f, o * NB : (o + 1) * NB]
            out.append(jnp.sum(value, axis=0, keepdims=True))
        return out

    def own_edges(pair):
        f = 2 * pair + 1
        for o, offset in enumerate(OFFSETS):
            left, right = edges(f, f + 1, offset, offset)
            pair_grad[f - 1, o : o + 1] = left
            pair_grad[f, o : o + 1] = right
            pair_grad_turned[f, 25 - o : 26 - o] = left
            pair_grad_turned[f + 1, 25 - o : 26 - o] = right

    for pair in range(2):
        own_edges(pair)
    for dx, dy in LATERALS:
        up, down = (dx, dy, 1), (dx, dy, -1)
        left, right = edges(0, 5, up, down)
        pair_grad_turned[0, 25 - ROW_OF[up] : 26 - ROW_OF[up]] = left
        pair_grad_turned[5, 25 - ROW_OF[down] : 26 - ROW_OF[down]] = right

    force_parts = []
    for f in range(1, 5):
        source = jnp.where(
            row < 9, pair_grad_turned[f - 1], jnp.where(row < 17, pair_grad_turned[f], pair_grad_turned[f + 1])
        )
        pull = (pair_grad[f - 1] + take(source, site)) * inverse_radius[f - 1]
        force_parts.append(
            jnp.concatenate([jnp.sum(pull * reach[f - 1, c], axis=0, keepdims=True) for c in range(3)], axis=0)
        )
    force = jnp.concatenate(force_parts, axis=1)

    forces[0:3] = force
    forces[3:8] = jnp.zeros((5, 4 * LAYER), F32)


def sums_kernel(parity, middle, forces, along, path, table, kept, sent):
    even = parity[0] == 0
    low, high = middle[26:29, :], middle[29:32, :]
    force, beside = forces[0:3], path[0:3]
    up = jnp.where(even, high - low, beside - high)
    down = jnp.where(even, low - beside, high - low)
    lane = iota((1, LAYER), 1)
    values = jnp.where(
        lane == 0, along[3:4, 0:1], jnp.where(lane == 6, jnp.broadcast_to(path[3:4, 0:1], (1, LAYER)), 0.0)
    )
    for k, term in enumerate((force * up, force * down, up * up, down * down, up * down)):
        total = jnp.sum(jnp.sum(term, axis=1, keepdims=True), axis=0, keepdims=True)
        values = values + jnp.where(lane == k + 1, total, 0.0)
    table[...] = jnp.broadcast_to(values, table.shape)
    both = jnp.concatenate([force, beside, jnp.zeros((2, 4 * LAYER), F32)], axis=0)
    left, right = both[:, : 2 * LAYER], both[:, 2 * LAYER :]
    kept[...] = jnp.where(even, left, right)
    sent[...] = jnp.where(even, right, left)


def combine_kernel(images, image_group, parity, climbing, table, own, kept, received, site_of_slot, out, energies):
    even = parity[0] == 0
    total = table[0:8]
    for k in range(8, table.shape[0], 8):
        total = total + table[k : k + 8]
    total = total[0:4] + total[4:8]
    total = total[0:2] + total[2:4]
    energy = (total[0:1, 6:7], total[0:1, 0:1], total[1:2, 0:1], total[1:2, 6:7])
    low, high = own[26:29, :], own[29:32, :]
    f_kept, f_received = kept[0:3, :], received[0:3, :]
    p_kept, p_received = kept[3:6, :], received[3:6, :]
    sides = (
        (jnp.where(even, f_kept, f_received), high - low, low - jnp.where(even, p_kept, p_received)),
        (jnp.where(even, f_received, f_kept), jnp.where(even, p_received, p_kept) - high, high - low),
    )
    slot = site_of_slot[...]
    for k, (force, up, down) in enumerate(sides):
        image = 2 * image_group[0] + k
        here = total[k : k + 1]
        v_prev, v_here, v_next = energy[k : k + 3]
        big = jnp.maximum(jnp.abs(v_next - v_here), jnp.abs(v_prev - v_here))
        small = jnp.minimum(jnp.abs(v_next - v_here), jnp.abs(v_prev - v_here))
        rising = jnp.logical_and(v_next > v_here, v_here > v_prev)
        falling = jnp.logical_and(v_next < v_here, v_here < v_prev)
        higher = v_next > v_prev
        a = jnp.where(rising, 1.0, jnp.where(falling, 0.0, jnp.where(higher, big, small)))
        b = jnp.where(rising, 0.0, jnp.where(falling, 1.0, jnp.where(higher, small, big)))
        fu, fd, uu, dd, ud = (here[:, i : i + 1] for i in range(1, 6))
        tangent_sq = a * a * uu + 2.0 * a * b * ud + b * b * dd
        norm = jnp.sqrt(tangent_sq)
        along = (a * fu + b * fd) / norm
        pull = STIFFNESS * (jnp.sqrt(uu) - jnp.sqrt(dd))
        amount = jnp.where(image == climbing[0], 2.0 * along, along - pull) / norm
        tangent = a * up + b * down
        result = force - amount * tangent
        end = jnp.logical_or(image == 0, image == images - 1)
        result = jnp.where(end, 0.0, result)
        result = jnp.concatenate([result, jnp.zeros((5, 2 * LAYER), F32)], axis=0)
        for part in range(NZL):
            index = slot[:, part * LAYER : (part + 1) * LAYER]
            low_index = index & (LAYER - 1)
            back = jnp.where(index < LAYER, take(result[:, :LAYER], low_index), take(result[:, LAYER:], low_index))
            for c in range(3):
                out[c, k : k + 1, part * LAYER : (part + 1) * LAYER] = back[c : c + 1]
        energies[k] = here[0, 0]


def vmem():
    return pl.BlockSpec(memory_space=pltpu.VMEM)


def hbm():
    return pl.BlockSpec(memory_space=pltpu.HBM)


def stay(array):
    return pltpu.with_memory_space_constraint(array, pltpu.HBM)


def smem():
    return pl.BlockSpec(memory_space=pltpu.SMEM)


def local(
    positions,
    neighbours,
    ghost_slots,
    climbing,
    w_radial1,
    w_square,
    w_hidden,
    w_message,
    w_radial2,
    w_output,
    w_energy,
):
    slabs = lax.axis_size("slab")
    groups = lax.axis_size("image")
    group = lax.axis_index("image")
    slab = lax.axis_index("slab")
    parity = slab % 2
    even = parity == 0
    parity_arg = parity.astype(I32).reshape(1)

    small = pltpu.CompilerParams(vmem_limit_bytes=4 * 1024 * 1024)
    prepared, site_of_slot = pl.pallas_call(
        prepare_kernel,
        out_shape=(
            jax.ShapeDtypeStruct((ROWS, 2 * LAYER), F32),
            jax.ShapeDtypeStruct((8, 2 * LAYER), I32),
        ),
        in_specs=[hbm()] * 3,
        out_specs=(vmem(), vmem()),
        scratch_shapes=[
            pltpu.VMEM((64, LAYER), I32),
            pltpu.VMEM((2, LAYER), I32),
            pltpu.VMEM((3, 2, 2 * LAYER), F32),
            pltpu.SemaphoreType.DMA((3,)),
        ],
        compiler_params=small,
    )(
        stay(neighbours.reshape(64, LAYER)), stay(ghost_slots), stay(positions.transpose(1, 0, 2))
    )

    mate = lax.ppermute(prepared, "slab", [(i, i ^ 1) for i in range(slabs)])
    middle = jnp.concatenate([jnp.where(even, prepared, mate), jnp.where(even, mate, prepared)], axis=1)
    far = lax.ppermute(
        middle, "slab", [(i, (i + 2) % slabs) if i % 2 == 0 else (i, (i - 2) % slabs) for i in range(slabs)]
    )
    def whole(*extents):
        return jax.ShapeDtypeStruct(extents, F32)

    turned, straight, radial, radial_turned, energy_column = pl.pallas_call(
        weights_kernel,
        out_shape=(
            jax.ShapeDtypeStruct((4, 2 * CH, 2 * CH), BF16),
            jax.ShapeDtypeStruct((4, 2 * CH, 2 * CH), BF16),
            jax.ShapeDtypeStruct((2, 2 * NB, 2 * CH), BF16),
            jax.ShapeDtypeStruct((2, CH, 4 * NB), BF16),
            whole(CH, CH),
        ),
        in_specs=[hbm()] * 7,
        out_specs=tuple(vmem() for _ in range(5)),
        scratch_shapes=[
            pltpu.VMEM((4, CH, CH), F32),
            pltpu.VMEM((2, NB, CH), F32),
            pltpu.VMEM((1, CH), F32),
            pltpu.SemaphoreType.DMA((7,)),
        ],
        compiler_params=small,
        cost_estimate=pl.CostEstimate(flops=10**8, bytes_accessed=1 << 22, transcendentals=0),
    )(*map(stay, (w_square, w_hidden, w_message, w_output, w_radial1, w_radial2, w_energy.reshape(1, CH))))

    far, turned, straight = lax.optimization_barrier((far, turned, straight))
    traded = lax.ppermute(far, "slab", [(i, i ^ 1) for i in range(slabs)])

    along, *saved = pl.pallas_call(
        lambda *refs: forward_kernel(slabs * NZL * LATTICE, *refs),
        out_shape=(
            whole(8, 4 * LAYER),
            whole(4, 3, 32, LAYER),
            whole(4, 32, LAYER),
            whole(6, 32 * NB, LAYER),
            whole(6, CH, LAYER),
            whole(6, CH, LAYER),
            whole(9, 10, CH, LAYER),
            whole(10, 32 * NB, LAYER),
            whole(8, CH, LAYER),
        ),
        in_specs=[smem()] + [vmem()] * 7,
        out_specs=tuple(vmem() for _ in range(9)),
        scratch_shapes=[
            pltpu.VMEM((12, 8, LAYER), F32),
            pltpu.VMEM((10, NB, LAYER), F32),
            pltpu.VMEM((10, CH, LAYER), F32),
        ],
        compiler_params=pltpu.CompilerParams(vmem_limit_bytes=20 * 1024 * 1024),
    )(
        parity_arg,
        far,
        middle,
        traded,
        turned,
        straight,
        radial_turned,
        energy_column,
    )

    hops = []
    for g in range(groups):
        for s in range(slabs):
            if s % 2 and g + 1 < groups:
                hops.append((g * slabs + s, (g + 1) * slabs + s - 1))
            if s % 2 == 0 and g > 0:
                hops.append((g * slabs + s, (g - 1) * slabs + s + 1))
    path = lax.ppermute(along, ("image", "slab"), hops)

    forces = pl.pallas_call(
        backward_kernel,
        out_shape=whole(8, 4 * LAYER),
        in_specs=[vmem()] * 11,
        out_specs=vmem(),
        scratch_shapes=[
            pltpu.VMEM((6, NB, LAYER), F32),
            pltpu.VMEM((4, 32, LAYER), F32),
            pltpu.VMEM((6, 32, LAYER), F32),
        ],
        compiler_params=pltpu.CompilerParams(vmem_limit_bytes=20 * 1024 * 1024),
        cost_estimate=pl.CostEstimate(flops=4 * 10**9, bytes_accessed=1 << 22, transcendentals=0),
    )(*saved, straight, radial, radial_turned)

    table, kept, sent = pl.pallas_call(
        sums_kernel,
        out_shape=(whole(slabs, LAYER), whole(8, 2 * LAYER), whole(8, 2 * LAYER)),
        in_specs=[smem()] + [vmem()] * 4,
        out_specs=(vmem(), vmem(), vmem()),
        compiler_params=small,
    )(parity_arg, middle, forces, along, path)

    received = lax.ppermute(sent, "slab", [(i, i ^ 1) for i in range(slabs)])
    table = lax.all_to_all(table.reshape(slabs, 1, LAYER), "slab", 0, 0, tiled=False).reshape(slabs, LAYER)

    result, energies = pl.pallas_call(
        lambda *refs: combine_kernel(2 * groups, *refs),
        out_shape=(
            jax.ShapeDtypeStruct((3, 2, 2 * LAYER), F32),
            jax.ShapeDtypeStruct((2,), F32),
        ),
        in_specs=[smem()] * 3 + [vmem()] * 5,
        out_specs=(vmem(), smem()),
        compiler_params=small,
    )(
        group.astype(I32).reshape(1),
        parity_arg,
        climbing,
        table,
        prepared,
        kept,
        received,
        site_of_slot,
    )
    return result.transpose(1, 0, 2), energies


def solution(mesh):
    return jax.shard_map(
        local,
        mesh=mesh,
        in_specs=(
            P("image", None, "slab"),
            P("slab"),
            P(None, "slab"),
            P(),
            P(),
            P(),
            P(),
            P(),
            P(),
            P(),
            P(),
        ),
        out_specs=(P("image", None, "slab"), P("image")),
        check_vma=False,
    )
```

```python
import math

import jax
import jax.numpy as jnp
from jax import lax
from jax.experimental import pallas as pl
from jax.experimental.pallas import tpu as pltpu
from jax.sharding import PartitionSpec as P

NB = 8
NX = 16
NY = 8
NZL = 2
LAYER = 128
CH = 128
NOFF = 26
ROWS = 32

LATTICE = 2.55
CUTOFF = 5.0
STIFFNESS = 5.0
F32 = jnp.float32
BF16 = jnp.bfloat16
I32 = jnp.int32

OFFSETS = [
    (dx, dy, dz)
    for dz in (-1, 0, 1)
    for dy in (-1, 0, 1)
    for dx in (-1, 0, 1)
    if (dx, dy, dz) != (0, 0, 0)
]
ROW_OF = {offset: row for row, offset in enumerate(OFFSETS)}
LATERALS = [(dx, dy) for dy in (-1, 0, 1) for dx in (-1, 0, 1)]
LATERAL_OF = {lateral: number for number, lateral in enumerate(LATERALS)}


def take(values, index):
    return jnp.take_along_axis(values, index, axis=1, mode="promise_in_bounds")


def iota(shape, dim):
    return lax.broadcasted_iota(I32, shape, dim)


def shifted_site(shape, dx, dy):
    lane = iota(shape, len(shape) - 1)
    return ((((lane >> 4) + dy) & (NY - 1)) << 4) | ((lane + dx) & (NX - 1))


def site_of_row():
    row = iota((32, LAYER), 0)
    code = row + (row >= 13).astype(I32)
    level = (code >= 9).astype(I32) + (code >= 18).astype(I32)
    rest = code - 9 * level
    line = (rest >= 3).astype(I32) + (rest >= 6).astype(I32)
    column = rest - 3 * line
    return shifted_site((32, LAYER), column - 1, line - 1) & (LAYER - 1)


def silu_parts(values):
    sigma = 1.0 / (1.0 + jnp.exp(-values))
    return values * sigma, sigma * (1.0 + values * (1.0 - sigma))


def halves(values):
    high = values.astype(BF16)
    low = (values - high.astype(F32)).astype(BF16)
    return high, low


def stationary(matrix):
    high, low = halves(matrix)
    return jnp.concatenate(
        [jnp.concatenate([high, high], axis=1), jnp.concatenate([low, low], axis=1)], axis=0
    )


def product(packed, values):
    high, low = halves(values)
    out = jnp.dot(packed, jnp.concatenate([high, low], axis=0), preferred_element_type=F32)
    rows = packed.shape[0] // 2
    return out[:rows] + out[rows:]


def radial_stationary(matrix):
    high, low = halves(matrix.T)
    return jnp.concatenate([high, high, low, low], axis=1)


def radial_moving(values):
    high = values.astype(BF16).astype(F32)
    both = jnp.concatenate([high, values - high], axis=0).astype(BF16)
    return jnp.concatenate([both, both], axis=0)


def prepare_kernel(
    neighbours_hbm, ghost_hbm, positions_hbm, out, site_of_slot, neighbours, ghost_slots, positions, arrived
):
    copies = [
        pltpu.make_async_copy(source, target, arrived.at[number])
        for number, (source, target) in enumerate(
            ((ghost_hbm, ghost_slots), (neighbours_hbm, neighbours), (positions_hbm, positions))
        )
    ]
    for copy in copies:
        copy.start()
    for copy in copies:
        copy.wait()
    slots = ghost_slots[...]
    inverse = jnp.zeros((8, 2 * LAYER), F32)
    for layer in range(NZL):
        hit = (jnp.broadcast_to(slots[layer : layer + 1], (2 * LAYER, LAYER)) == iota((2 * LAYER, LAYER), 0))
        sites = (iota((8, LAYER), 1) + layer * LAYER).astype(F32).astype(BF16)
        inverse = inverse + lax.dot_general(
            sites,
            jnp.where(hit, 1.0, 0.0).astype(BF16),
            (((1,), (1,)), ((), ())),
            preferred_element_type=F32,
        )
    inverse = inverse.astype(I32)
    site_of_slot[...] = inverse
    first = jnp.broadcast_to(inverse[0:1, :LAYER], (32, LAYER))
    second = jnp.broadcast_to(inverse[0:1, LAYER:], (32, LAYER))
    sides = [
        jnp.concatenate(
            [positions[c, k : k + 1, half * LAYER : (half + 1) * LAYER] for k in range(2) for c in range(3)]
            + [jnp.zeros((2, LAYER), F32)],
            axis=0,
        )
        for half in range(2)
    ]
    listed = neighbours[...].astype(F32)
    turned = jnp.concatenate([listed, jnp.zeros((64, LAYER), F32)], axis=0).T
    site = iota((32, LAYER), 1)
    row = iota((32, LAYER), 0)
    for layer in range(NZL):
        here = slice(layer * LAYER, (layer + 1) * LAYER)
        slot = jnp.broadcast_to(slots[layer : layer + 1], (8, LAYER))
        low = slot & (LAYER - 1)
        coords = jnp.where(slot < LAYER, take(sides[0], low), take(sides[1], low))
        slot = jnp.broadcast_to(slots[layer : layer + 1], (32, LAYER))
        picked = take(turned[0:32], slot >> 2)
        for part in range(1, 4):
            picked = jnp.where((slot & 3) == part, take(turned[32 * part : 32 * part + 32], slot >> 2), picked)
        entry = picked.astype(I32)
        low = entry & (LAYER - 1)
        own = jnp.where(entry < LAYER, take(first, low), take(second, low))
        inside = entry < 2 * LAYER
        level = jnp.where(inside, own >> 7, jnp.where(entry < 3 * LAYER, -1, NZL))
        target = jnp.where(inside, own & (LAYER - 1), low)
        column = ((target & (NX - 1)) - (site & (NX - 1)) + 1) & (NX - 1)
        line = ((target >> 4) - (site >> 4) + 1) & (NY - 1)
        code = (level - layer + 1) * 9 + line * 3 + column
        code = jnp.where(code > 13, code - 1, code) & 31
        bits = jnp.where(entry >= 0, jnp.left_shift(jnp.ones_like(code), code), 0)
        bits = bits[0:16] | bits[16:32]
        bits = bits[0:8] | bits[8:16]
        bits = bits[0:4] | bits[4:8]
        bits = bits[0:2] | bits[2:4]
        bits = bits[0:1] | bits[1:2]
        mask = (jnp.broadcast_to(bits, (32, LAYER)) >> row) & 1
        out[0:NOFF, here] = mask[0:NOFF].astype(F32)
        out[NOFF:32, here] = coords[0:6]


SIN_TERMS = [(-1.0) ** k / math.factorial(2 * k + 1) for k in range(7)]
COS_TERMS = [(-1.0) ** k / math.factorial(2 * k) for k in range(8)]


def horner(terms, square):
    total = jnp.full_like(square, terms[-1])
    for term in terms[-2::-1]:
        total = total * square + term
    return total


SQUARE, HIDDEN, MESSAGE, OUTPUT = range(4)


def weights_kernel(
    w_square,
    w_hidden,
    w_message,
    w_output,
    w_radial1,
    w_radial2,
    w_energy,
    turned,
    straight,
    radial,
    radial_turned,
    energy,
    squares,
    radials,
    column,
    arrived,
):
    moves = [(ref, squares.at[number]) for number, ref in enumerate((w_square, w_hidden, w_message, w_output))]
    moves += [(w_radial1, radials.at[0]), (w_radial2, radials.at[1]), (w_energy, column)]
    copies = [pltpu.make_async_copy(*move, arrived.at[number]) for number, move in enumerate(moves)]
    for copy in copies:
        copy.start()
    for copy in copies:
        copy.wait()
    for number in range(4):
        turned[number] = stationary(squares[number].T)
        straight[number] = stationary(squares[number])
    for number in range(2):
        radial[number] = stationary(radials[number])
        radial_turned[number] = radial_stationary(radials[number])
    energy[...] = jnp.broadcast_to(column[...], (CH, CH)).T


def forward_kernel(
    cell_z,
    side,
    far,
    middle,
    traded,
    turned,
    straight,
    radial_turned,
    w_energy,
    along,
    reach,
    inverse_radius,
    slope,
    radial_mix,
    hidden_slope,
    message,
    phi,
    grad_out,
    coords,
    summed,
    hidden,
    outer,
):
    even = (side[0] & 1) == 0
    place = side[0] >> 1
    outer[place] = far[...]
    outer[1 - place] = traded[...]

    def level_rows(level, first, last):
        here = slice(level % 4 * LAYER, (level % 4 + 1) * LAYER)
        if 4 <= level < 8:
            return middle[first:last, here]
        return outer[0 if level < 4 else 1, first:last, here]

    for level in range(12):
        both = level_rows(level, 24, 32)
        coords[level, 0:3] = jnp.where(even, both[2:5], both[5:8])
    row = iota((32, LAYER), 0)
    site = site_of_row()
    boxes = (NX * LATTICE, NY * LATTICE, cell_z)

    for e in range(10):
        mask = jnp.where(row < NOFF, level_rows(e + 1, 0, 32), 0.0)
        squared = None
        for c in range(3):
            centre = coords[e + 1, c : c + 1]
            source = jnp.where(
                row < 9,
                jnp.broadcast_to(coords[e, c : c + 1], (32, LAYER)),
                jnp.where(
                    row < 17,
                    jnp.broadcast_to(centre, (32, LAYER)),
                    jnp.broadcast_to(coords[e + 2, c : c + 1], (32, LAYER)),
                ),
            )
            d = take(source, site) - jnp.broadcast_to(centre, (32, LAYER))
            box = jnp.float32(boxes[c])
            half = jnp.float32(0.5) * box
            d = jnp.where(d > half, d - box, jnp.where(d < -half, d + box, d))
            if 3 <= e <= 6:
                reach[e - 3, c] = d
            squared = d * d if squared is None else squared + d * d
        squared = jnp.where(squared > 0.0, squared, 1.0)
        radius = jnp.sqrt(squared)
        inverse = 1.0 / radius
        if 3 <= e <= 6:
            inverse_radius[e - 3] = inverse
        inside = radius < CUTOFF
        angle = jnp.minimum(radius * (math.pi / (2.0 * CUTOFF)), 0.5 * math.pi)
        square = angle * angle
        sine = angle * horner(SIN_TERMS, square)
        cosine = horner(COS_TERMS, square)
        sine1 = 2.0 * sine * cosine
        cosine1 = 1.0 - 2.0 * sine * sine
        smooth = jnp.where(inside, cosine * cosine, 0.0)
        cut_slope = jnp.where(inside, (-math.pi / CUTOFF) * sine * cosine, 0.0)
        scale = mask * smooth * inverse
        tilt = mask * (cut_slope - smooth * inverse) * inverse
        twice = 2.0 * cosine1
        s_prev, s_here = jnp.zeros_like(sine1), sine1
        c_prev, c_here = jnp.ones_like(sine1), cosine1
        for b in range(NB):
            phi[e, pl.ds(b, 32, stride=NB), :] = scale * s_here
            if 2 <= e <= 7:
                slope[e - 2, pl.ds(b, 32, stride=NB), :] = tilt * s_here + scale * (
                    ((b + 1) * math.pi / CUTOFF) * c_here
                )
            s_prev, s_here = s_here, twice * s_here - s_prev
            c_prev, c_here = c_here, twice * c_here - c_prev
        total = phi[e, 0:NB]
        for o in range(1, NOFF):
            total = total + phi[e, o * NB : (o + 1) * NB]
        summed[e] = total

    first, second = radial_turned[0], radial_turned[1]
    square_t, hidden_t, message_t = turned[SQUARE], turned[HIDDEN], turned[MESSAGE]

    held = {}

    def node_mix(pair):
        mix = jnp.dot(
            first,
            radial_moving(jnp.concatenate([summed[2 * pair], summed[2 * pair + 1]], axis=1)),
            preferred_element_type=F32,
        )
        for k in range(2):
            if 2 <= 2 * pair <= 6:
                radial_mix[2 * pair + k - 2] = mix[:, k * LAYER : (k + 1) * LAYER]
        held[pair] = mix, product(square_t, mix * mix)

    def node_hidden(pair):
        mix, mixed = held[pair]
        held[pair] = product(hidden_t, mix + mixed)

    def node_message(pair):
        act, act_slope = silu_parts(held[pair])
        for k in range(2):
            hidden[2 * pair + k] = act[:, k * LAYER : (k + 1) * LAYER]
            if 2 <= 2 * pair <= 6:
                hidden_slope[2 * pair + k - 2] = act_slope[:, k * LAYER : (k + 1) * LAYER]
        held[pair] = product(message_t, act)

    def node_send(pair):
        for k in range(2):
            for number, (dx, dy) in enumerate(LATERALS):
                part = held[pair][:, k * LAYER : (k + 1) * LAYER]
                if (dx, dy) != (0, 0):
                    part = take(part, shifted_site((CH, LAYER), dx, dy))
                message[number, 2 * pair + k] = part

    stages = (node_mix, node_hidden, node_message, node_send)
    for step in range(5 + len(stages) - 1):
        for number, stage in enumerate(stages):
            if 0 <= step - number < 5:
                stage(step - number)

    output_t, output_n = turned[OUTPUT], straight[OUTPUT]

    def readout(pair):
        a = 2 * pair
        e = a + 1
        total = jnp.concatenate([hidden[e], hidden[e + 1]], axis=1)
        for o, (dx, dy, dz) in enumerate(OFFSETS):
            here = slice(o * NB, (o + 1) * NB)
            radial = jnp.dot(
                second,
                radial_moving(jnp.concatenate([phi[e, here], phi[e + 1, here]], axis=1)),
                preferred_element_type=F32,
            )
            number = LATERAL_OF[(dx, dy)]
            total = total + radial * jnp.concatenate([message[number, e + dz], message[number, e + 1 + dz]], axis=1)
        held[pair] = total

    weight = jnp.concatenate([w_energy[...]] * 2, axis=1)
    energies = []

    def readout_energy(pair):
        act, act_slope = silu_parts(product(output_t, held[pair]))
        if 1 <= pair <= 2:
            energies.append(jnp.sum(weight * act, axis=0, keepdims=True))
        held[pair] = weight * act_slope

    def readout_grad(pair):
        grad = product(output_n, held[pair])
        grad_out[2 * pair] = grad[:, :LAYER]
        grad_out[2 * pair + 1] = grad[:, LAYER:]

    stages = (readout, readout_energy, readout_grad)
    for step in range(4 + len(stages) - 1):
        for number, stage in enumerate(stages):
            if 0 <= step - number < 4:
                stage(step - number)
    energy = energies[0] + energies[1]

    along[0:3] = jnp.where(even, middle[26:29, :], middle[29:32, :])
    along[3:4] = jnp.where(iota((1, 4 * LAYER), 1) == 0, jnp.sum(energy), 0.0)
    along[4:8] = jnp.zeros((4, 4 * LAYER), F32)


def backward_kernel(
    reach,
    inverse_radius,
    slope,
    radial_mix,
    hidden_slope,
    message,
    phi,
    grad_out,
    straight,
    radial,
    radial_turned,
    forces,
    grad_summed,
    pair_grad,
    pair_grad_turned,
):
    row = iota((32, LAYER), 0)
    site = site_of_row()
    square_n, hidden_n, message_n = straight[SQUARE], straight[HIDDEN], straight[MESSAGE]
    first_n, second_n = radial[0], radial[1]
    second = radial_turned[1]

    def back(pair):
        f = 2 * pair
        parts = [None, None]
        for dx, dy in LATERALS:
            total = None
            for dz in (-1, 0, 1):
                if (dx, dy, dz) == (0, 0, 0):
                    continue
                a = f + 1 - dz
                o = ROW_OF[(dx, dy, dz)]
                here = slice(o * NB, (o + 1) * NB)
                edge_radial = jnp.dot(
                    second,
                    radial_moving(jnp.concatenate([phi[a + 1, here], phi[a + 2, here]], axis=1)),
                    preferred_element_type=F32,
                )
                term = edge_radial * jnp.concatenate([grad_out[a], grad_out[a + 1]], axis=1)
                total = term if total is None else total + term
            for k in range(2):
                part = total[:, k * LAYER : (k + 1) * LAYER]
                if (dx, dy) != (0, 0):
                    part = take(part, shifted_site((CH, LAYER), -dx, -dy))
                parts[k] = part if parts[k] is None else parts[k] + part
        return jnp.concatenate(parts, axis=1)

    grad_message = jnp.concatenate([back(pair) for pair in range(3)], axis=1)
    grad_hidden = jnp.concatenate([grad_out[a] for a in range(1, 7)], axis=1) + product(message_n, grad_message)
    grad_pre = grad_hidden * jnp.concatenate([hidden_slope[f] for f in range(6)], axis=1)
    grad_mixed = product(hidden_n, grad_pre)
    mix = jnp.concatenate([radial_mix[f] for f in range(6)], axis=1)
    grad = product(first_n, grad_mixed + 2.0 * mix * product(square_n, grad_mixed))
    for f in range(6):
        grad_summed[f] = grad[:, f * LAYER : (f + 1) * LAYER]

    for f in range(6):
        pair_grad_turned[f] = jnp.zeros((32, LAYER), F32)
    for f in range(4):
        pair_grad[f] = jnp.zeros((32, LAYER), F32)

    def edges(f0, f1, offset0, offset1):
        number = LATERAL_OF[offset0[:2]]
        moved = jnp.concatenate(
            [
                grad_out[f0 + 1] * message[number, f0 + 2 + offset0[2]],
                grad_out[f1 + 1] * message[number, f1 + 2 + offset1[2]],
            ],
            axis=1,
        )
        grad = product(second_n, moved)
        out = []
        for k, (f, offset) in enumerate(((f0, offset0), (f1, offset1))):
            o = ROW_OF[offset]
            value = (grad[:, k * LAYER : (k + 1) * LAYER] + grad_summed[f]) * slope[f, o * NB : (o + 1) * NB]
            out.append(jnp.sum(value, axis=0, keepdims=True))
        return out

    def own_edges(pair):
        f = 2 * pair + 1
        for o, offset in enumerate(OFFSETS):
            left, right = edges(f, f + 1, offset, offset)
            pair_grad[f - 1, o : o + 1] = left
            pair_grad[f, o : o + 1] = right
            pair_grad_turned[f, 25 - o : 26 - o] = left
            pair_grad_turned[f + 1, 25 - o : 26 - o] = right

    for pair in range(2):
        own_edges(pair)
    for dx, dy in LATERALS:
        up, down = (dx, dy, 1), (dx, dy, -1)
        left, right = edges(0, 5, up, down)
        pair_grad_turned[0, 25 - ROW_OF[up] : 26 - ROW_OF[up]] = left
        pair_grad_turned[5, 25 - ROW_OF[down] : 26 - ROW_OF[down]] = right

    force_parts = []
    for f in range(1, 5):
        source = jnp.where(
            row < 9, pair_grad_turned[f - 1], jnp.where(row < 17, pair_grad_turned[f], pair_grad_turned[f + 1])
        )
        pull = (pair_grad[f - 1] + take(source, site)) * inverse_radius[f - 1]
        force_parts.append(
            jnp.concatenate([jnp.sum(pull * reach[f - 1, c], axis=0, keepdims=True) for c in range(3)], axis=0)
        )
    force = jnp.concatenate(force_parts, axis=1)

    forces[0:3] = force
    forces[3:8] = jnp.zeros((5, 4 * LAYER), F32)


def sums_kernel(parity, middle, forces, along, path, table, kept, sent):
    even = parity[0] == 0
    low, high = middle[26:29, :], middle[29:32, :]
    force, beside = forces[0:3], path[0:3]
    up = jnp.where(even, high - low, beside - high)
    down = jnp.where(even, low - beside, high - low)
    lane = iota((1, LAYER), 1)
    values = jnp.where(
        lane == 0, along[3:4, 0:1], jnp.where(lane == 6, jnp.broadcast_to(path[3:4, 0:1], (1, LAYER)), 0.0)
    )
    for k, term in enumerate((force * up, force * down, up * up, down * down, up * down)):
        total = jnp.sum(jnp.sum(term, axis=1, keepdims=True), axis=0, keepdims=True)
        values = values + jnp.where(lane == k + 1, total, 0.0)
    table[...] = jnp.broadcast_to(values, table.shape)
    both = jnp.concatenate([force, beside, jnp.zeros((2, 4 * LAYER), F32)], axis=0)
    left, right = both[:, : 2 * LAYER], both[:, 2 * LAYER :]
    kept[...] = jnp.where(even, left, right)
    sent[...] = jnp.where(even, right, left)


def combine_kernel(images, image_group, parity, climbing, table, own, kept, received, site_of_slot, out, energies):
    even = parity[0] == 0
    total = table[0:8]
    for k in range(8, table.shape[0], 8):
        total = total + table[k : k + 8]
    total = total[0:4] + total[4:8]
    total = total[0:2] + total[2:4]
    energy = (total[0:1, 6:7], total[0:1, 0:1], total[1:2, 0:1], total[1:2, 6:7])
    low, high = own[26:29, :], own[29:32, :]
    f_kept, f_received = kept[0:3, :], received[0:3, :]
    p_kept, p_received = kept[3:6, :], received[3:6, :]
    sides = (
        (jnp.where(even, f_kept, f_received), high - low, low - jnp.where(even, p_kept, p_received)),
        (jnp.where(even, f_received, f_kept), jnp.where(even, p_received, p_kept) - high, high - low),
    )
    slot = site_of_slot[...]
    for k, (force, up, down) in enumerate(sides):
        image = 2 * image_group[0] + k
        here = total[k : k + 1]
        v_prev, v_here, v_next = energy[k : k + 3]
        big = jnp.maximum(jnp.abs(v_next - v_here), jnp.abs(v_prev - v_here))
        small = jnp.minimum(jnp.abs(v_next - v_here), jnp.abs(v_prev - v_here))
        rising = jnp.logical_and(v_next > v_here, v_here > v_prev)
        falling = jnp.logical_and(v_next < v_here, v_here < v_prev)
        higher = v_next > v_prev
        a = jnp.where(rising, 1.0, jnp.where(falling, 0.0, jnp.where(higher, big, small)))
        b = jnp.where(rising, 0.0, jnp.where(falling, 1.0, jnp.where(higher, small, big)))
        fu, fd, uu, dd, ud = (here[:, i : i + 1] for i in range(1, 6))
        tangent_sq = a * a * uu + 2.0 * a * b * ud + b * b * dd
        norm = jnp.sqrt(tangent_sq)
        along = (a * fu + b * fd) / norm
        pull = STIFFNESS * (jnp.sqrt(uu) - jnp.sqrt(dd))
        amount = jnp.where(image == climbing[0], 2.0 * along, along - pull) / norm
        tangent = a * up + b * down
        result = force - amount * tangent
        end = jnp.logical_or(image == 0, image == images - 1)
        result = jnp.where(end, 0.0, result)
        result = jnp.concatenate([result, jnp.zeros((5, 2 * LAYER), F32)], axis=0)
        for part in range(NZL):
            index = slot[:, part * LAYER : (part + 1) * LAYER]
            low_index = index & (LAYER - 1)
            back = jnp.where(index < LAYER, take(result[:, :LAYER], low_index), take(result[:, LAYER:], low_index))
            for c in range(3):
                out[c, k : k + 1, part * LAYER : (part + 1) * LAYER] = back[c : c + 1]
        energies[k] = here[0, 0]


def vmem():
    return pl.BlockSpec(memory_space=pltpu.VMEM)


def hbm():
    return pl.BlockSpec(memory_space=pltpu.HBM)


def stay(array):
    return pltpu.with_memory_space_constraint(array, pltpu.HBM)


def smem():
    return pl.BlockSpec(memory_space=pltpu.SMEM)


def local(
    positions,
    neighbours,
    ghost_slots,
    climbing,
    w_radial1,
    w_square,
    w_hidden,
    w_message,
    w_radial2,
    w_output,
    w_energy,
):
    slabs = lax.axis_size("slab")
    groups = lax.axis_size("image")
    group = lax.axis_index("image")
    slab = lax.axis_index("slab")
    parity = slab % 2
    even = parity == 0
    parity_arg = parity.astype(I32).reshape(1)

    small = pltpu.CompilerParams(vmem_limit_bytes=4 * 1024 * 1024)
    prepared, site_of_slot = pl.pallas_call(
        prepare_kernel,
        out_shape=(
            jax.ShapeDtypeStruct((ROWS, 2 * LAYER), F32),
            jax.ShapeDtypeStruct((8, 2 * LAYER), I32),
        ),
        in_specs=[hbm()] * 3,
        out_specs=(vmem(), vmem()),
        scratch_shapes=[
            pltpu.VMEM((64, LAYER), I32),
            pltpu.VMEM((2, LAYER), I32),
            pltpu.VMEM((3, 2, 2 * LAYER), F32),
            pltpu.SemaphoreType.DMA((3,)),
        ],
        compiler_params=small,
    )(
        stay(neighbours.reshape(64, LAYER)), stay(ghost_slots), stay(positions.transpose(1, 0, 2))
    )

    mate = lax.ppermute(prepared, "slab", [(i, i ^ 1) for i in range(slabs)])
    middle = jnp.concatenate([jnp.where(even, prepared, mate), jnp.where(even, mate, prepared)], axis=1)
    pairs = slabs // 2
    partners = []
    for i in range(slabs):
        p = i // 2
        other = p ^ 1 if i % 2 == 0 else (p + 1 if p % 2 else p - 1) % pairs
        partners.append((i, 2 * other + i % 2))
    far = lax.ppermute(middle, "slab", partners)
    side = ((slab & 1) | ((((slab >> 1) + slab + 1) & 1) << 1)).astype(I32).reshape(1)

    def whole(*extents):
        return jax.ShapeDtypeStruct(extents, F32)

    turned, straight, radial, radial_turned, energy_column = pl.pallas_call(
        weights_kernel,
        out_shape=(
            jax.ShapeDtypeStruct((4, 2 * CH, 2 * CH), BF16),
            jax.ShapeDtypeStruct((4, 2 * CH, 2 * CH), BF16),
            jax.ShapeDtypeStruct((2, 2 * NB, 2 * CH), BF16),
            jax.ShapeDtypeStruct((2, CH, 4 * NB), BF16),
            whole(CH, CH),
        ),
        in_specs=[hbm()] * 7,
        out_specs=tuple(vmem() for _ in range(5)),
        scratch_shapes=[
            pltpu.VMEM((4, CH, CH), F32),
            pltpu.VMEM((2, NB, CH), F32),
            pltpu.VMEM((1, CH), F32),
            pltpu.SemaphoreType.DMA((7,)),
        ],
        compiler_params=small,
        cost_estimate=pl.CostEstimate(flops=10**8, bytes_accessed=1 << 22, transcendentals=0),
    )(*map(stay, (w_square, w_hidden, w_message, w_output, w_radial1, w_radial2, w_energy.reshape(1, CH))))

    far, turned, straight = lax.optimization_barrier((far, turned, straight))
    traded = lax.ppermute(far, "slab", [(i, i ^ 1) for i in range(slabs)])

    along, *saved = pl.pallas_call(
        lambda *refs: forward_kernel(slabs * NZL * LATTICE, *refs),
        out_shape=(
            whole(8, 4 * LAYER),
            whole(4, 3, 32, LAYER),
            whole(4, 32, LAYER),
            whole(6, 32 * NB, LAYER),
            whole(6, CH, LAYER),
            whole(6, CH, LAYER),
            whole(9, 10, CH, LAYER),
            whole(10, 32 * NB, LAYER),
            whole(8, CH, LAYER),
        ),
        in_specs=[smem()] + [vmem()] * 7,
        out_specs=tuple(vmem() for _ in range(9)),
        scratch_shapes=[
            pltpu.VMEM((12, 8, LAYER), F32),
            pltpu.VMEM((10, NB, LAYER), F32),
            pltpu.VMEM((10, CH, LAYER), F32),
            pltpu.VMEM((2, ROWS, 4 * LAYER), F32),
        ],
        compiler_params=pltpu.CompilerParams(vmem_limit_bytes=20 * 1024 * 1024),
    )(
        side,
        far,
        middle,
        traded,
        turned,
        straight,
        radial_turned,
        energy_column,
    )

    hops = []
    for g in range(groups):
        for s in range(slabs):
            if s % 2 and g + 1 < groups:
                hops.append((g * slabs + s, (g + 1) * slabs + s - 1))
            if s % 2 == 0 and g > 0:
                hops.append((g * slabs + s, (g - 1) * slabs + s + 1))
    path = lax.ppermute(along, ("image", "slab"), hops)

    forces = pl.pallas_call(
        backward_kernel,
        out_shape=whole(8, 4 * LAYER),
        in_specs=[vmem()] * 11,
        out_specs=vmem(),
        scratch_shapes=[
            pltpu.VMEM((6, NB, LAYER), F32),
            pltpu.VMEM((4, 32, LAYER), F32),
            pltpu.VMEM((6, 32, LAYER), F32),
        ],
        compiler_params=pltpu.CompilerParams(vmem_limit_bytes=20 * 1024 * 1024),
        cost_estimate=pl.CostEstimate(flops=4 * 10**9, bytes_accessed=1 << 22, transcendentals=0),
    )(*saved, straight, radial, radial_turned)

    table, kept, sent = pl.pallas_call(
        sums_kernel,
        out_shape=(whole(slabs, LAYER), whole(8, 2 * LAYER), whole(8, 2 * LAYER)),
        in_specs=[smem()] + [vmem()] * 4,
        out_specs=(vmem(), vmem(), vmem()),
        compiler_params=small,
    )(parity_arg, middle, forces, along, path)

    received = lax.ppermute(sent, "slab", [(i, i ^ 1) for i in range(slabs)])
    table = lax.all_to_all(table.reshape(slabs, 1, LAYER), "slab", 0, 0, tiled=False).reshape(slabs, LAYER)

    result, energies = pl.pallas_call(
        lambda *refs: combine_kernel(2 * groups, *refs),
        out_shape=(
            jax.ShapeDtypeStruct((3, 2, 2 * LAYER), F32),
            jax.ShapeDtypeStruct((2,), F32),
        ),
        in_specs=[smem()] * 3 + [vmem()] * 5,
        out_specs=(vmem(), smem()),
        compiler_params=small,
    )(
        group.astype(I32).reshape(1),
        parity_arg,
        climbing,
        table,
        prepared,
        kept,
        received,
        site_of_slot,
    )
    return result.transpose(1, 0, 2), energies


def solution(mesh):
    return jax.shard_map(
        local,
        mesh=mesh,
        in_specs=(
            P("image", None, "slab"),
            P("slab"),
            P(None, "slab"),
            P(),
            P(),
            P(),
            P(),
            P(),
            P(),
            P(),
            P(),
        ),
        out_specs=(P("image", None, "slab"), P("image")),
        check_vma=False,
    )
```

```python
import math

import jax
import jax.numpy as jnp
from jax import lax
from jax.experimental import pallas as pl
from jax.experimental.pallas import tpu as pltpu
from jax.sharding import PartitionSpec as P

NB = 8
NX = 16
NY = 8
NZL = 2
LAYER = 128
CH = 128
NOFF = 26
ROWS = 32

LATTICE = 2.55
CUTOFF = 5.0
STIFFNESS = 5.0
F32 = jnp.float32
BF16 = jnp.bfloat16
I32 = jnp.int32

OFFSETS = [
    (dx, dy, dz)
    for dz in (-1, 0, 1)
    for dy in (-1, 0, 1)
    for dx in (-1, 0, 1)
    if (dx, dy, dz) != (0, 0, 0)
]
ROW_OF = {offset: row for row, offset in enumerate(OFFSETS)}
LATERALS = [(dx, dy) for dy in (-1, 0, 1) for dx in (-1, 0, 1)]
LATERAL_OF = {lateral: number for number, lateral in enumerate(LATERALS)}


def take(values, index):
    return jnp.take_along_axis(values, index, axis=1, mode="promise_in_bounds")


def iota(shape, dim):
    return lax.broadcasted_iota(I32, shape, dim)


def shifted_site(shape, dx, dy):
    lane = iota(shape, len(shape) - 1)
    return ((((lane >> 4) + dy) & (NY - 1)) << 4) | ((lane + dx) & (NX - 1))


def site_of_row():
    row = iota((32, LAYER), 0)
    code = row + (row >= 13).astype(I32)
    level = (code >= 9).astype(I32) + (code >= 18).astype(I32)
    rest = code - 9 * level
    line = (rest >= 3).astype(I32) + (rest >= 6).astype(I32)
    column = rest - 3 * line
    return shifted_site((32, LAYER), column - 1, line - 1) & (LAYER - 1)


def silu_parts(values):
    sigma = 1.0 / (1.0 + jnp.exp(-values))
    return values * sigma, sigma * (1.0 + values * (1.0 - sigma))


def halves(values):
    high = values.astype(BF16)
    low = (values - high.astype(F32)).astype(BF16)
    return high, low


def stationary(matrix):
    high, low = halves(matrix)
    return jnp.concatenate(
        [jnp.concatenate([high, high], axis=1), jnp.concatenate([low, low], axis=1)], axis=0
    )


def product(packed, values):
    high, low = halves(values)
    out = jnp.dot(packed, jnp.concatenate([high, low], axis=0), preferred_element_type=F32)
    rows = packed.shape[0] // 2
    return out[:rows] + out[rows:]


def radial_stationary(matrix):
    high, low = halves(matrix.T)
    return jnp.concatenate([high, high, low, low], axis=1)


def radial_moving(values):
    high = values.astype(BF16).astype(F32)
    both = jnp.concatenate([high, values - high], axis=0).astype(BF16)
    return jnp.concatenate([both, both], axis=0)


def prepare_kernel(
    neighbours_hbm, ghost_hbm, positions_hbm, out, site_of_slot, neighbours, ghost_slots, positions, arrived
):
    copies = [
        pltpu.make_async_copy(source, target, arrived.at[number])
        for number, (source, target) in enumerate(
            ((ghost_hbm, ghost_slots), (neighbours_hbm, neighbours), (positions_hbm, positions))
        )
    ]
    for copy in copies:
        copy.start()
    for copy in copies:
        copy.wait()
    slots = ghost_slots[...]
    inverse = jnp.zeros((8, 2 * LAYER), F32)
    for layer in range(NZL):
        hit = (jnp.broadcast_to(slots[layer : layer + 1], (2 * LAYER, LAYER)) == iota((2 * LAYER, LAYER), 0))
        sites = (iota((8, LAYER), 1) + layer * LAYER).astype(F32).astype(BF16)
        inverse = inverse + lax.dot_general(
            sites,
            jnp.where(hit, 1.0, 0.0).astype(BF16),
            (((1,), (1,)), ((), ())),
            preferred_element_type=F32,
        )
    inverse = inverse.astype(I32)
    site_of_slot[...] = inverse
    first = jnp.broadcast_to(inverse[0:1, :LAYER], (32, LAYER))
    second = jnp.broadcast_to(inverse[0:1, LAYER:], (32, LAYER))
    sides = [
        jnp.concatenate(
            [positions[c, k : k + 1, half * LAYER : (half + 1) * LAYER] for k in range(2) for c in range(3)]
            + [jnp.zeros((2, LAYER), F32)],
            axis=0,
        )
        for half in range(2)
    ]
    listed = neighbours[...].astype(F32)
    turned = jnp.concatenate([listed, jnp.zeros((64, LAYER), F32)], axis=0).T
    site = iota((32, LAYER), 1)
    row = iota((32, LAYER), 0)
    for layer in range(NZL):
        here = slice(layer * LAYER, (layer + 1) * LAYER)
        slot = jnp.broadcast_to(slots[layer : layer + 1], (8, LAYER))
        low = slot & (LAYER - 1)
        coords = jnp.where(slot < LAYER, take(sides[0], low), take(sides[1], low))
        slot = jnp.broadcast_to(slots[layer : layer + 1], (32, LAYER))
        picked = take(turned[0:32], slot >> 2)
        for part in range(1, 4):
            picked = jnp.where((slot & 3) == part, take(turned[32 * part : 32 * part + 32], slot >> 2), picked)
        entry = picked.astype(I32)
        low = entry & (LAYER - 1)
        own = jnp.where(entry < LAYER, take(first, low), take(second, low))
        inside = entry < 2 * LAYER
        level = jnp.where(inside, own >> 7, jnp.where(entry < 3 * LAYER, -1, NZL))
        target = jnp.where(inside, own & (LAYER - 1), low)
        column = ((target & (NX - 1)) - (site & (NX - 1)) + 1) & (NX - 1)
        line = ((target >> 4) - (site >> 4) + 1) & (NY - 1)
        code = (level - layer + 1) * 9 + line * 3 + column
        code = jnp.where(code > 13, code - 1, code) & 31
        bits = jnp.where(entry >= 0, jnp.left_shift(jnp.ones_like(code), code), 0)
        bits = bits[0:16] | bits[16:32]
        bits = bits[0:8] | bits[8:16]
        bits = bits[0:4] | bits[4:8]
        bits = bits[0:2] | bits[2:4]
        bits = bits[0:1] | bits[1:2]
        mask = (jnp.broadcast_to(bits, (32, LAYER)) >> row) & 1
        out[0:NOFF, here] = mask[0:NOFF].astype(F32)
        out[NOFF:32, here] = coords[0:6]


SIN_TERMS = [(-1.0) ** k / math.factorial(2 * k + 1) for k in range(7)]
COS_TERMS = [(-1.0) ** k / math.factorial(2 * k) for k in range(8)]


def horner(terms, square):
    total = jnp.full_like(square, terms[-1])
    for term in terms[-2::-1]:
        total = total * square + term
    return total


SQUARE, HIDDEN, MESSAGE, OUTPUT = range(4)


def weights_kernel(
    w_square,
    w_hidden,
    w_message,
    w_output,
    w_radial1,
    w_radial2,
    w_energy,
    turned,
    straight,
    radial,
    radial_turned,
    energy,
    squares,
    radials,
    column,
    arrived,
):
    moves = [(ref, squares.at[number]) for number, ref in enumerate((w_square, w_hidden, w_message, w_output))]
    moves += [(w_radial1, radials.at[0]), (w_radial2, radials.at[1]), (w_energy, column)]
    copies = [pltpu.make_async_copy(*move, arrived.at[number]) for number, move in enumerate(moves)]
    for copy in copies:
        copy.start()
    for copy in copies:
        copy.wait()
    for number in range(4):
        turned[number] = stationary(squares[number].T)
        straight[number] = stationary(squares[number])
    for number in range(2):
        radial[number] = stationary(radials[number])
        radial_turned[number] = radial_stationary(radials[number])
    energy[...] = jnp.broadcast_to(column[...], (CH, CH)).T


def forward_kernel(
    cell_z,
    far,
    middle,
    traded,
    turned,
    straight,
    radial_turned,
    w_energy,
    along,
    reach,
    inverse_radius,
    slope,
    radial_mix,
    hidden_slope,
    message,
    phi,
    grad_out,
    coords,
    summed,
    hidden,
    outer,
):
    slab = lax.axis_index("slab")
    even = (slab & 1) == 0
    place = ((slab >> 1) + slab + 1) & 1
    outer[place] = far[...]
    outer[1 - place] = traded[...]

    def level_rows(level, first, last):
        here = slice(level % 4 * LAYER, (level % 4 + 1) * LAYER)
        if 4 <= level < 8:
            return middle[first:last, here]
        return outer[0 if level < 4 else 1, first:last, here]

    for level in range(12):
        both = level_rows(level, 24, 32)
        coords[level, 0:3] = jnp.where(even, both[2:5], both[5:8])
    row = iota((32, LAYER), 0)
    site = site_of_row()
    boxes = (NX * LATTICE, NY * LATTICE, cell_z)

    for e in range(10):
        mask = jnp.where(row < NOFF, level_rows(e + 1, 0, 32), 0.0)
        squared = None
        for c in range(3):
            centre = coords[e + 1, c : c + 1]
            source = jnp.where(
                row < 9,
                jnp.broadcast_to(coords[e, c : c + 1], (32, LAYER)),
                jnp.where(
                    row < 17,
                    jnp.broadcast_to(centre, (32, LAYER)),
                    jnp.broadcast_to(coords[e + 2, c : c + 1], (32, LAYER)),
                ),
            )
            d = take(source, site) - jnp.broadcast_to(centre, (32, LAYER))
            box = jnp.float32(boxes[c])
            half = jnp.float32(0.5) * box
            d = jnp.where(d > half, d - box, jnp.where(d < -half, d + box, d))
            if 3 <= e <= 6:
                reach[e - 3, c] = d
            squared = d * d if squared is None else squared + d * d
        squared = jnp.where(squared > 0.0, squared, 1.0)
        radius = jnp.sqrt(squared)
        inverse = 1.0 / radius
        if 3 <= e <= 6:
            inverse_radius[e - 3] = inverse
        inside = radius < CUTOFF
        angle = jnp.minimum(radius * (math.pi / (2.0 * CUTOFF)), 0.5 * math.pi)
        square = angle * angle
        sine = angle * horner(SIN_TERMS, square)
        cosine = horner(COS_TERMS, square)
        sine1 = 2.0 * sine * cosine
        cosine1 = 1.0 - 2.0 * sine * sine
        smooth = jnp.where(inside, cosine * cosine, 0.0)
        cut_slope = jnp.where(inside, (-math.pi / CUTOFF) * sine * cosine, 0.0)
        scale = mask * smooth * inverse
        tilt = mask * (cut_slope - smooth * inverse) * inverse
        twice = 2.0 * cosine1
        s_prev, s_here = jnp.zeros_like(sine1), sine1
        c_prev, c_here = jnp.ones_like(sine1), cosine1
        for b in range(NB):
            phi[e, pl.ds(b, 32, stride=NB), :] = scale * s_here
            if 2 <= e <= 7:
                slope[e - 2, pl.ds(b, 32, stride=NB), :] = tilt * s_here + scale * (
                    ((b + 1) * math.pi / CUTOFF) * c_here
                )
            s_prev, s_here = s_here, twice * s_here - s_prev
            c_prev, c_here = c_here, twice * c_here - c_prev
        total = phi[e, 0:NB]
        for o in range(1, NOFF):
            total = total + phi[e, o * NB : (o + 1) * NB]
        summed[e] = total

    first, second = radial_turned[0], radial_turned[1]
    square_t, hidden_t, message_t = turned[SQUARE], turned[HIDDEN], turned[MESSAGE]

    held = {}

    def node_mix(pair):
        mix = jnp.dot(
            first,
            radial_moving(jnp.concatenate([summed[2 * pair], summed[2 * pair + 1]], axis=1)),
            preferred_element_type=F32,
        )
        for k in range(2):
            if 2 <= 2 * pair <= 6:
                radial_mix[2 * pair + k - 2] = mix[:, k * LAYER : (k + 1) * LAYER]
        held[pair] = mix, product(square_t, mix * mix)

    def node_hidden(pair):
        mix, mixed = held[pair]
        held[pair] = product(hidden_t, mix + mixed)

    def node_message(pair):
        act, act_slope = silu_parts(held[pair])
        for k in range(2):
            hidden[2 * pair + k] = act[:, k * LAYER : (k + 1) * LAYER]
            if 2 <= 2 * pair <= 6:
                hidden_slope[2 * pair + k - 2] = act_slope[:, k * LAYER : (k + 1) * LAYER]
        held[pair] = product(message_t, act)

    def node_send(pair):
        for k in range(2):
            for number, (dx, dy) in enumerate(LATERALS):
                part = held[pair][:, k * LAYER : (k + 1) * LAYER]
                if (dx, dy) != (0, 0):
                    part = take(part, shifted_site((CH, LAYER), dx, dy))
                message[number, 2 * pair + k] = part

    stages = (node_mix, node_hidden, node_message, node_send)
    for step in range(5 + len(stages) - 1):
        for number, stage in enumerate(stages):
            if 0 <= step - number < 5:
                stage(step - number)

    output_t, output_n = turned[OUTPUT], straight[OUTPUT]

    def readout(pair):
        a = 2 * pair
        e = a + 1
        total = jnp.concatenate([hidden[e], hidden[e + 1]], axis=1)
        for o, (dx, dy, dz) in enumerate(OFFSETS):
            here = slice(o * NB, (o + 1) * NB)
            radial = jnp.dot(
                second,
                radial_moving(jnp.concatenate([phi[e, here], phi[e + 1, here]], axis=1)),
                preferred_element_type=F32,
            )
            number = LATERAL_OF[(dx, dy)]
            total = total + radial * jnp.concatenate([message[number, e + dz], message[number, e + 1 + dz]], axis=1)
        held[pair] = total

    weight = jnp.concatenate([w_energy[...]] * 2, axis=1)
    energies = []

    def readout_energy(pair):
        act, act_slope = silu_parts(product(output_t, held[pair]))
        if 1 <= pair <= 2:
            energies.append(jnp.sum(weight * act, axis=0, keepdims=True))
        held[pair] = weight * act_slope

    def readout_grad(pair):
        grad = product(output_n, held[pair])
        grad_out[2 * pair] = grad[:, :LAYER]
        grad_out[2 * pair + 1] = grad[:, LAYER:]

    stages = (readout, readout_energy, readout_grad)
    for step in range(4 + len(stages) - 1):
        for number, stage in enumerate(stages):
            if 0 <= step - number < 4:
                stage(step - number)
    energy = energies[0] + energies[1]

    along[0:3] = jnp.where(even, middle[26:29, :], middle[29:32, :])
    along[3:4] = jnp.where(iota((1, 4 * LAYER), 1) == 0, jnp.sum(energy), 0.0)
    along[4:8] = jnp.zeros((4, 4 * LAYER), F32)


def backward_kernel(
    reach,
    inverse_radius,
    slope,
    radial_mix,
    hidden_slope,
    message,
    phi,
    grad_out,
    straight,
    radial,
    radial_turned,
    forces,
    grad_summed,
    pair_grad,
    pair_grad_turned,
):
    row = iota((32, LAYER), 0)
    site = site_of_row()
    square_n, hidden_n, message_n = straight[SQUARE], straight[HIDDEN], straight[MESSAGE]
    first_n, second_n = radial[0], radial[1]
    second = radial_turned[1]

    def back(pair):
        f = 2 * pair
        parts = [None, None]
        for dx, dy in LATERALS:
            total = None
            for dz in (-1, 0, 1):
                if (dx, dy, dz) == (0, 0, 0):
                    continue
                a = f + 1 - dz
                o = ROW_OF[(dx, dy, dz)]
                here = slice(o * NB, (o + 1) * NB)
                edge_radial = jnp.dot(
                    second,
                    radial_moving(jnp.concatenate([phi[a + 1, here], phi[a + 2, here]], axis=1)),
                    preferred_element_type=F32,
                )
                term = edge_radial * jnp.concatenate([grad_out[a], grad_out[a + 1]], axis=1)
                total = term if total is None else total + term
            for k in range(2):
                part = total[:, k * LAYER : (k + 1) * LAYER]
                if (dx, dy) != (0, 0):
                    part = take(part, shifted_site((CH, LAYER), -dx, -dy))
                parts[k] = part if parts[k] is None else parts[k] + part
        return jnp.concatenate(parts, axis=1)

    grad_message = jnp.concatenate([back(pair) for pair in range(3)], axis=1)
    grad_hidden = jnp.concatenate([grad_out[a] for a in range(1, 7)], axis=1) + product(message_n, grad_message)
    grad_pre = grad_hidden * jnp.concatenate([hidden_slope[f] for f in range(6)], axis=1)
    grad_mixed = product(hidden_n, grad_pre)
    mix = jnp.concatenate([radial_mix[f] for f in range(6)], axis=1)
    grad = product(first_n, grad_mixed + 2.0 * mix * product(square_n, grad_mixed))
    for f in range(6):
        grad_summed[f] = grad[:, f * LAYER : (f + 1) * LAYER]

    for f in range(6):
        pair_grad_turned[f] = jnp.zeros((32, LAYER), F32)
    for f in range(4):
        pair_grad[f] = jnp.zeros((32, LAYER), F32)

    def edges(f0, f1, offset0, offset1):
        number = LATERAL_OF[offset0[:2]]
        moved = jnp.concatenate(
            [
                grad_out[f0 + 1] * message[number, f0 + 2 + offset0[2]],
                grad_out[f1 + 1] * message[number, f1 + 2 + offset1[2]],
            ],
            axis=1,
        )
        grad = product(second_n, moved)
        out = []
        for k, (f, offset) in enumerate(((f0, offset0), (f1, offset1))):
            o = ROW_OF[offset]
            value = (grad[:, k * LAYER : (k + 1) * LAYER] + grad_summed[f]) * slope[f, o * NB : (o + 1) * NB]
            out.append(jnp.sum(value, axis=0, keepdims=True))
        return out

    def own_edges(pair):
        f = 2 * pair + 1
        for o, offset in enumerate(OFFSETS):
            left, right = edges(f, f + 1, offset, offset)
            pair_grad[f - 1, o : o + 1] = left
            pair_grad[f, o : o + 1] = right
            pair_grad_turned[f, 25 - o : 26 - o] = left
            pair_grad_turned[f + 1, 25 - o : 26 - o] = right

    for pair in range(2):
        own_edges(pair)
    for dx, dy in LATERALS:
        up, down = (dx, dy, 1), (dx, dy, -1)
        left, right = edges(0, 5, up, down)
        pair_grad_turned[0, 25 - ROW_OF[up] : 26 - ROW_OF[up]] = left
        pair_grad_turned[5, 25 - ROW_OF[down] : 26 - ROW_OF[down]] = right

    force_parts = []
    for f in range(1, 5):
        source = jnp.where(
            row < 9, pair_grad_turned[f - 1], jnp.where(row < 17, pair_grad_turned[f], pair_grad_turned[f + 1])
        )
        pull = (pair_grad[f - 1] + take(source, site)) * inverse_radius[f - 1]
        force_parts.append(
            jnp.concatenate([jnp.sum(pull * reach[f - 1, c], axis=0, keepdims=True) for c in range(3)], axis=0)
        )
    force = jnp.concatenate(force_parts, axis=1)

    forces[0:3] = force
    forces[3:8] = jnp.zeros((5, 4 * LAYER), F32)


def sums_kernel(middle, forces, along, path, table, kept, sent):
    even = (lax.axis_index("slab") & 1) == 0
    low, high = middle[26:29, :], middle[29:32, :]
    force, beside = forces[0:3], path[0:3]
    up = jnp.where(even, high - low, beside - high)
    down = jnp.where(even, low - beside, high - low)
    lane = iota((1, LAYER), 1)
    values = jnp.where(
        lane == 0, along[3:4, 0:1], jnp.where(lane == 6, jnp.broadcast_to(path[3:4, 0:1], (1, LAYER)), 0.0)
    )
    for k, term in enumerate((force * up, force * down, up * up, down * down, up * down)):
        total = jnp.sum(jnp.sum(term, axis=1, keepdims=True), axis=0, keepdims=True)
        values = values + jnp.where(lane == k + 1, total, 0.0)
    table[...] = jnp.broadcast_to(values, table.shape)
    both = jnp.concatenate([force, beside, jnp.zeros((2, 4 * LAYER), F32)], axis=0)
    left, right = both[:, : 2 * LAYER], both[:, 2 * LAYER :]
    kept[...] = jnp.where(even, left, right)
    sent[...] = jnp.where(even, right, left)


def combine_kernel(images, climbing, table, own, kept, received, site_of_slot, out, energies):
    even = (lax.axis_index("slab") & 1) == 0
    total = table[0:8]
    for k in range(8, table.shape[0], 8):
        total = total + table[k : k + 8]
    total = total[0:4] + total[4:8]
    total = total[0:2] + total[2:4]
    energy = (total[0:1, 6:7], total[0:1, 0:1], total[1:2, 0:1], total[1:2, 6:7])
    low, high = own[26:29, :], own[29:32, :]
    f_kept, f_received = kept[0:3, :], received[0:3, :]
    p_kept, p_received = kept[3:6, :], received[3:6, :]
    sides = (
        (jnp.where(even, f_kept, f_received), high - low, low - jnp.where(even, p_kept, p_received)),
        (jnp.where(even, f_received, f_kept), jnp.where(even, p_received, p_kept) - high, high - low),
    )
    slot = site_of_slot[...]
    for k, (force, up, down) in enumerate(sides):
        image = 2 * lax.axis_index("image") + k
        here = total[k : k + 1]
        v_prev, v_here, v_next = energy[k : k + 3]
        big = jnp.maximum(jnp.abs(v_next - v_here), jnp.abs(v_prev - v_here))
        small = jnp.minimum(jnp.abs(v_next - v_here), jnp.abs(v_prev - v_here))
        rising = jnp.logical_and(v_next > v_here, v_here > v_prev)
        falling = jnp.logical_and(v_next < v_here, v_here < v_prev)
        higher = v_next > v_prev
        a = jnp.where(rising, 1.0, jnp.where(falling, 0.0, jnp.where(higher, big, small)))
        b = jnp.where(rising, 0.0, jnp.where(falling, 1.0, jnp.where(higher, small, big)))
        fu, fd, uu, dd, ud = (here[:, i : i + 1] for i in range(1, 6))
        tangent_sq = a * a * uu + 2.0 * a * b * ud + b * b * dd
        norm = jnp.sqrt(tangent_sq)
        along = (a * fu + b * fd) / norm
        pull = STIFFNESS * (jnp.sqrt(uu) - jnp.sqrt(dd))
        amount = jnp.where(image == climbing[0], 2.0 * along, along - pull) / norm
        tangent = a * up + b * down
        result = force - amount * tangent
        end = jnp.logical_or(image == 0, image == images - 1)
        result = jnp.where(end, 0.0, result)
        result = jnp.concatenate([result, jnp.zeros((5, 2 * LAYER), F32)], axis=0)
        for part in range(NZL):
            index = slot[:, part * LAYER : (part + 1) * LAYER]
            low_index = index & (LAYER - 1)
            back = jnp.where(index < LAYER, take(result[:, :LAYER], low_index), take(result[:, LAYER:], low_index))
            for c in range(3):
                out[c, k : k + 1, part * LAYER : (part + 1) * LAYER] = back[c : c + 1]
        energies[k] = here[0, 0]


def vmem():
    return pl.BlockSpec(memory_space=pltpu.VMEM)


def hbm():
    return pl.BlockSpec(memory_space=pltpu.HBM)


def stay(array):
    return pltpu.with_memory_space_constraint(array, pltpu.HBM)


def smem():
    return pl.BlockSpec(memory_space=pltpu.SMEM)


def local(
    positions,
    neighbours,
    ghost_slots,
    climbing,
    w_radial1,
    w_square,
    w_hidden,
    w_message,
    w_radial2,
    w_output,
    w_energy,
):
    slabs = lax.axis_size("slab")
    groups = lax.axis_size("image")
    slab = lax.axis_index("slab")
    parity = slab % 2
    even = parity == 0

    small = pltpu.CompilerParams(vmem_limit_bytes=4 * 1024 * 1024)
    prepared, site_of_slot = pl.pallas_call(
        prepare_kernel,
        out_shape=(
            jax.ShapeDtypeStruct((ROWS, 2 * LAYER), F32),
            jax.ShapeDtypeStruct((8, 2 * LAYER), I32),
        ),
        in_specs=[hbm()] * 3,
        out_specs=(vmem(), vmem()),
        scratch_shapes=[
            pltpu.VMEM((64, LAYER), I32),
            pltpu.VMEM((2, LAYER), I32),
            pltpu.VMEM((3, 2, 2 * LAYER), F32),
            pltpu.SemaphoreType.DMA((3,)),
        ],
        compiler_params=small,
    )(
        stay(neighbours.reshape(64, LAYER)), stay(ghost_slots), stay(positions.transpose(1, 0, 2))
    )

    mate = lax.ppermute(prepared, "slab", [(i, i ^ 1) for i in range(slabs)])
    middle = jnp.concatenate([jnp.where(even, prepared, mate), jnp.where(even, mate, prepared)], axis=1)
    pairs = slabs // 2
    partners = []
    for i in range(slabs):
        p = i // 2
        other = p ^ 1 if i % 2 == 0 else (p + 1 if p % 2 else p - 1) % pairs
        partners.append((i, 2 * other + i % 2))
    far = lax.ppermute(middle, "slab", partners)
    def whole(*extents):
        return jax.ShapeDtypeStruct(extents, F32)

    turned, straight, radial, radial_turned, energy_column = pl.pallas_call(
        weights_kernel,
        out_shape=(
            jax.ShapeDtypeStruct((4, 2 * CH, 2 * CH), BF16),
            jax.ShapeDtypeStruct((4, 2 * CH, 2 * CH), BF16),
            jax.ShapeDtypeStruct((2, 2 * NB, 2 * CH), BF16),
            jax.ShapeDtypeStruct((2, CH, 4 * NB), BF16),
            whole(CH, CH),
        ),
        in_specs=[hbm()] * 7,
        out_specs=tuple(vmem() for _ in range(5)),
        scratch_shapes=[
            pltpu.VMEM((4, CH, CH), F32),
            pltpu.VMEM((2, NB, CH), F32),
            pltpu.VMEM((1, CH), F32),
            pltpu.SemaphoreType.DMA((7,)),
        ],
        compiler_params=small,
        cost_estimate=pl.CostEstimate(flops=10**8, bytes_accessed=1 << 22, transcendentals=0),
    )(*map(stay, (w_square, w_hidden, w_message, w_output, w_radial1, w_radial2, w_energy.reshape(1, CH))))

    far, turned, straight = lax.optimization_barrier((far, turned, straight))
    traded = lax.ppermute(far, "slab", [(i, i ^ 1) for i in range(slabs)])

    along, *saved = pl.pallas_call(
        lambda *refs: forward_kernel(slabs * NZL * LATTICE, *refs),
        out_shape=(
            whole(8, 4 * LAYER),
            whole(4, 3, 32, LAYER),
            whole(4, 32, LAYER),
            whole(6, 32 * NB, LAYER),
            whole(6, CH, LAYER),
            whole(6, CH, LAYER),
            whole(9, 10, CH, LAYER),
            whole(10, 32 * NB, LAYER),
            whole(8, CH, LAYER),
        ),
        in_specs=[vmem()] * 7,
        out_specs=tuple(vmem() for _ in range(9)),
        scratch_shapes=[
            pltpu.VMEM((12, 8, LAYER), F32),
            pltpu.VMEM((10, NB, LAYER), F32),
            pltpu.VMEM((10, CH, LAYER), F32),
            pltpu.VMEM((2, ROWS, 4 * LAYER), F32),
        ],
        compiler_params=pltpu.CompilerParams(vmem_limit_bytes=20 * 1024 * 1024),
    )(
        far,
        middle,
        traded,
        turned,
        straight,
        radial_turned,
        energy_column,
    )

    hops = []
    for g in range(groups):
        for s in range(slabs):
            if s % 2 and g + 1 < groups:
                hops.append((g * slabs + s, (g + 1) * slabs + s - 1))
            if s % 2 == 0 and g > 0:
                hops.append((g * slabs + s, (g - 1) * slabs + s + 1))
    path = lax.ppermute(along, ("image", "slab"), hops)

    forces = pl.pallas_call(
        backward_kernel,
        out_shape=whole(8, 4 * LAYER),
        in_specs=[vmem()] * 11,
        out_specs=vmem(),
        scratch_shapes=[
            pltpu.VMEM((6, NB, LAYER), F32),
            pltpu.VMEM((4, 32, LAYER), F32),
            pltpu.VMEM((6, 32, LAYER), F32),
        ],
        compiler_params=pltpu.CompilerParams(vmem_limit_bytes=20 * 1024 * 1024),
        cost_estimate=pl.CostEstimate(flops=4 * 10**9, bytes_accessed=1 << 22, transcendentals=0),
    )(*saved, straight, radial, radial_turned)

    table, kept, sent = pl.pallas_call(
        sums_kernel,
        out_shape=(whole(slabs, LAYER), whole(8, 2 * LAYER), whole(8, 2 * LAYER)),
        in_specs=[vmem()] * 4,
        out_specs=(vmem(), vmem(), vmem()),
        compiler_params=small,
    )(middle, forces, along, path)

    received = lax.ppermute(sent, "slab", [(i, i ^ 1) for i in range(slabs)])
    table = lax.all_to_all(table.reshape(slabs, 1, LAYER), "slab", 0, 0, tiled=False).reshape(slabs, LAYER)

    result, energies = pl.pallas_call(
        lambda *refs: combine_kernel(2 * groups, *refs),
        out_shape=(
            jax.ShapeDtypeStruct((3, 2, 2 * LAYER), F32),
            jax.ShapeDtypeStruct((2,), F32),
        ),
        in_specs=[smem()] + [vmem()] * 5,
        out_specs=(vmem(), smem()),
        compiler_params=small,
    )(
        climbing,
        table,
        prepared,
        kept,
        received,
        site_of_slot,
    )
    return result.transpose(1, 0, 2), energies


def solution(mesh):
    return jax.shard_map(
        local,
        mesh=mesh,
        in_specs=(
            P("image", None, "slab"),
            P("slab"),
            P(None, "slab"),
            P(),
            P(),
            P(),
            P(),
            P(),
            P(),
            P(),
            P(),
        ),
        out_specs=(P("image", None, "slab"), P("image")),
        check_vma=False,
    )
```

```python
import math

import jax
import jax.numpy as jnp
from jax import lax
from jax.experimental import pallas as pl
from jax.experimental.pallas import tpu as pltpu
from jax.sharding import PartitionSpec as P

NB = 8
NX = 16
NY = 8
NZL = 2
LAYER = 128
CH = 128
NOFF = 26
ROWS = 32

LATTICE = 2.55
CUTOFF = 5.0
STIFFNESS = 5.0
F32 = jnp.float32
BF16 = jnp.bfloat16
I32 = jnp.int32

OFFSETS = [
    (dx, dy, dz)
    for dz in (-1, 0, 1)
    for dy in (-1, 0, 1)
    for dx in (-1, 0, 1)
    if (dx, dy, dz) != (0, 0, 0)
]
ROW_OF = {offset: row for row, offset in enumerate(OFFSETS)}
LATERALS = [(dx, dy) for dy in (-1, 0, 1) for dx in (-1, 0, 1)]
LATERAL_OF = {lateral: number for number, lateral in enumerate(LATERALS)}


def take(values, index):
    return jnp.take_along_axis(values, index, axis=1, mode="promise_in_bounds")


def iota(shape, dim):
    return lax.broadcasted_iota(I32, shape, dim)


def shifted_site(shape, dx, dy):
    lane = iota(shape, len(shape) - 1)
    return ((((lane >> 4) + dy) & (NY - 1)) << 4) | ((lane + dx) & (NX - 1))


def site_of_row():
    row = iota((32, LAYER), 0)
    code = row + (row >= 13).astype(I32)
    level = (code >= 9).astype(I32) + (code >= 18).astype(I32)
    rest = code - 9 * level
    line = (rest >= 3).astype(I32) + (rest >= 6).astype(I32)
    column = rest - 3 * line
    return shifted_site((32, LAYER), column - 1, line - 1) & (LAYER - 1)


def silu_parts(values):
    sigma = 1.0 / (1.0 + jnp.exp(-values))
    return values * sigma, sigma * (1.0 + values * (1.0 - sigma))


def halves(values):
    high = values.astype(BF16)
    low = (values - high.astype(F32)).astype(BF16)
    return high, low


def stationary(matrix):
    high, low = halves(matrix)
    return jnp.concatenate(
        [jnp.concatenate([high, high], axis=1), jnp.concatenate([low, low], axis=1)], axis=0
    )


def product(packed, values):
    high, low = halves(values)
    out = jnp.dot(packed, jnp.concatenate([high, low], axis=0), preferred_element_type=F32)
    rows = packed.shape[0] // 2
    return out[:rows] + out[rows:]


def radial_stationary(matrix):
    high, low = halves(matrix.T)
    return jnp.concatenate([high, high, low, low], axis=1)


def radial_moving(values):
    high = values.astype(BF16).astype(F32)
    both = jnp.concatenate([high, values - high], axis=0).astype(BF16)
    return jnp.concatenate([both, both], axis=0)


def prepare_kernel(
    neighbours_hbm, ghost_hbm, positions_hbm, out, site_of_slot, neighbours, ghost_slots, positions, arrived
):
    copies = [
        pltpu.make_async_copy(source, target, arrived.at[number])
        for number, (source, target) in enumerate(
            ((ghost_hbm, ghost_slots), (neighbours_hbm, neighbours), (positions_hbm, positions))
        )
    ]
    for copy in copies:
        copy.start()
    copies[0].wait()
    slots = ghost_slots[...]
    inverse = jnp.zeros((8, 2 * LAYER), F32)
    for layer in range(NZL):
        hit = (jnp.broadcast_to(slots[layer : layer + 1], (2 * LAYER, LAYER)) == iota((2 * LAYER, LAYER), 0))
        sites = (iota((8, LAYER), 1) + layer * LAYER).astype(F32).astype(BF16)
        inverse = inverse + lax.dot_general(
            sites,
            jnp.where(hit, 1.0, 0.0).astype(BF16),
            (((1,), (1,)), ((), ())),
            preferred_element_type=F32,
        )
    inverse = inverse.astype(I32)
    site_of_slot[...] = inverse
    first = jnp.broadcast_to(inverse[0:1, :LAYER], (32, LAYER))
    second = jnp.broadcast_to(inverse[0:1, LAYER:], (32, LAYER))
    copies[1].wait()
    copies[2].wait()
    sides = [
        jnp.concatenate(
            [positions[c, k : k + 1, half * LAYER : (half + 1) * LAYER] for k in range(2) for c in range(3)]
            + [jnp.zeros((2, LAYER), F32)],
            axis=0,
        )
        for half in range(2)
    ]
    listed = neighbours[...].astype(F32)
    turned = jnp.concatenate([listed, jnp.zeros((64, LAYER), F32)], axis=0).T
    site = iota((32, LAYER), 1)
    row = iota((32, LAYER), 0)
    for layer in range(NZL):
        here = slice(layer * LAYER, (layer + 1) * LAYER)
        slot = jnp.broadcast_to(slots[layer : layer + 1], (8, LAYER))
        low = slot & (LAYER - 1)
        coords = jnp.where(slot < LAYER, take(sides[0], low), take(sides[1], low))
        slot = jnp.broadcast_to(slots[layer : layer + 1], (32, LAYER))
        picked = take(turned[0:32], slot >> 2)
        for part in range(1, 4):
            picked = jnp.where((slot & 3) == part, take(turned[32 * part : 32 * part + 32], slot >> 2), picked)
        entry = picked.astype(I32)
        low = entry & (LAYER - 1)
        own = jnp.where(entry < LAYER, take(first, low), take(second, low))
        inside = entry < 2 * LAYER
        level = jnp.where(inside, own >> 7, jnp.where(entry < 3 * LAYER, -1, NZL))
        target = jnp.where(inside, own & (LAYER - 1), low)
        column = ((target & (NX - 1)) - (site & (NX - 1)) + 1) & (NX - 1)
        line = ((target >> 4) - (site >> 4) + 1) & (NY - 1)
        code = (level - layer + 1) * 9 + line * 3 + column
        code = jnp.where(code > 13, code - 1, code) & 31
        bits = jnp.where(entry >= 0, jnp.left_shift(jnp.ones_like(code), code), 0)
        bits = bits[0:16] | bits[16:32]
        bits = bits[0:8] | bits[8:16]
        bits = bits[0:4] | bits[4:8]
        bits = bits[0:2] | bits[2:4]
        bits = bits[0:1] | bits[1:2]
        mask = (jnp.broadcast_to(bits, (32, LAYER)) >> row) & 1
        out[0:NOFF, here] = mask[0:NOFF].astype(F32)
        out[NOFF:32, here] = coords[0:6]


SIN_TERMS = [(-1.0) ** k / math.factorial(2 * k + 1) for k in range(7)]
COS_TERMS = [(-1.0) ** k / math.factorial(2 * k) for k in range(8)]


def horner(terms, square):
    total = jnp.full_like(square, terms[-1])
    for term in terms[-2::-1]:
        total = total * square + term
    return total


SQUARE, HIDDEN, MESSAGE, OUTPUT = range(4)


def weights_kernel(
    w_square,
    w_hidden,
    w_message,
    w_output,
    w_radial1,
    w_radial2,
    w_energy,
    turned,
    straight,
    radial,
    radial_turned,
    energy,
    squares,
    radials,
    column,
    arrived,
):
    moves = [(ref, squares.at[number]) for number, ref in enumerate((w_square, w_hidden, w_message, w_output))]
    moves += [(w_radial1, radials.at[0]), (w_radial2, radials.at[1]), (w_energy, column)]
    copies = [pltpu.make_async_copy(*move, arrived.at[number]) for number, move in enumerate(moves)]
    for copy in copies:
        copy.start()
    for copy in copies:
        copy.wait()
    for number in range(4):
        turned[number] = stationary(squares[number].T)
        straight[number] = stationary(squares[number])
    for number in range(2):
        radial[number] = stationary(radials[number])
        radial_turned[number] = radial_stationary(radials[number])
    energy[...] = jnp.broadcast_to(column[...], (CH, CH)).T


def forward_kernel(
    cell_z,
    far,
    middle,
    traded,
    turned,
    straight,
    radial_turned,
    w_energy,
    along,
    reach,
    inverse_radius,
    slope,
    radial_mix,
    hidden_slope,
    message,
    phi,
    grad_out,
    coords,
    summed,
    hidden,
    outer,
):
    slab = lax.axis_index("slab")
    even = (slab & 1) == 0
    place = ((slab >> 1) + slab + 1) & 1
    outer[place] = far[...]
    outer[1 - place] = traded[...]

    def level_rows(level, first, last):
        here = slice(level % 4 * LAYER, (level % 4 + 1) * LAYER)
        if 4 <= level < 8:
            return middle[first:last, here]
        return outer[0 if level < 4 else 1, first:last, here]

    for level in range(12):
        both = level_rows(level, 24, 32)
        coords[level, 0:3] = jnp.where(even, both[2:5], both[5:8])
    row = iota((32, LAYER), 0)
    site = site_of_row()
    boxes = (NX * LATTICE, NY * LATTICE, cell_z)

    for e in range(10):
        mask = jnp.where(row < NOFF, level_rows(e + 1, 0, 32), 0.0)
        squared = None
        for c in range(3):
            centre = coords[e + 1, c : c + 1]
            source = jnp.where(
                row < 9,
                jnp.broadcast_to(coords[e, c : c + 1], (32, LAYER)),
                jnp.where(
                    row < 17,
                    jnp.broadcast_to(centre, (32, LAYER)),
                    jnp.broadcast_to(coords[e + 2, c : c + 1], (32, LAYER)),
                ),
            )
            d = take(source, site) - jnp.broadcast_to(centre, (32, LAYER))
            box = jnp.float32(boxes[c])
            half = jnp.float32(0.5) * box
            d = jnp.where(d > half, d - box, jnp.where(d < -half, d + box, d))
            if 3 <= e <= 6:
                reach[e - 3, c] = d
            squared = d * d if squared is None else squared + d * d
        squared = jnp.where(squared > 0.0, squared, 1.0)
        radius = jnp.sqrt(squared)
        inverse = 1.0 / radius
        if 3 <= e <= 6:
            inverse_radius[e - 3] = inverse
        inside = radius < CUTOFF
        angle = jnp.minimum(radius * (math.pi / (2.0 * CUTOFF)), 0.5 * math.pi)
        square = angle * angle
        sine = angle * horner(SIN_TERMS, square)
        cosine = horner(COS_TERMS, square)
        sine1 = 2.0 * sine * cosine
        cosine1 = 1.0 - 2.0 * sine * sine
        smooth = jnp.where(inside, cosine * cosine, 0.0)
        cut_slope = jnp.where(inside, (-math.pi / CUTOFF) * sine * cosine, 0.0)
        scale = mask * smooth * inverse
        tilt = mask * (cut_slope - smooth * inverse) * inverse
        twice = 2.0 * cosine1
        s_prev, s_here = jnp.zeros_like(sine1), sine1
        c_prev, c_here = jnp.ones_like(sine1), cosine1
        for b in range(NB):
            phi[e, pl.ds(b, 32, stride=NB), :] = scale * s_here
            if 2 <= e <= 7:
                slope[e - 2, pl.ds(b, 32, stride=NB), :] = tilt * s_here + scale * (
                    ((b + 1) * math.pi / CUTOFF) * c_here
                )
            s_prev, s_here = s_here, twice * s_here - s_prev
            c_prev, c_here = c_here, twice * c_here - c_prev
        total = phi[e, 0:NB]
        for o in range(1, NOFF):
            total = total + phi[e, o * NB : (o + 1) * NB]
        summed[e] = total

    first, second = radial_turned[0], radial_turned[1]
    square_t, hidden_t, message_t = turned[SQUARE], turned[HIDDEN], turned[MESSAGE]

    held = {}

    def node_mix(pair):
        mix = jnp.dot(
            first,
            radial_moving(jnp.concatenate([summed[2 * pair], summed[2 * pair + 1]], axis=1)),
            preferred_element_type=F32,
        )
        for k in range(2):
            if 2 <= 2 * pair <= 6:
                radial_mix[2 * pair + k - 2] = mix[:, k * LAYER : (k + 1) * LAYER]
        held[pair] = mix, product(square_t, mix * mix)

    def node_hidden(pair):
        mix, mixed = held[pair]
        held[pair] = product(hidden_t, mix + mixed)

    def node_message(pair):
        act, act_slope = silu_parts(held[pair])
        for k in range(2):
            hidden[2 * pair + k] = act[:, k * LAYER : (k + 1) * LAYER]
            if 2 <= 2 * pair <= 6:
                hidden_slope[2 * pair + k - 2] = act_slope[:, k * LAYER : (k + 1) * LAYER]
        held[pair] = product(message_t, act)

    def node_send(pair):
        for k in range(2):
            for number, (dx, dy) in enumerate(LATERALS):
                part = held[pair][:, k * LAYER : (k + 1) * LAYER]
                if (dx, dy) != (0, 0):
                    part = take(part, shifted_site((CH, LAYER), dx, dy))
                message[number, 2 * pair + k] = part

    stages = (node_mix, node_hidden, node_message, node_send)
    for step in range(5 + len(stages) - 1):
        for number, stage in enumerate(stages):
            if 0 <= step - number < 5:
                stage(step - number)

    output_t, output_n = turned[OUTPUT], straight[OUTPUT]

    def readout(pair):
        a = 2 * pair
        e = a + 1
        total = jnp.concatenate([hidden[e], hidden[e + 1]], axis=1)
        for o, (dx, dy, dz) in enumerate(OFFSETS):
            here = slice(o * NB, (o + 1) * NB)
            radial = jnp.dot(
                second,
                radial_moving(jnp.concatenate([phi[e, here], phi[e + 1, here]], axis=1)),
                preferred_element_type=F32,
            )
            number = LATERAL_OF[(dx, dy)]
            total = total + radial * jnp.concatenate([message[number, e + dz], message[number, e + 1 + dz]], axis=1)
        held[pair] = total

    weight = jnp.concatenate([w_energy[...]] * 2, axis=1)
    energies = []

    def readout_energy(pair):
        act, act_slope = silu_parts(product(output_t, held[pair]))
        if 1 <= pair <= 2:
            energies.append(jnp.sum(weight * act, axis=0, keepdims=True))
        held[pair] = weight * act_slope

    def readout_grad(pair):
        grad = product(output_n, held[pair])
        grad_out[2 * pair] = grad[:, :LAYER]
        grad_out[2 * pair + 1] = grad[:, LAYER:]

    stages = (readout, readout_energy, readout_grad)
    for step in range(4 + len(stages) - 1):
        for number, stage in enumerate(stages):
            if 0 <= step - number < 4:
                stage(step - number)
    energy = energies[0] + energies[1]

    along[0:3] = jnp.where(even, middle[26:29, :], middle[29:32, :])
    along[3:4] = jnp.where(iota((1, 4 * LAYER), 1) == 0, jnp.sum(energy), 0.0)
    along[4:8] = jnp.zeros((4, 4 * LAYER), F32)


def backward_kernel(
    reach,
    inverse_radius,
    slope,
    radial_mix,
    hidden_slope,
    message,
    phi,
    grad_out,
    straight,
    radial,
    radial_turned,
    forces,
    grad_summed,
    pair_grad,
    pair_grad_turned,
):
    row = iota((32, LAYER), 0)
    site = site_of_row()
    square_n, hidden_n, message_n = straight[SQUARE], straight[HIDDEN], straight[MESSAGE]
    first_n, second_n = radial[0], radial[1]
    second = radial_turned[1]

    def back(pair):
        f = 2 * pair
        parts = [None, None]
        for dx, dy in LATERALS:
            total = None
            for dz in (-1, 0, 1):
                if (dx, dy, dz) == (0, 0, 0):
                    continue
                a = f + 1 - dz
                o = ROW_OF[(dx, dy, dz)]
                here = slice(o * NB, (o + 1) * NB)
                edge_radial = jnp.dot(
                    second,
                    radial_moving(jnp.concatenate([phi[a + 1, here], phi[a + 2, here]], axis=1)),
                    preferred_element_type=F32,
                )
                term = edge_radial * jnp.concatenate([grad_out[a], grad_out[a + 1]], axis=1)
                total = term if total is None else total + term
            for k in range(2):
                part = total[:, k * LAYER : (k + 1) * LAYER]
                if (dx, dy) != (0, 0):
                    part = take(part, shifted_site((CH, LAYER), -dx, -dy))
                parts[k] = part if parts[k] is None else parts[k] + part
        return jnp.concatenate(parts, axis=1)

    grad_message = jnp.concatenate([back(pair) for pair in range(3)], axis=1)
    grad_hidden = jnp.concatenate([grad_out[a] for a in range(1, 7)], axis=1) + product(message_n, grad_message)
    grad_pre = grad_hidden * jnp.concatenate([hidden_slope[f] for f in range(6)], axis=1)
    grad_mixed = product(hidden_n, grad_pre)
    mix = jnp.concatenate([radial_mix[f] for f in range(6)], axis=1)
    grad = product(first_n, grad_mixed + 2.0 * mix * product(square_n, grad_mixed))
    for f in range(6):
        grad_summed[f] = grad[:, f * LAYER : (f + 1) * LAYER]

    for f in range(6):
        pair_grad_turned[f] = jnp.zeros((32, LAYER), F32)
    for f in range(4):
        pair_grad[f] = jnp.zeros((32, LAYER), F32)

    def edges(f0, f1, offset0, offset1):
        number = LATERAL_OF[offset0[:2]]
        moved = jnp.concatenate(
            [
                grad_out[f0 + 1] * message[number, f0 + 2 + offset0[2]],
                grad_out[f1 + 1] * message[number, f1 + 2 + offset1[2]],
            ],
            axis=1,
        )
        grad = product(second_n, moved)
        out = []
        for k, (f, offset) in enumerate(((f0, offset0), (f1, offset1))):
            o = ROW_OF[offset]
            value = (grad[:, k * LAYER : (k + 1) * LAYER] + grad_summed[f]) * slope[f, o * NB : (o + 1) * NB]
            out.append(jnp.sum(value, axis=0, keepdims=True))
        return out

    def own_edges(pair):
        f = 2 * pair + 1
        for o, offset in enumerate(OFFSETS):
            left, right = edges(f, f + 1, offset, offset)
            pair_grad[f - 1, o : o + 1] = left
            pair_grad[f, o : o + 1] = right
            pair_grad_turned[f, 25 - o : 26 - o] = left
            pair_grad_turned[f + 1, 25 - o : 26 - o] = right

    for pair in range(2):
        own_edges(pair)
    for dx, dy in LATERALS:
        up, down = (dx, dy, 1), (dx, dy, -1)
        left, right = edges(0, 5, up, down)
        pair_grad_turned[0, 25 - ROW_OF[up] : 26 - ROW_OF[up]] = left
        pair_grad_turned[5, 25 - ROW_OF[down] : 26 - ROW_OF[down]] = right

    force_parts = []
    for f in range(1, 5):
        source = jnp.where(
            row < 9, pair_grad_turned[f - 1], jnp.where(row < 17, pair_grad_turned[f], pair_grad_turned[f + 1])
        )
        pull = (pair_grad[f - 1] + take(source, site)) * inverse_radius[f - 1]
        force_parts.append(
            jnp.concatenate([jnp.sum(pull * reach[f - 1, c], axis=0, keepdims=True) for c in range(3)], axis=0)
        )
    force = jnp.concatenate(force_parts, axis=1)

    forces[0:3] = force
    forces[3:8] = jnp.zeros((5, 4 * LAYER), F32)


def sums_kernel(middle, forces, along, path, table, kept, sent):
    even = (lax.axis_index("slab") & 1) == 0
    low, high = middle[26:29, :], middle[29:32, :]
    force, beside = forces[0:3], path[0:3]
    up = jnp.where(even, high - low, beside - high)
    down = jnp.where(even, low - beside, high - low)
    lane = iota((1, LAYER), 1)
    values = jnp.where(
        lane == 0, along[3:4, 0:1], jnp.where(lane == 6, jnp.broadcast_to(path[3:4, 0:1], (1, LAYER)), 0.0)
    )
    for k, term in enumerate((force * up, force * down, up * up, down * down, up * down)):
        total = jnp.sum(jnp.sum(term, axis=1, keepdims=True), axis=0, keepdims=True)
        values = values + jnp.where(lane == k + 1, total, 0.0)
    table[...] = jnp.broadcast_to(values, table.shape)
    both = jnp.concatenate([force, beside, jnp.zeros((2, 4 * LAYER), F32)], axis=0)
    left, right = both[:, : 2 * LAYER], both[:, 2 * LAYER :]
    kept[...] = jnp.where(even, left, right)
    sent[...] = jnp.where(even, right, left)


def combine_kernel(images, climbing, table, own, kept, received, site_of_slot, out, energies):
    even = (lax.axis_index("slab") & 1) == 0
    total = table[0:8]
    for k in range(8, table.shape[0], 8):
        total = total + table[k : k + 8]
    total = total[0:4] + total[4:8]
    total = total[0:2] + total[2:4]
    energy = (total[0:1, 6:7], total[0:1, 0:1], total[1:2, 0:1], total[1:2, 6:7])
    low, high = own[26:29, :], own[29:32, :]
    f_kept, f_received = kept[0:3, :], received[0:3, :]
    p_kept, p_received = kept[3:6, :], received[3:6, :]
    sides = (
        (jnp.where(even, f_kept, f_received), high - low, low - jnp.where(even, p_kept, p_received)),
        (jnp.where(even, f_received, f_kept), jnp.where(even, p_received, p_kept) - high, high - low),
    )
    slot = site_of_slot[...]
    for k, (force, up, down) in enumerate(sides):
        image = 2 * lax.axis_index("image") + k
        here = total[k : k + 1]
        v_prev, v_here, v_next = energy[k : k + 3]
        big = jnp.maximum(jnp.abs(v_next - v_here), jnp.abs(v_prev - v_here))
        small = jnp.minimum(jnp.abs(v_next - v_here), jnp.abs(v_prev - v_here))
        rising = jnp.logical_and(v_next > v_here, v_here > v_prev)
        falling = jnp.logical_and(v_next < v_here, v_here < v_prev)
        higher = v_next > v_prev
        a = jnp.where(rising, 1.0, jnp.where(falling, 0.0, jnp.where(higher, big, small)))
        b = jnp.where(rising, 0.0, jnp.where(falling, 1.0, jnp.where(higher, small, big)))
        fu, fd, uu, dd, ud = (here[:, i : i + 1] for i in range(1, 6))
        tangent_sq = a * a * uu + 2.0 * a * b * ud + b * b * dd
        norm = jnp.sqrt(tangent_sq)
        along = (a * fu + b * fd) / norm
        pull = STIFFNESS * (jnp.sqrt(uu) - jnp.sqrt(dd))
        amount = jnp.where(image == climbing[0], 2.0 * along, along - pull) / norm
        tangent = a * up + b * down
        result = force - amount * tangent
        end = jnp.logical_or(image == 0, image == images - 1)
        result = jnp.where(end, 0.0, result)
        result = jnp.concatenate([result, jnp.zeros((5, 2 * LAYER), F32)], axis=0)
        for part in range(NZL):
            index = slot[:, part * LAYER : (part + 1) * LAYER]
            low_index = index & (LAYER - 1)
            back = jnp.where(index < LAYER, take(result[:, :LAYER], low_index), take(result[:, LAYER:], low_index))
            for c in range(3):
                out[c, k : k + 1, part * LAYER : (part + 1) * LAYER] = back[c : c + 1]
        energies[k] = here[0, 0]


def vmem():
    return pl.BlockSpec(memory_space=pltpu.VMEM)


def hbm():
    return pl.BlockSpec(memory_space=pltpu.HBM)


def stay(array):
    return pltpu.with_memory_space_constraint(array, pltpu.HBM)


def smem():
    return pl.BlockSpec(memory_space=pltpu.SMEM)


def local(
    positions,
    neighbours,
    ghost_slots,
    climbing,
    w_radial1,
    w_square,
    w_hidden,
    w_message,
    w_radial2,
    w_output,
    w_energy,
):
    slabs = lax.axis_size("slab")
    groups = lax.axis_size("image")
    slab = lax.axis_index("slab")
    parity = slab % 2
    even = parity == 0

    small = pltpu.CompilerParams(vmem_limit_bytes=4 * 1024 * 1024)
    prepared, site_of_slot = pl.pallas_call(
        prepare_kernel,
        out_shape=(
            jax.ShapeDtypeStruct((ROWS, 2 * LAYER), F32),
            jax.ShapeDtypeStruct((8, 2 * LAYER), I32),
        ),
        in_specs=[hbm()] * 3,
        out_specs=(vmem(), vmem()),
        scratch_shapes=[
            pltpu.VMEM((64, LAYER), I32),
            pltpu.VMEM((2, LAYER), I32),
            pltpu.VMEM((3, 2, 2 * LAYER), F32),
            pltpu.SemaphoreType.DMA((3,)),
        ],
        compiler_params=small,
    )(
        stay(neighbours.reshape(64, LAYER)), stay(ghost_slots), stay(positions.transpose(1, 0, 2))
    )

    mate = lax.ppermute(prepared, "slab", [(i, i ^ 1) for i in range(slabs)])
    middle = jnp.concatenate([jnp.where(even, prepared, mate), jnp.where(even, mate, prepared)], axis=1)
    pairs = slabs // 2
    partners = []
    for i in range(slabs):
        p = i // 2
        other = p ^ 1 if i % 2 == 0 else (p + 1 if p % 2 else p - 1) % pairs
        partners.append((i, 2 * other + i % 2))
    far = lax.ppermute(middle, "slab", partners)
    def whole(*extents):
        return jax.ShapeDtypeStruct(extents, F32)

    turned, straight, radial, radial_turned, energy_column = pl.pallas_call(
        weights_kernel,
        out_shape=(
            jax.ShapeDtypeStruct((4, 2 * CH, 2 * CH), BF16),
            jax.ShapeDtypeStruct((4, 2 * CH, 2 * CH), BF16),
            jax.ShapeDtypeStruct((2, 2 * NB, 2 * CH), BF16),
            jax.ShapeDtypeStruct((2, CH, 4 * NB), BF16),
            whole(CH, CH),
        ),
        in_specs=[hbm()] * 7,
        out_specs=tuple(vmem() for _ in range(5)),
        scratch_shapes=[
            pltpu.VMEM((4, CH, CH), F32),
            pltpu.VMEM((2, NB, CH), F32),
            pltpu.VMEM((1, CH), F32),
            pltpu.SemaphoreType.DMA((7,)),
        ],
        compiler_params=small,
        cost_estimate=pl.CostEstimate(flops=10**8, bytes_accessed=1 << 22, transcendentals=0),
    )(*map(stay, (w_square, w_hidden, w_message, w_output, w_radial1, w_radial2, w_energy.reshape(1, CH))))

    far, turned, straight = lax.optimization_barrier((far, turned, straight))
    traded = lax.ppermute(far, "slab", [(i, i ^ 1) for i in range(slabs)])

    along, *saved = pl.pallas_call(
        lambda *refs: forward_kernel(slabs * NZL * LATTICE, *refs),
        out_shape=(
            whole(8, 4 * LAYER),
            whole(4, 3, 32, LAYER),
            whole(4, 32, LAYER),
            whole(6, 32 * NB, LAYER),
            whole(6, CH, LAYER),
            whole(6, CH, LAYER),
            whole(9, 10, CH, LAYER),
            whole(10, 32 * NB, LAYER),
            whole(8, CH, LAYER),
        ),
        in_specs=[vmem()] * 7,
        out_specs=tuple(vmem() for _ in range(9)),
        scratch_shapes=[
            pltpu.VMEM((12, 8, LAYER), F32),
            pltpu.VMEM((10, NB, LAYER), F32),
            pltpu.VMEM((10, CH, LAYER), F32),
            pltpu.VMEM((2, ROWS, 4 * LAYER), F32),
        ],
        compiler_params=pltpu.CompilerParams(vmem_limit_bytes=20 * 1024 * 1024),
    )(
        far,
        middle,
        traded,
        turned,
        straight,
        radial_turned,
        energy_column,
    )

    hops = []
    for g in range(groups):
        for s in range(slabs):
            if s % 2 and g + 1 < groups:
                hops.append((g * slabs + s, (g + 1) * slabs + s - 1))
            if s % 2 == 0 and g > 0:
                hops.append((g * slabs + s, (g - 1) * slabs + s + 1))
    path = lax.ppermute(along, ("image", "slab"), hops)

    forces = pl.pallas_call(
        backward_kernel,
        out_shape=whole(8, 4 * LAYER),
        in_specs=[vmem()] * 11,
        out_specs=vmem(),
        scratch_shapes=[
            pltpu.VMEM((6, NB, LAYER), F32),
            pltpu.VMEM((4, 32, LAYER), F32),
            pltpu.VMEM((6, 32, LAYER), F32),
        ],
        compiler_params=pltpu.CompilerParams(vmem_limit_bytes=20 * 1024 * 1024),
        cost_estimate=pl.CostEstimate(flops=4 * 10**9, bytes_accessed=1 << 22, transcendentals=0),
    )(*saved, straight, radial, radial_turned)

    table, kept, sent = pl.pallas_call(
        sums_kernel,
        out_shape=(whole(slabs, LAYER), whole(8, 2 * LAYER), whole(8, 2 * LAYER)),
        in_specs=[vmem()] * 4,
        out_specs=(vmem(), vmem(), vmem()),
        compiler_params=small,
    )(middle, forces, along, path)

    received = lax.ppermute(sent, "slab", [(i, i ^ 1) for i in range(slabs)])
    table = lax.all_to_all(table.reshape(slabs, 1, LAYER), "slab", 0, 0, tiled=False).reshape(slabs, LAYER)

    result, energies = pl.pallas_call(
        lambda *refs: combine_kernel(2 * groups, *refs),
        out_shape=(
            jax.ShapeDtypeStruct((3, 2, 2 * LAYER), F32),
            jax.ShapeDtypeStruct((2,), F32),
        ),
        in_specs=[smem()] + [vmem()] * 5,
        out_specs=(vmem(), smem()),
        compiler_params=small,
    )(
        climbing,
        table,
        prepared,
        kept,
        received,
        site_of_slot,
    )
    return result.transpose(1, 0, 2), energies


def solution(mesh):
    return jax.shard_map(
        local,
        mesh=mesh,
        in_specs=(
            P("image", None, "slab"),
            P("slab"),
            P(None, "slab"),
            P(),
            P(),
            P(),
            P(),
            P(),
            P(),
            P(),
            P(),
        ),
        out_specs=(P("image", None, "slab"), P("image")),
        check_vma=False,
    )
```
